32 devices in a mesh: frow: 8 (over z, x), fcol: 4 (over y, core).
Axes of the slice: x: 2, y: 2, z: 4, core: 2. Of those that a mesh axis runs over, the one named last changes fastest.
Arguments:
- facets: float32 [2, 1024, 4096], P(None, 'frow', 'fcol'), may hold values from -6 to 6
- column_start: int32 [1], replicated, may hold values from 0 to 4095
- subgrid_start: int32 [8], replicated, may hold values from 0 to 1023
- vis_count: int32 [8], P('frow'), may hold values from 1 to 64
- vis_row: int32 [8, 64], P('frow'), may hold values from 0 to 511
- vis_weight: float32 [8, 64, 512], P('frow', None, 'fcol'), may hold values from -1 to 1
Outputs:
- corrected: float32 [8, 512, 2, 512], P('frow', 'fcol')
- facet_update: float32 [2, 1024, 4096], P(None, 'frow', 'fcol')
The draws below stay inside these ranges and needn't reach their ends.
All inputs are finite; a program needn't handle non-finite values.
Results may differ from the reference program's by a relative error of at most 0.0003.
Values sent between devices are 32-bit elements; how exact they have to be, the bound alone decides.
No kernel may reach another device: no remote copies, remote signals or barrier semaphores. Data moves between devices by JAX's collectives and lax.ppermute only.
A program may use at most 64 MiB of HBM per device.

```python
import math
import jax
import jax.numpy as jnp
from jax import lax

SG = 512
MAXB = 64
NSUB = 8
N1 = 1024
N2 = 4096


def place_ends(values, rng, least, high):
    place = [jax.random.randint(jax.random.fold_in(rng, axis), (), 0, length) for axis, length in enumerate(values.shape)]
    main_axis = values.shape.index(max(values.shape))
    neighbour = place[:main_axis] + [(place[main_axis] + 1) % values.shape[main_axis]] + place[main_axis + 1:]
    return values.at[tuple(place)].set(least).at[tuple(neighbour)].set(high)


def steps_of(stream_key, extent, shards, low, top_value):
    level = 1.0
    for dim, shards_of in shards:
        steps = jax.random.uniform(jax.random.fold_in(jax.random.fold_in(stream_key, 6), dim), (shards_of,), jnp.float32, low / len(shards), top_value / len(shards))
        level = level * jnp.repeat(jnp.exp(steps), extent[dim] // shards_of).reshape((-1,) + (1,) * (len(extent) - 1 - dim))
    return level


def bell_draw(stream_key, shape, deviation, reach, cuts=(), held_as=jnp.bfloat16):
    loudness = steps_of(stream_key, shape, cuts, -0.22, 0.18) if cuts else 1.0
    result = jax.random.normal(stream_key, shape, jnp.float32) * deviation * loudness
    return jnp.minimum(jnp.maximum(result, -reach), reach).astype(held_as)


def setup_inputs(seed: int = 0) -> dict:
    key_of = jax.random.split(jax.random.key(seed), 7)
    facets = bell_draw(key_of[0], (2, N1, N2), 1.0, 6.0, ((1, 8), (2, 4)), jnp.float32)
    column_start = jax.random.randint(key_of[1], (1,), 0, N2).astype(jnp.int32)
    subgrid_start = place_ends(jax.random.randint(key_of[2], (NSUB,), 0, N1), jax.random.fold_in(key_of[2], 1), 0, N1 - 1).astype(jnp.int32)
    vis_count = place_ends(jax.random.randint(key_of[3], (NSUB,), 1, MAXB + 1), jax.random.fold_in(key_of[3], 1), 1, MAXB).astype(jnp.int32)
    vis_row = place_ends(jax.random.randint(key_of[4], (NSUB, MAXB), 0, SG), jax.random.fold_in(key_of[4], 1), 0, SG - 1).astype(jnp.int32)
    vis_weight = jnp.clip(jax.random.uniform(key_of[5], (NSUB, MAXB, SG), jnp.float32, -1.0, 1.0) * steps_of(key_of[5], (NSUB, MAXB, SG), ((0, 8), (2, 4)), -0.4, 0.0), -1.0, 1.0)
    return {"facets": facets, "column_start": column_start, "subgrid_start": subgrid_start, "vis_count": vis_count, "vis_row": vis_row, "vis_weight": vis_weight}


HIGH = lax.Precision.HIGHEST

def table(first, count, anchor, length, modulus):
    freqs = (first + jnp.arange(count, dtype=jnp.int32)) % modulus
    coords = anchor + jnp.arange(length, dtype=jnp.int32)
    phase = freqs[:, None] * coords[None, :] % modulus
    angle = phase.astype(jnp.float32) * jnp.float32(2.0 * math.pi / modulus)
    scale = jnp.float32(1.0 / math.sqrt(modulus))
    return (jnp.cos(angle) * scale, jnp.sin(angle) * scale)

def contract(form, left, right):
    return jnp.einsum(form, left, right, precision=HIGH)

def reference(facets, column_start, subgrid_start, vis_count, vis_row, vis_weight):
    real_part, imag_part = (facets[0], facets[1])
    col_cos, col_sin = table(column_start[0], SG, 0, N2, N2)
    strip_re = contract('qy,xy->qx', col_cos, real_part) + contract('qy,xy->qx', col_sin, imag_part)
    strip_im = contract('qy,xy->qx', col_cos, imag_part) - contract('qy,xy->qx', col_sin, real_part)

    def forward(first):
        row_cos, row_sin = table(first, SG, 0, N1, N1)
        sub_re = contract('qx,px->qp', strip_re, row_cos) + contract('qx,px->qp', strip_im, row_sin)
        sub_im = contract('qx,px->qp', strip_im, row_cos) - contract('qx,px->qp', strip_re, row_sin)
        return jnp.stack([sub_re, sub_im], 1)
    subs = lax.map(forward, subgrid_start)
    live = (jnp.arange(MAXB, dtype=jnp.int32)[None, :] < vis_count[:, None]).astype(jnp.float32)
    onehot = (vis_row[:, :, None] == jnp.arange(SG, dtype=jnp.int32)[None, None, :]).astype(jnp.float32)
    gain = 1.0 + contract('sbq,sbp->sqp', vis_weight * live[:, :, None], onehot)
    corrected = subs * gain[:, :, None, :]

    def adjoint(carry, items):
        first, grid = items
        row_cos, row_sin = table(first, SG, 0, N1, N1)
        back_re = contract('qp,px->qx', grid[:, 0], row_cos) - contract('qp,px->qx', grid[:, 1], row_sin)
        back_im = contract('qp,px->qx', grid[:, 1], row_cos) + contract('qp,px->qx', grid[:, 0], row_sin)
        return ((carry[0] + back_re, carry[1] + back_im), None)
    start = (jnp.zeros((SG, N1), jnp.float32), jnp.zeros((SG, N1), jnp.float32))
    (back_re, back_im), unused = lax.scan(adjoint, start, (subgrid_start, corrected))
    image_re = contract('qx,qy->xy', back_re, col_cos) - contract('qx,qy->xy', back_im, col_sin)
    image_im = contract('qx,qy->xy', back_im, col_cos) + contract('qx,qy->xy', back_re, col_sin)
    return (corrected, jnp.stack([image_re, image_im]))
```

```python
import functools
import math

import jax
import jax.numpy as jnp
import ml_dtypes
import numpy as np
from jax import lax
from jax.experimental import pallas as pl
from jax.experimental.pallas import tpu as pltpu
from jax.sharding import PartitionSpec as P

SG = 512
MAXB = 64
META = 8

BF = jnp.bfloat16
F32 = jnp.float32
NN = (((1,), (0,)), ((), ()))
NT = (((1,), (1,)), ((), ()))


def halves(value):
    high = value.astype(BF)
    return high, (value - high.astype(F32)).astype(BF)


def dot3(left, right, dims):
    def dot(a, b):
        return lax.dot_general(a, b, dims, preferred_element_type=F32)
    return dot(left[0], right[0]) + (dot(left[0], right[1]) + dot(left[1], right[0]))


def unit(phase, modulus, scale=1.0):
    angle = (phase & (modulus - 1)).astype(F32) * F32(2.0 * math.pi / modulus)
    return jnp.cos(angle) * F32(scale), jnp.sin(angle) * F32(scale)


def lanes(count, rows=1):
    return lax.broadcasted_iota(jnp.int32, (rows, count), 1)


def to_column(row):
    return jnp.transpose(jnp.broadcast_to(row, (8, row.shape[1])))[:, 0:1]


def wave_table(rows, cols, modulus):
    phase = np.arange(rows, dtype=np.int64)[:, None] * np.arange(cols, dtype=np.int64)[None, :] % modulus
    angle = phase * (2.0 * np.pi / modulus)
    parts = np.stack([np.cos(angle), np.sin(angle)])
    high = parts.astype(ml_dtypes.bfloat16)
    low = (parts - high.astype(np.float64)).astype(ml_dtypes.bfloat16)
    return np.concatenate([high, low])


def strip_kernel(cols_total, info, x_ref, e_ref, turn_ref, out_ref, z_hi, z_lo):
    height, width = x_ref.shape[1:]
    count = e_ref.shape[2]

    @pl.when(pl.program_id(0) == 0)
    def _():
        pc, ps = unit(info[1] * (info[0] * width + lanes(width)), cols_total, 1.0 / math.sqrt(cols_total))
        re, im = x_ref[0], x_ref[1]
        z = jnp.concatenate([re * pc + im * ps, im * pc - re * ps])
        z_hi[...], z_lo[...] = halves(z)

    z = (z_hi[...], z_lo[...])
    e = (e_ref[0, 0:2].reshape(2 * count, width), e_ref[0, 2:4].reshape(2 * count, width))
    acc = dot3(e, z, NT)
    cos, sin = acc[:count], acc[count:]
    re = cos[:, :height] + sin[:, height:]
    im = cos[:, height:] - sin[:, :height]
    tc, ts = turn_ref[0, 0], turn_ref[0, 1]
    out_ref[0, 0] = re * tc + im * ts
    out_ref[0, 1] = im * tc - re * ts


def strips(info, facets, table, turn, parity, cols_total):
    blocks, _, count, width = table.shape
    height = facets.shape[1]
    half = blocks // 2
    block = lambda g, info: info[0] ^ (2 * g + parity)
    return pl.pallas_call(
        functools.partial(strip_kernel, cols_total),
        grid_spec=pltpu.PrefetchScalarGridSpec(
            num_scalar_prefetch=1,
            grid=(half,),
            in_specs=[
                pl.BlockSpec((2, height, width), lambda g, info: (0, 0, 0)),
                pl.BlockSpec((1, 4, count, width), lambda g, info: (block(g, info), 0, 0, 0)),
                pl.BlockSpec((1, 2, count, height), lambda g, info: (info[0], 0, block(g, info), 0)),
            ],
            out_specs=pl.BlockSpec((1, 2, count, height), lambda g, info: (g, 0, 0, 0)),
            scratch_shapes=[pltpu.VMEM((2 * height, width), BF)] * 2,
        ),
        out_shape=jax.ShapeDtypeStruct((half, 2, count, height), F32),
        compiler_params=pltpu.CompilerParams(vmem_limit_bytes=32 << 20),
        name="strips",
    )(info, facets, table, turn)


def add_message(info, r, s, message, b_ref, state, height, count, rows_total):
    mine = info[1]
    strip, rest = message[: 2 * count], message[2 * count :]
    pc, ps = unit(mine * (r * height + lanes(height)), rows_total, 1.0 / math.sqrt(rows_total))
    re, im = strip[:count], strip[count:]
    re, im = re * pc + im * ps, im * pc - re * ps
    left = halves(jnp.concatenate([jnp.concatenate([re, im], 1), jnp.concatenate([im, -re], 1)]))
    right = (b_ref[0:2].reshape(2 * height, rows_total), b_ref[2:4].reshape(2 * height, rows_total))
    part = dot3(left, right, NN)
    freq = lanes(rows_total)
    pc, ps = unit(freq * (r * height), rows_total)
    re, im = part[:count], part[count:]
    add_re, add_im = re * pc + im * ps, im * pc - re * ps

    width = message.shape[1]
    flat = jnp.concatenate([rest, jnp.zeros((width - rest.shape[0], width), F32)])
    turned = jnp.transpose(flat)
    weight = turned[:count, :MAXB]
    row = turned[:MAXB, MAXB : MAXB + 1].astype(jnp.int32)
    place = jnp.where(row < 0, -1, (row + (s - mine)) & (rows_total - 1))
    hot = (lanes(rows_total, MAXB) == place).astype(F32).astype(BF)
    gain = lax.dot_general(
        jnp.concatenate(halves(weight), 1), jnp.concatenate([hot, hot]), NN, preferred_element_type=F32
    )
    gain = gain + (((freq + (mine - s)) & (rows_total - 1)) < SG).astype(F32)
    if state is None:
        return add_re, add_im, gain
    return state[0] + add_re, state[1] + add_im, state[2] + gain


def gather_kernel(n_messages, first, height, count, rows_total, info, *refs):
    b_ref, refs = refs[0], refs[1:]
    state = None
    if not first:
        state, refs = (refs[0][0], refs[0][1], refs[0][2]), refs[1:]
    messages, out_ref = refs[:n_messages], refs[n_messages]
    for i in range(n_messages):
        state = add_message(info, info[2 + 2 * i], info[3 + 2 * i], messages[i][...], b_ref, state, height, count, rows_total)
    for i in range(3):
        out_ref[i] = state[i]


def gather_step(info, table, state, messages, count):
    height, rows_total = table.shape[1:]
    first = state is None
    operands = [table] + ([] if first else [state]) + list(messages)
    return pl.pallas_call(
        functools.partial(gather_kernel, len(messages), first, height, count, rows_total),
        in_specs=[pl.BlockSpec(memory_space=pltpu.SMEM)] + [pl.BlockSpec(memory_space=pltpu.VMEM)] * len(operands),
        out_specs=pl.BlockSpec(memory_space=pltpu.VMEM),
        out_shape=jax.ShapeDtypeStruct((3, count, rows_total), F32),
        compiler_params=pltpu.CompilerParams(vmem_limit_bytes=32 << 20),
        cost_estimate=pl.CostEstimate(flops=10**9, bytes_accessed=4 << 20, transcendentals=0),
        name="gather_step",
    )(info, *operands)


def back_kernel(height, count, rows_total, info, b_ref, state_ref, gain_ref, top_ref, bottom_ref, corrected_ref, back_ref):
    state = state_ref[0], state_ref[1], state_ref[2]
    message = jnp.concatenate([top_ref[...], bottom_ref[...]])
    re, im, gain = add_message(info, info[2], info[3], message, b_ref, state, height, count, rows_total)
    mine, r = info[1], info[0]
    corrected_ref[0] = re[:, :SG] * gain_ref[...]
    corrected_ref[1] = im[:, :SG] * gain_ref[...]
    re, im = re * gain, im * gain
    pc, ps = unit(lanes(rows_total) * (r * height), rows_total)
    both = halves(jnp.concatenate([re * pc - im * ps, im * pc + re * ps]))
    table = (b_ref[0:2].reshape(2 * height, rows_total), b_ref[2:4].reshape(2 * height, rows_total))
    acc = dot3(table, both, NT)
    re = acc[:height, :count] - acc[height:, count:]
    im = acc[:height, count:] + acc[height:, :count]
    pc, ps = unit(mine * (r * height + lanes(height)), rows_total, 1.0 / math.sqrt(rows_total))
    pc, ps = to_column(pc), to_column(ps)
    back_ref[0] = re * pc - im * ps
    back_ref[1] = im * pc + re * ps


def back_step(info, table, state, gain, halves_of, count):
    height, rows_total = table.shape[1:]
    vmem = pl.BlockSpec(memory_space=pltpu.VMEM)
    return pl.pallas_call(
        functools.partial(back_kernel, height, count, rows_total),
        in_specs=[pl.BlockSpec(memory_space=pltpu.SMEM)] + [vmem] * 5,
        out_specs=[vmem] * 2,
        out_shape=[
            jax.ShapeDtypeStruct((2, count, SG), F32),
            jax.ShapeDtypeStruct((2, height, count), F32),
        ],
        compiler_params=pltpu.CompilerParams(vmem_limit_bytes=32 << 20),
        name="back_step",
    )(info, table, state, gain, *halves_of)


def image_kernel(gs, first, last, cols_total, blocks, info, e_ref, *refs):
    backs, refs = refs[: len(gs)], refs[len(gs) :]
    if not first:
        acc_ref, refs = refs[0], refs[1:]
    out_ref, tables, sems = refs
    count, width = tables.shape[2:]
    height = out_ref.shape[1]
    own = info[0]
    copies = [pltpu.make_async_copy(e_ref.at[own ^ g], tables.at[i], sems.at[i]) for i, g in enumerate(gs)]
    for copy in copies:
        copy.start()
    acc = None if first else jnp.concatenate([acc_ref[0], acc_ref[1]])
    for i, g in enumerate(gs):
        freq = (own ^ g) * count + lanes(count)
        pc, ps = unit(freq * (own * (cols_total // blocks)), cols_total)
        re, im = backs[i][0], backs[i][1]
        re, im = re * pc - im * ps, im * pc + re * ps
        left = halves(jnp.concatenate([jnp.concatenate([re, -im], 1), jnp.concatenate([im, re], 1)]))
        copies[i].wait()
        right = (tables[i, 0:2].reshape(2 * count, width), tables[i, 2:4].reshape(2 * count, width))
        part = dot3(left, right, NN)
        acc = part if acc is None else acc + part
    re, im = acc[:height], acc[height:]
    if last:
        pc, ps = unit(info[1] * (own * width + lanes(width)), cols_total, 1.0 / math.sqrt(cols_total))
        re, im = re * pc - im * ps, im * pc + re * ps
    out_ref[0] = re
    out_ref[1] = im


def image_step(info, table, gs, backs, acc, last, cols_total):
    blocks, _, count, width = table.shape
    height = backs[0].shape[1]
    first = acc is None
    operands = list(backs) + ([] if first else [acc])
    vmem = pl.BlockSpec(memory_space=pltpu.VMEM)
    return pl.pallas_call(
        functools.partial(image_kernel, gs, first, last, cols_total, blocks),
        in_specs=[pl.BlockSpec(memory_space=pltpu.SMEM), pl.BlockSpec(memory_space=pl.ANY)] + [vmem] * len(operands),
        out_specs=vmem,
        out_shape=jax.ShapeDtypeStruct((2, height, width), F32),
        scratch_shapes=[pltpu.VMEM((len(gs), 4, count, width), BF), pltpu.SemaphoreType.DMA((len(gs),))],
        compiler_params=pltpu.CompilerParams(vmem_limit_bytes=32 << 20),
        cost_estimate=pl.CostEstimate(flops=10**9, bytes_accessed=4 << 20, transcendentals=0),
        name="image_step",
    )(info, table, *operands)


def swap(value, axis, bit):
    return lax.ppermute(value, axis, [(i, i ^ bit) for i in range(lax.axis_size(axis))])


def per_device(facets, column_start, subgrid_start, vis_count, vis_row, vis_weight):
    row = lax.axis_index("frow")
    col = lax.axis_index("fcol")
    rows = lax.axis_size("frow")
    cols = lax.axis_size("fcol")
    height, width = facets.shape[1:]
    rows_total, cols_total = height * rows, width * cols
    count = SG // cols
    assert vis_count.shape[0] == 1 and count <= height

    e_table = jnp.asarray(wave_table(SG, width, cols_total).reshape(4, cols, count, width).transpose(1, 0, 2, 3))
    b_table = jnp.asarray(wave_table(height, rows_total, rows_total))
    angle = np.arange(cols)[:, None] * np.arange(SG)[None, :] % cols * (2.0 * np.pi / cols)
    turn = np.stack([np.cos(angle), np.sin(angle)], 1).astype(np.float32)
    turn = jnp.asarray(np.broadcast_to(turn[..., None], turn.shape + (height,)).copy())

    info = jnp.stack([col, column_start[0]]).astype(jnp.int32)
    sent = strips(info, facets, e_table, turn, 1, cols_total)
    kept = strips(info, facets, e_table, turn, 0, cols_total)
    strip = kept + swap(sent, "fcol", 1)
    bit = 2
    while bit < cols:
        pairs = strip.reshape((-1, 2) + strip.shape[1:])
        strip = pairs[:, 0] + swap(pairs[:, 1], "fcol", bit)
        bit *= 2

    live = jnp.arange(MAXB, dtype=jnp.int32)[None, :] < vis_count[:, None]
    meta = jnp.where(live, vis_row, -1).astype(F32)
    meta = jnp.pad(meta, ((0, META - 1), (0, height - MAXB)))
    weights = jnp.pad(vis_weight[0], ((0, 0), (0, height - count)))
    own = jnp.concatenate([strip.reshape(2 * count, height), weights, meta])

    order = list(range(0, rows, 2)) + list(range(rows - 1, 0, -2))
    place = np.argsort(order)
    ahead = [(order[i], order[(i + 1) % rows]) for i in range(rows)]
    behind = [(b, a) for a, b in ahead]
    order_array, place_array = jnp.asarray(order, jnp.int32), jnp.asarray(place, jnp.int32)
    at = place_array[row]
    mine = subgrid_start[row]

    def facts(*steps):
        found = [row.astype(jnp.int32), mine]
        for step in steps:
            source = order_array[(at + step) % rows]
            found += [source, subgrid_start[source]]
        return jnp.stack(found)

    state = gather_step(facts(0), b_table, None, [own], count)
    gain = state[2, :, :SG]
    up = down = own
    for step in range(1, rows // 2):
        up = lax.ppermute(up, "frow", ahead)
        down = lax.ppermute(down, "frow", behind)
        state = gather_step(facts(-step, step), b_table, state, [up, down], count)
    cut = (own.shape[0] // 2 + 7) // 8 * 8
    top = lax.ppermute(up[:cut], "frow", ahead)
    bottom = lax.ppermute(down[cut:], "frow", behind)
    corrected, back = back_step(facts(rows // 2), b_table, state, gain, [top, bottom], count)

    near, far = [back], None
    bit = 1
    far = [swap(back, "fcol", cols // 2)]
    while bit < cols // 2:
        near += [swap(b, "fcol", bit) for b in near]
        far += [swap(b, "fcol", bit) for b in far]
        bit *= 2
    acc = image_step(info, e_table, tuple(range(cols // 2)), near, None, False, cols_total)
    update = image_step(info, e_table, tuple(range(cols // 2, cols)), far, acc, True, cols_total)
    return jnp.transpose(corrected, (1, 0, 2))[None], update


def solution(mesh):
    return jax.shard_map(
        per_device,
        mesh=mesh,
        in_specs=(
            P(None, "frow", "fcol"),
            P(),
            P(),
            P("frow"),
            P("frow", None),
            P("frow", None, "fcol"),
        ),
        out_specs=(P("frow", "fcol", None, None), P(None, "frow", "fcol")),
        check_vma=False,
    )
```

```python
import functools
import math

import jax
import jax.numpy as jnp
import ml_dtypes
import numpy as np
from jax import lax
from jax.experimental import pallas as pl
from jax.experimental.pallas import tpu as pltpu
from jax.sharding import PartitionSpec as P

SG = 512
MAXB = 64
META = 8

BF = jnp.bfloat16
F32 = jnp.float32
NN = (((1,), (0,)), ((), ()))
NT = (((1,), (1,)), ((), ()))
VMEM = pl.BlockSpec(memory_space=pltpu.VMEM)
SMEM = pl.BlockSpec(memory_space=pltpu.SMEM)
HBM = pl.BlockSpec(memory_space=pltpu.HBM)
LIMIT = pltpu.CompilerParams(vmem_limit_bytes=32 << 20)


def halves(value):
    high = value.astype(BF)
    return high, (value - high.astype(F32)).astype(BF)


def dot3(left, right, dims):
    def dot(a, b):
        return lax.dot_general(a, b, dims, preferred_element_type=F32)
    return dot(left[0], right[0]) + (dot(left[0], right[1]) + dot(left[1], right[0]))


def unit(phase, modulus, scale=1.0):
    angle = (phase & (modulus - 1)).astype(F32) * F32(2.0 * math.pi / modulus)
    return jnp.cos(angle) * F32(scale), jnp.sin(angle) * F32(scale)


def lanes(count, rows=1):
    return lax.broadcasted_iota(jnp.int32, (rows, count), 1)


def to_column(row):
    return jnp.transpose(jnp.broadcast_to(row, (8, row.shape[1])))[:, 0:1]


def wave_table(rows, cols, modulus):
    phase = np.arange(rows, dtype=np.int64)[:, None] * np.arange(cols, dtype=np.int64)[None, :] % modulus
    angle = phase * (2.0 * np.pi / modulus)
    parts = np.stack([np.cos(angle), np.sin(angle)])
    high = parts.astype(ml_dtypes.bfloat16)
    low = (parts - high.astype(np.float64)).astype(ml_dtypes.bfloat16)
    return np.concatenate([high, low])


def ring_place(r, rows):
    return jnp.where(lax.rem(r, 2) == 0, r // 2, rows - 1 - r // 2)


def ring_block(place, rows):
    place = lax.rem(place + rows, rows)
    return jnp.where(place < rows // 2, 2 * place, 2 * (rows - 1 - place) + 1)


def strip_kernel(gs, cols_total, start_ref, x_ref, e_ref, out_ref, tables, sems):
    height, width = x_ref.shape[1:]
    count = tables.shape[2]
    own = lax.axis_index("fcol")
    copies = [pltpu.make_async_copy(e_ref.at[own ^ g], tables.at[i], sems.at[i]) for i, g in enumerate(gs)]
    for copy in copies:
        copy.start()
    pc, ps = unit(start_ref[0] * (own * width + lanes(width)), cols_total, 1.0 / math.sqrt(cols_total))
    re, im = x_ref[0], x_ref[1]
    z = halves(jnp.concatenate([re * pc + im * ps, im * pc - re * ps]))
    for i, g in enumerate(gs):
        tc, ts = unit(((own ^ g) * count + lanes(count)) * (own * width), cols_total)
        tc, ts = to_column(tc), to_column(ts)
        copies[i].wait()
        e = (tables[i, 0:2].reshape(2 * count, width), tables[i, 2:4].reshape(2 * count, width))
        acc = dot3(e, z, NT)
        cos, sin = acc[:count], acc[count:]
        re = cos[:, :height] + sin[:, height:]
        im = cos[:, height:] - sin[:, :height]
        out_ref[i, 0] = re * tc + im * ts
        out_ref[i, 1] = im * tc - re * ts


def strips(column_start, facets, table, gs, cols_total):
    _, _, count, width = table.shape
    height = facets.shape[1]
    return pl.pallas_call(
        functools.partial(strip_kernel, gs, cols_total),
        in_specs=[SMEM, VMEM, HBM],
        out_specs=VMEM,
        out_shape=jax.ShapeDtypeStruct((len(gs), 2, count, height), F32),
        scratch_shapes=[pltpu.VMEM((len(gs), 4, count, width), BF), pltpu.SemaphoreType.DMA((len(gs),))],
        compiler_params=LIMIT,
        name="strips",
    )(column_start, facets, table)


def add_message(starts, r, message, b_ref, roots_ref, state, height, count, rows_total):
    mine, other = starts[lax.axis_index("frow")], starts[r]
    strip, rest = message[: 2 * count], message[2 * count :]
    pc, ps = unit(mine * (r * height + lanes(height)), rows_total, 1.0 / math.sqrt(rows_total))
    re, im = strip[:count], strip[count:]
    re, im = re * pc + im * ps, im * pc - re * ps
    high, low = halves(jnp.concatenate([jnp.concatenate([re, im], 1), jnp.concatenate([im, -re], 1)]))
    part = lax.dot_general(
        jnp.concatenate([high, low, high], 1), b_ref[...].reshape(6 * height, rows_total), NN, preferred_element_type=F32
    )
    freq = lanes(rows_total)
    pc, ps = roots_ref[r, 0:1], roots_ref[r, 1:2]
    re, im = part[:count], part[count:]
    add_re, add_im = re * pc + im * ps, im * pc - re * ps

    width = message.shape[1]
    flat = jnp.concatenate([rest, jnp.zeros((width - rest.shape[0], width), F32)])
    turned = jnp.transpose(flat)
    weight = turned[:count, :MAXB]
    row = turned[:MAXB, MAXB : MAXB + 1].astype(jnp.int32)
    place = jnp.where(row < 0, -1, (row + (other - mine)) & (rows_total - 1))
    hot = (lanes(rows_total, MAXB) == place).astype(F32).astype(BF)
    gain = lax.dot_general(
        jnp.concatenate(halves(weight), 1), jnp.concatenate([hot, hot]), NN, preferred_element_type=F32
    )
    gain = gain + (((freq + (mine - other)) & (rows_total - 1)) < SG).astype(F32)
    if state is None:
        return add_re, add_im, gain
    return state[0] + add_re, state[1] + add_im, state[2] + gain


def gather_kernel(steps, rows, height, count, starts, b_ref, roots_ref, *refs):
    state = None
    if len(refs) > len(steps) + 1:
        state, refs = (refs[0][0], refs[0][1], refs[0][2]), refs[1:]
    at = ring_place(lax.axis_index("frow"), rows)
    for step, message in zip(steps, refs):
        r = ring_block(at + step, rows)
        state = add_message(starts, r, message[...], b_ref, roots_ref, state, height, count, rows * height)
    for i in range(3):
        refs[-1][i] = state[i]


def gather_step(starts, table, roots, state, messages, steps, count):
    height, rows_total = table.shape[1:]
    operands = [table, roots] + ([] if state is None else [state]) + list(messages)
    return pl.pallas_call(
        functools.partial(gather_kernel, steps, rows_total // height, height, count),
        in_specs=[SMEM] + [VMEM] * len(operands),
        out_specs=VMEM,
        out_shape=jax.ShapeDtypeStruct((3, count, rows_total), F32),
        compiler_params=LIMIT,
        cost_estimate=pl.CostEstimate(flops=10**9, bytes_accessed=4 << 20, transcendentals=0),
        name="gather_step",
    )(starts, *operands)


def back_kernel(rows, height, count, starts, b_ref, roots_ref, state_ref, top_ref, bottom_ref, back_ref, sub_ref):
    state = state_ref[0], state_ref[1], state_ref[2]
    message = jnp.concatenate([top_ref[...], bottom_ref[...]])
    rows_total = rows * height
    own = lax.axis_index("frow")
    r = ring_block(ring_place(own, rows) + rows // 2, rows)
    re, im, gain = add_message(starts, r, message, b_ref, roots_ref, state, height, count, rows_total)
    sub_ref[0] = re[:, :SG]
    sub_ref[1] = im[:, :SG]
    re, im = re * gain, im * gain
    pc, ps = roots_ref[own, 0:1], roots_ref[own, 1:2]
    both = halves(jnp.concatenate([re * pc - im * ps, im * pc + re * ps]))
    table = (b_ref[0:2].reshape(2 * height, rows_total), b_ref[4:6].reshape(2 * height, rows_total))
    acc = dot3(table, both, NT)
    re = acc[:height, :count] - acc[height:, count:]
    im = acc[:height, count:] + acc[height:, :count]
    pc, ps = unit(starts[own] * (own * height + lanes(height)), rows_total, 1.0 / math.sqrt(rows_total))
    pc, ps = to_column(pc), to_column(ps)
    back_ref[0] = re * pc - im * ps
    back_ref[1] = im * pc + re * ps


def back_step(starts, table, roots, state, parts, count):
    height, rows_total = table.shape[1:]
    return pl.pallas_call(
        functools.partial(back_kernel, rows_total // height, height, count),
        in_specs=[SMEM] + [VMEM] * 5,
        out_specs=[VMEM] * 2,
        out_shape=[
            jax.ShapeDtypeStruct((2, height, count), F32),
            jax.ShapeDtypeStruct((2, count, SG), F32),
        ],
        compiler_params=LIMIT,
        name="back_step",
    )(starts, table, roots, state, *parts)


def correct_kernel(sub_ref, gain_ref, out_ref):
    count = sub_ref.shape[1]
    pieces = SG // 128
    for part in range(2):
        value = sub_ref[part] * gain_ref[2, :, :SG]
        for i in range(pieces):
            out_ref[pl.ds(2 * i + part, count, stride=2 * pieces), :] = value[:, 128 * i : 128 * (i + 1)]


def correct_step(sub, first_state):
    count = sub.shape[1]
    out = pl.pallas_call(
        correct_kernel,
        in_specs=[VMEM] * 2,
        out_specs=VMEM,
        out_shape=jax.ShapeDtypeStruct((count * 2 * SG // 128, 128), F32),
        compiler_params=LIMIT,
        cost_estimate=pl.CostEstimate(flops=10**9, bytes_accessed=4 << 20, transcendentals=0),
        name="correct_step",
    )(sub, first_state)
    out = out.reshape(count, SG // 128, 2, 128)
    return jnp.transpose(out, (0, 2, 1, 3)).reshape(1, count, 2, SG)


def image_kernel(gs, cols_total, blocks, start_ref, e_ref, *refs):
    backs, refs = refs[: len(gs)], refs[len(gs) :]
    out_ref = refs[-1]
    _, height, width = out_ref.shape
    count = e_ref.shape[2]
    own = lax.axis_index("fcol")
    last = len(refs) > 1
    acc = jnp.concatenate([refs[0][0], refs[0][1]]) if last else None
    for back, g in zip(backs, gs):
        freq = (own ^ g) * count + lanes(count)
        pc, ps = unit(freq * (own * width), cols_total)
        re, im = back[0], back[1]
        re, im = re * pc - im * ps, im * pc + re * ps
        left = halves(jnp.concatenate([jnp.concatenate([re, -im], 1), jnp.concatenate([im, re], 1)]))
        right = (e_ref[own ^ g, 0:2].reshape(2 * count, width), e_ref[own ^ g, 2:4].reshape(2 * count, width))
        part = dot3(left, right, NN)
        acc = part if acc is None else acc + part
    re, im = acc[:height], acc[height:]
    if last:
        pc, ps = unit(start_ref[0] * (own * width + lanes(width)), cols_total, 1.0 / math.sqrt(cols_total))
        re, im = re * pc - im * ps, im * pc + re * ps
    out_ref[0] = re
    out_ref[1] = im


def image_step(column_start, table, gs, backs, acc, cols_total):
    blocks, _, _, width = table.shape
    height = backs[0].shape[1]
    operands = list(backs) + ([] if acc is None else [acc])
    return pl.pallas_call(
        functools.partial(image_kernel, gs, cols_total, blocks),
        in_specs=[SMEM] + [VMEM] * (1 + len(operands)),
        out_specs=VMEM,
        out_shape=jax.ShapeDtypeStruct((2, height, width), F32),
        compiler_params=LIMIT,
        cost_estimate=pl.CostEstimate(flops=10**9, bytes_accessed=4 << 20, transcendentals=0),
        name="image_step",
    )(column_start, table, *operands)


def swap(value, axis, bit):
    return lax.ppermute(value, axis, [(i, i ^ bit) for i in range(lax.axis_size(axis))])


def per_device(facets, column_start, subgrid_start, vis_count, vis_row, vis_weight):
    rows = lax.axis_size("frow")
    cols = lax.axis_size("fcol")
    height, width = facets.shape[1:]
    rows_total, cols_total = height * rows, width * cols
    count = SG // cols
    assert vis_count.shape[0] == 1 and count <= height

    e_table = jnp.asarray(wave_table(SG, width, cols_total).reshape(4, cols, count, width).transpose(1, 0, 2, 3))
    b_table = wave_table(height, rows_total, rows_total)
    b_table = jnp.asarray(np.concatenate([b_table[:2], b_table]))
    angle = np.arange(rows)[:, None] * np.arange(rows_total)[None, :] % rows * (2.0 * np.pi / rows)
    roots = jnp.asarray(np.stack([np.cos(angle), np.sin(angle)], 1).astype(np.float32))

    sent = strips(column_start, facets, e_table, tuple(range(1, cols, 2)), cols_total)
    kept = strips(column_start, facets, e_table, tuple(range(0, cols, 2)), cols_total)
    strip = kept + swap(sent, "fcol", 1)
    bit = 2
    while bit < cols:
        pairs = strip.reshape((-1, 2) + strip.shape[1:])
        strip = pairs[:, 0] + swap(pairs[:, 1], "fcol", bit)
        bit *= 2

    live = jnp.arange(MAXB, dtype=jnp.int32)[None, :] < vis_count[:, None]
    meta = jnp.where(live, vis_row, -1).astype(F32)
    meta = jnp.pad(meta, ((0, META - 1), (0, height - MAXB)))
    weights = jnp.pad(vis_weight[0], ((0, 0), (0, height - count)))
    own = jnp.concatenate([strip.reshape(2 * count, height), weights, meta])

    order = list(range(0, rows, 2)) + list(range(rows - 1, 0, -2))
    ahead = [(order[i], order[(i + 1) % rows]) for i in range(rows)]
    behind = [(b, a) for a, b in ahead]
    first_state = state = gather_step(subgrid_start, b_table, roots, None, [own], (0,), count)
    up = down = own
    for step in range(1, rows // 2):
        up = lax.ppermute(up, "frow", ahead)
        down = lax.ppermute(down, "frow", behind)
        state = gather_step(subgrid_start, b_table, roots, state, [up, down], (-step, step), count)
    cut = (own.shape[0] // 2 + 7) // 8 * 8
    top = lax.ppermute(up[:cut], "frow", ahead)
    bottom = lax.ppermute(down[cut:], "frow", behind)
    back, sub = back_step(subgrid_start, b_table, roots, state, [top, bottom], count)

    near, far = [back], [swap(back, "fcol", cols // 2)]
    bit = 1
    while bit < cols // 2:
        near += [swap(b, "fcol", bit) for b in near]
        bit *= 2
    acc = image_step(column_start, e_table, tuple(range(cols // 2)), near, None, cols_total)
    corrected = correct_step(sub, first_state)
    far[0], acc, corrected = lax.optimization_barrier((far[0], acc, corrected))
    bit = 1
    while bit < cols // 2:
        far += [swap(b, "fcol", bit) for b in far]
        bit *= 2
    update = image_step(column_start, e_table, tuple(range(cols // 2, cols)), far, acc, cols_total)
    return corrected, update


def solution(mesh):
    return jax.shard_map(
        per_device,
        mesh=mesh,
        in_specs=(
            P(None, "frow", "fcol"),
            P(),
            P(),
            P("frow"),
            P("frow", None),
            P("frow", None, "fcol"),
        ),
        out_specs=(P("frow", "fcol", None, None), P(None, "frow", "fcol")),
        check_vma=False,
    )
```

```python
import functools
import math

import jax
import jax.numpy as jnp
import ml_dtypes
import numpy as np
from jax import lax
from jax.experimental import pallas as pl
from jax.experimental.pallas import tpu as pltpu
from jax.sharding import PartitionSpec as P

SG = 512
MAXB = 64
META = 8

BF = jnp.bfloat16
F32 = jnp.float32
NN = (((1,), (0,)), ((), ()))
NT = (((1,), (1,)), ((), ()))
VMEM = pl.BlockSpec(memory_space=pltpu.VMEM)
SMEM = pl.BlockSpec(memory_space=pltpu.SMEM)
LIMIT = pltpu.CompilerParams(vmem_limit_bytes=32 << 20)


def halves(value):
    high = value.astype(BF)
    return high, (value - high.astype(F32)).astype(BF)


def dot3(left, right, dims):
    def dot(a, b):
        return lax.dot_general(a, b, dims, preferred_element_type=F32)
    return dot(left[0], right[0]) + (dot(left[0], right[1]) + dot(left[1], right[0]))


def unit(phase, modulus, scale=1.0):
    angle = (phase & (modulus - 1)).astype(F32) * F32(2.0 * math.pi / modulus)
    return jnp.cos(angle) * F32(scale), jnp.sin(angle) * F32(scale)


def lanes(count, rows=1):
    return lax.broadcasted_iota(jnp.int32, (rows, count), 1)


def wave_parts(rows, stride, cols, modulus):
    phase = np.arange(rows, dtype=np.int64)[:, None] * (stride * np.arange(cols, dtype=np.int64))[None, :] % modulus
    angle = phase * (2.0 * np.pi / modulus)
    return np.stack([np.cos(angle), np.sin(angle)])


def wave_table(rows, cols, modulus):
    parts = wave_parts(rows, 1, cols, modulus)
    high = parts.astype(ml_dtypes.bfloat16)
    low = (parts - high.astype(np.float64)).astype(ml_dtypes.bfloat16)
    return np.concatenate([high, low])


def ring_place(r, rows):
    return jnp.where(lax.rem(r, 2) == 0, r // 2, rows - 1 - r // 2)


def ring_block(place, rows):
    place = lax.rem(place + rows, rows)
    return jnp.where(place < rows // 2, 2 * place, 2 * (rows - 1 - place) + 1)


def wave_kernel(width, cols_total, base_ref, steps_ref):
    own = lax.axis_index("fcol")
    blocks, _, count, _ = base_ref.shape
    row = lax.broadcasted_iota(jnp.int32, (count, 128), 0)
    for ref, coord in ((base_ref, lanes(128)), (steps_ref, lanes(128) * 128 + own * width)):
        cos, sin = unit(row * coord, cols_total)
        for g in range(blocks):
            pc, ps = unit((own ^ g) * count * coord, cols_total)
            ref[g, 0] = cos * pc - sin * ps
            ref[g, 1] = sin * pc + cos * ps


def waves_of(count, width, cols_total):
    shape = jax.ShapeDtypeStruct((SG // count, 2, count, 128), F32)
    return pl.pallas_call(
        functools.partial(wave_kernel, width, cols_total),
        out_specs=[VMEM] * 2,
        out_shape=[shape] * 2,
        compiler_params=LIMIT,
        cost_estimate=pl.CostEstimate(flops=10**9, bytes_accessed=2 << 20, transcendentals=0),
        name="waves",
    )()


def strip_kernel(gs, cols_total, first, *refs):
    source_ref, base_ref, steps_ref, out_ref = refs[1:5] if first else refs
    own = lax.axis_index("fcol")
    height, width = out_ref.shape[-1], source_ref.shape[-1]
    if first:
        pc, ps = unit(refs[0][0:1, 0:1] * (own * width + lanes(width)), cols_total, 1.0 / math.sqrt(cols_total))
        re, im = source_ref[0], source_ref[1]
        z = halves(jnp.concatenate([re * pc + im * ps, im * pc - re * ps]))
        z_ref, phase_ref = refs[5:]
        z_ref[0], z_ref[1] = z
        phase_ref[0:1], phase_ref[1:2] = pc, ps
    else:
        z = source_ref[0], source_ref[1]
    for i, g in enumerate(gs):
        turn_cos, turn_sin, base_cos, base_sin = steps_ref[g, 0], steps_ref[g, 1], base_ref[g, 0], base_ref[g, 1]
        cos, sin = [], []
        for t in range(width // 128):
            tc, ts = turn_cos[:, t : t + 1], turn_sin[:, t : t + 1]
            cos.append(tc * base_cos - ts * base_sin)
            sin.append(ts * base_cos + tc * base_sin)
        waves = halves(jnp.concatenate([jnp.concatenate(cos, 1), jnp.concatenate(sin, 1)]))
        acc = dot3(waves, z, NT)
        count = out_ref.shape[2]
        cos, sin = acc[:count], acc[count:]
        out_ref[i, 0] = cos[:, :height] + sin[:, height:]
        out_ref[i, 1] = cos[:, height:] - sin[:, :height]


def strips(column_start, source, waves, gs, cols_total, first=False, cost=10**9):
    count = waves[0].shape[2]
    height, width = source.shape[1] // (1 if first else 2), source.shape[2]
    operands = ([column_start] if first else []) + [source, *waves]
    out = pl.pallas_call(
        functools.partial(strip_kernel, gs, cols_total, int(first)),
        in_specs=[VMEM] * len(operands),
        out_specs=[VMEM] * (3 if first else 1),
        out_shape=[jax.ShapeDtypeStruct((len(gs), 2, count, height), F32)]
        + ([jax.ShapeDtypeStruct((2, 2 * height, width), BF), jax.ShapeDtypeStruct((2, width), F32)] if first else []),
        compiler_params=LIMIT,
        cost_estimate=pl.CostEstimate(flops=cost, bytes_accessed=cost // 1000, transcendentals=0),
        name="strips",
    )(*operands)
    return out if first else out[0]


def pack_kernel(terms, *refs):
    weight_ref, row_ref, live_ref, out_ref = refs[terms:]
    count = refs[0].shape[2]
    strip = sum(ref[0] for ref in refs[:terms])
    out_ref[:count], out_ref[count : 2 * count] = strip[0], strip[1]
    width = out_ref.shape[1]
    weight = weight_ref[0]
    if count < width:
        weight = jnp.concatenate([weight, jnp.zeros((MAXB, width - count), F32)], 1)
    out_ref[2 * count : 2 * count + MAXB] = weight
    row = jnp.where(lanes(MAXB) < live_ref[0:1, 0:1], row_ref[...], -1).astype(F32)
    row = jnp.concatenate([row, jnp.zeros((1, width - MAXB), F32)], 1)
    out_ref[2 * count + MAXB :] = jnp.broadcast_to(row, (META, width))


def pack(terms, weight, row, live, count, height):
    return pl.pallas_call(
        functools.partial(pack_kernel, len(terms)),
        in_specs=[VMEM] * (len(terms) + 3),
        out_specs=VMEM,
        out_shape=jax.ShapeDtypeStruct((2 * count + MAXB + META, height), F32),
        compiler_params=LIMIT,
        name="pack",
    )(*terms, weight, row, live)


def add_message(starts, r, message, b_ref, roots_ref, state, height, count, rows_total):
    mine, other = starts[lax.axis_index("frow")], starts[r]
    strip, rest = message[: 2 * count], message[2 * count :]
    pc, ps = unit(mine * (r * height + lanes(height)), rows_total, 1.0 / math.sqrt(rows_total))
    re, im = strip[:count], strip[count:]
    re, im = re * pc + im * ps, im * pc - re * ps
    high, low = halves(jnp.concatenate([jnp.concatenate([re, im], 1), jnp.concatenate([im, -re], 1)]))
    part = lax.dot_general(
        jnp.concatenate([high, low, high], 1), b_ref[...].reshape(6 * height, rows_total), NN, preferred_element_type=F32
    )
    freq = lanes(rows_total)
    turn = lax.rem(r - lax.axis_index("frow") + rows_total // height, rows_total // height)
    pc, ps = roots_ref[turn, 0:1], roots_ref[turn, 1:2]
    re, im = part[:count], part[count:]
    add_re, add_im = re * pc + im * ps, im * pc - re * ps

    width = message.shape[1]
    flat = jnp.concatenate([rest, jnp.zeros((width - rest.shape[0], width), F32)])
    turned = jnp.transpose(flat)
    weight = turned[:count, :MAXB]
    row = turned[:MAXB, MAXB : MAXB + 1].astype(jnp.int32)
    place = jnp.where(row < 0, -1, (row + (other - mine)) & (rows_total - 1))
    hot = (lanes(rows_total, MAXB) == place).astype(F32).astype(BF)
    gain = lax.dot_general(
        jnp.concatenate(halves(weight), 1), jnp.concatenate([hot, hot]), NN, preferred_element_type=F32
    )
    gain = gain + (((freq + (mine - other)) & (rows_total - 1)) < SG).astype(F32)
    if state is None:
        return add_re, add_im, gain
    return state[0] + add_re, state[1] + add_im, state[2] + gain


def gather_kernel(steps, rows, height, count, starts, b_ref, roots_ref, *refs):
    state = None
    if len(refs) > len(steps) + 1:
        state, refs = (refs[0][0], refs[0][1], refs[0][2]), refs[1:]
    at = ring_place(lax.axis_index("frow"), rows)
    for step, message in zip(steps, refs):
        r = ring_block(at + step, rows)
        state = add_message(starts, r, message[...], b_ref, roots_ref, state, height, count, rows * height)
    for i in range(3):
        refs[-1][i] = state[i]


def gather_step(starts, table, roots, state, messages, steps, count):
    height, rows_total = table.shape[1:]
    operands = [table, roots] + ([] if state is None else [state]) + list(messages)
    return pl.pallas_call(
        functools.partial(gather_kernel, steps, rows_total // height, height, count),
        in_specs=[SMEM] + [VMEM] * len(operands),
        out_specs=VMEM,
        out_shape=jax.ShapeDtypeStruct((3, count, rows_total), F32),
        compiler_params=LIMIT,
        cost_estimate=pl.CostEstimate(flops=10**9, bytes_accessed=4 << 20, transcendentals=0),
        name="gather_step",
    )(starts, *operands)


def back_kernel(rows, height, count, starts, b_ref, turned_ref, roots_ref, state_ref, top_ref, bottom_ref, back_ref, sub_ref):
    state = state_ref[0], state_ref[1], state_ref[2]
    message = jnp.concatenate([top_ref[...], bottom_ref[...]])
    rows_total = rows * height
    own = lax.axis_index("frow")
    r = ring_block(ring_place(own, rows) + rows // 2, rows)
    re, im, gain = add_message(starts, r, message, b_ref, roots_ref, state, height, count, rows_total)
    sub_ref[0] = re[:, :SG]
    sub_ref[1] = im[:, :SG]
    high, low = halves(jnp.concatenate([re * gain, im * gain]))
    acc = lax.dot_general(high, turned_ref[...], NN, preferred_element_type=F32)
    acc = acc[:, : 2 * height] + (
        acc[:, 2 * height :] + lax.dot_general(low, turned_ref[:, : 2 * height], NN, preferred_element_type=F32)
    )
    re = acc[:count, :height] - acc[count:, height:]
    im = acc[count:, :height] + acc[:count, height:]
    pc, ps = unit(starts[own] * (own * height + lanes(height)), rows_total, 1.0 / math.sqrt(rows_total))
    back_ref[0] = jnp.transpose(re * pc - im * ps)
    back_ref[1] = jnp.transpose(im * pc + re * ps)


def back_step(starts, table, turned, roots, state, parts, count):
    height, rows_total = table.shape[1:]
    return pl.pallas_call(
        functools.partial(back_kernel, rows_total // height, height, count),
        in_specs=[SMEM] + [VMEM] * 6,
        out_specs=[VMEM] * 2,
        out_shape=[
            jax.ShapeDtypeStruct((2, height, count), F32),
            jax.ShapeDtypeStruct((2, count, SG), F32),
        ],
        compiler_params=LIMIT,
        name="back_step",
    )(starts, table, turned, roots, state, *parts)


def correct_kernel(sub_ref, gain_ref, roots_ref, out_ref):
    count = sub_ref.shape[1]
    pieces = SG // 128
    own = lax.axis_index("frow")
    pc, ps = roots_ref[own, 0:1, :SG], roots_ref[own, 1:2, :SG]
    re, im, gain = sub_ref[0], sub_ref[1], gain_ref[2, :, :SG]
    for part, value in enumerate([(re * pc + im * ps) * gain, (im * pc - re * ps) * gain]):
        for i in range(pieces):
            out_ref[pl.ds(2 * i + part, count, stride=2 * pieces), :] = value[:, 128 * i : 128 * (i + 1)]


def correct_step(sub, first_state, roots):
    count = sub.shape[1]
    out = pl.pallas_call(
        correct_kernel,
        in_specs=[VMEM] * 3,
        out_specs=VMEM,
        out_shape=jax.ShapeDtypeStruct((count * 2 * SG // 128, 128), F32),
        compiler_params=LIMIT,
        cost_estimate=pl.CostEstimate(flops=10**9, bytes_accessed=4 << 20, transcendentals=0),
        name="correct_step",
    )(sub, first_state, roots)
    out = out.reshape(count, SG // 128, 2, 128)
    return jnp.transpose(out, (0, 2, 1, 3)).reshape(1, count, 2, SG)


def image_kernel(gs, cols_total, first, last, phase_ref, e_ref, *refs):
    backs, refs = refs[: len(gs)], refs[len(gs) :]
    out_ref = refs[-1]
    _, height, width = out_ref.shape
    count = e_ref.shape[2]
    own = lax.axis_index("fcol")
    acc = None if first else jnp.concatenate([refs[0][0], refs[0][1]])
    for back, g in zip(backs, gs):
        freq = (own ^ g) * count + lanes(count)
        pc, ps = unit(freq * (own * width), cols_total)
        re, im = back[0], back[1]
        re, im = re * pc - im * ps, im * pc + re * ps
        left = halves(jnp.concatenate([jnp.concatenate([re, -im], 1), jnp.concatenate([im, re], 1)]))
        right = (e_ref[own ^ g, 0:2].reshape(2 * count, width), e_ref[own ^ g, 2:4].reshape(2 * count, width))
        part = dot3(left, right, NN)
        acc = part if acc is None else acc + part
    re, im = acc[:height], acc[height:]
    if last:
        pc, ps = phase_ref[0:1], phase_ref[1:2]
        re, im = re * pc - im * ps, im * pc + re * ps
    out_ref[0] = re
    out_ref[1] = im


def image_step(phase, table, gs, backs, acc, last, cols_total):
    width = table.shape[-1]
    height = backs[0].shape[1]
    first = acc is None
    operands = list(backs) + ([] if first else [acc])
    return pl.pallas_call(
        functools.partial(image_kernel, tuple(gs), cols_total, first, last),
        in_specs=[VMEM] * (2 + len(operands)),
        out_specs=VMEM,
        out_shape=jax.ShapeDtypeStruct((2, height, width), F32),
        compiler_params=LIMIT,
        cost_estimate=pl.CostEstimate(flops=10**9, bytes_accessed=4 << 20, transcendentals=0),
        name="image_step",
    )(phase, table, *operands)


def swap(value, axis, bit):
    return lax.ppermute(value, axis, [(i, i ^ bit) for i in range(lax.axis_size(axis))])


def per_device(facets, column_start, subgrid_start, vis_count, vis_row, vis_weight):
    rows = lax.axis_size("frow")
    cols = lax.axis_size("fcol")
    height, width = facets.shape[1:]
    rows_total, cols_total = height * rows, width * cols
    count = SG // cols
    assert vis_count.shape[0] == 1 and count <= height

    e_table = jnp.asarray(wave_table(SG, width, cols_total).reshape(4, cols, count, width).transpose(1, 0, 2, 3))
    b_table = wave_table(height, rows_total, rows_total)
    turned = jnp.asarray(b_table.reshape(4 * height, rows_total).T.copy())
    b_table = jnp.asarray(np.concatenate([b_table[:2], b_table]))
    angle = np.arange(rows)[:, None] * np.arange(rows_total)[None, :] % rows * (2.0 * np.pi / rows)
    roots = jnp.asarray(np.stack([np.cos(angle), np.sin(angle)], 1).astype(np.float32))

    top = cols // 2
    groups = [range(top + 1, cols, 2), range(top, cols, 2), range(1, top, 2), range(0, top, 2)]
    groups = [tuple(group) for group in groups]
    column_start = column_start.reshape(1, 1)
    waves = waves_of(count, width, cols_total)
    sent, z, phase = strips(column_start, facets, waves, groups[0], cols_total, first=True)
    far = strips(column_start, z, waves, groups[1], cols_total) + swap(sent, "fcol", 1)
    far, z = lax.optimization_barrier((far, z))
    far = swap(far, "fcol", top)
    sent = strips(column_start, z, waves, groups[2], cols_total, cost=10**6)
    terms = [strips(column_start, z, waves, groups[3], cols_total, cost=10**6), swap(sent, "fcol", 1), far]
    bit = 2
    while bit < top:
        pairs = sum(terms).reshape((-1, 2) + far.shape[1:])
        terms = [pairs[:, 0], swap(pairs[:, 1], "fcol", bit)]
        bit *= 2

    own = pack(terms, vis_weight, vis_row, vis_count.reshape(1, 1), count, height)
    order = list(range(0, rows, 2)) + list(range(rows - 1, 0, -2))
    ahead = [(order[i], order[(i + 1) % rows]) for i in range(rows)]
    behind = [(b, a) for a, b in ahead]
    first_state = state = gather_step(subgrid_start, b_table, roots, None, [own], (0,), count)
    up = down = own
    for step in range(1, rows // 2):
        up = lax.ppermute(up, "frow", ahead)
        down = lax.ppermute(down, "frow", behind)
        up, state = lax.optimization_barrier((up, state))
        state = gather_step(subgrid_start, b_table, roots, state, [up, down], (-step, step), count)
    cut = (own.shape[0] // 2 + 7) // 8 * 8
    parts = [lax.ppermute(up[:cut], "frow", ahead), lax.ppermute(down[cut:], "frow", behind)]
    back, sub = back_step(subgrid_start, b_table, turned, roots, state, parts, count)

    near, far = {0: back}, {top: swap(back, "fcol", top)}

    def spread(blocks, bit):
        return {g ^ bit: swap(b, "fcol", bit) for g, b in blocks.items()}

    def image(blocks, acc, last=False):
        return image_step(phase, e_table, blocks.keys(), list(blocks.values()), acc, last, cols_total)

    bit = top // 2
    while bit >= 1:
        near |= spread(near, bit)
        bit //= 2
    acc = image(near, None)
    corrected = correct_step(sub, first_state, roots)
    far[top], acc, corrected = lax.optimization_barrier((far[top], acc, corrected))
    bit = top // 2
    while bit > 1:
        far |= spread(far, bit)
        bit //= 2
    rest = spread(far, 1)
    acc = image(far, acc)
    return corrected, image(rest, acc, last=True)


def solution(mesh):
    return jax.shard_map(
        per_device,
        mesh=mesh,
        in_specs=(
            P(None, "frow", "fcol"),
            P(),
            P(),
            P("frow"),
            P("frow", None),
            P("frow", None, "fcol"),
        ),
        out_specs=(P("frow", "fcol", None, None), P(None, "frow", "fcol")),
        check_vma=False,
    )
```

```python
import functools
import math

import jax
import jax.numpy as jnp
import ml_dtypes
import numpy as np
from jax import lax
from jax.experimental import pallas as pl
from jax.experimental.pallas import tpu as pltpu
from jax.sharding import PartitionSpec as P

SG = 512
MAXB = 64
META = 8

BF = jnp.bfloat16
F32 = jnp.float32
NN = (((1,), (0,)), ((), ()))
NT = (((1,), (1,)), ((), ()))
VMEM = pl.BlockSpec(memory_space=pltpu.VMEM)
SMEM = pl.BlockSpec(memory_space=pltpu.SMEM)
LIMIT = pltpu.CompilerParams(vmem_limit_bytes=32 << 20)


def halves(value):
    high = value.astype(BF)
    return high, (value - high.astype(F32)).astype(BF)


def dot3(left, right, dims):
    def dot(a, b):
        return lax.dot_general(a, b, dims, preferred_element_type=F32)
    return dot(left[0], right[0]) + (dot(left[0], right[1]) + dot(left[1], right[0]))


def unit(phase, modulus, scale=1.0):
    angle = (phase & (modulus - 1)).astype(F32) * F32(2.0 * math.pi / modulus)
    return jnp.cos(angle) * F32(scale), jnp.sin(angle) * F32(scale)


def lanes(count, rows=1):
    return lax.broadcasted_iota(jnp.int32, (rows, count), 1)


def wave_parts(rows, stride, cols, modulus):
    phase = np.arange(rows, dtype=np.int64)[:, None] * (stride * np.arange(cols, dtype=np.int64))[None, :] % modulus
    angle = phase * (2.0 * np.pi / modulus)
    return np.stack([np.cos(angle), np.sin(angle)])


def wave_table(rows, cols, modulus):
    parts = wave_parts(rows, 1, cols, modulus)
    high = parts.astype(ml_dtypes.bfloat16)
    low = (parts - high.astype(np.float64)).astype(ml_dtypes.bfloat16)
    return np.concatenate([high, low])


def ring_place(r, rows):
    return jnp.where(lax.rem(r, 2) == 0, r // 2, rows - 1 - r // 2)


def ring_block(place, rows):
    place = lax.rem(place + rows, rows)
    return jnp.where(place < rows // 2, 2 * place, 2 * (rows - 1 - place) + 1)


def wave_kernel(width, cols_total, base_ref, steps_ref):
    own = lax.axis_index("fcol")
    blocks, _, count, _ = base_ref.shape
    row = lax.broadcasted_iota(jnp.int32, (count, 128), 0)
    for ref, coord in ((base_ref, lanes(128)), (steps_ref, lanes(128) * 128 + own * width)):
        cos, sin = unit(row * coord, cols_total)
        for g in range(blocks):
            pc, ps = unit((own ^ g) * count * coord, cols_total)
            ref[g, 0] = cos * pc - sin * ps
            ref[g, 1] = sin * pc + cos * ps


def waves_of(count, width, cols_total):
    shape = jax.ShapeDtypeStruct((SG // count, 2, count, 128), F32)
    return pl.pallas_call(
        functools.partial(wave_kernel, width, cols_total),
        out_specs=[VMEM] * 2,
        out_shape=[shape] * 2,
        compiler_params=LIMIT,
        cost_estimate=pl.CostEstimate(flops=10**9, bytes_accessed=2 << 20, transcendentals=0),
        name="waves",
    )()


def strip_kernel(gs, cols_total, first, *refs):
    source_ref, base_ref, steps_ref, out_ref = refs[1:5] if first else refs
    own = lax.axis_index("fcol")
    height, width = out_ref.shape[-1], source_ref.shape[-1]
    if first:
        pc, ps = unit(refs[0][0:1, 0:1] * (own * width + lanes(width)), cols_total, 1.0 / math.sqrt(cols_total))
        re, im = source_ref[0], source_ref[1]
        z = halves(jnp.concatenate([re * pc + im * ps, im * pc - re * ps]))
        z_ref, phase_ref = refs[5:]
        z_ref[0], z_ref[1] = z
        phase_ref[0:1], phase_ref[1:2] = pc, ps
    else:
        z = source_ref[0], source_ref[1]
    for i, g in enumerate(gs):
        turn_cos, turn_sin, base_cos, base_sin = steps_ref[g, 0], steps_ref[g, 1], base_ref[g, 0], base_ref[g, 1]
        cos, sin = [], []
        for t in range(width // 128):
            tc, ts = turn_cos[:, t : t + 1], turn_sin[:, t : t + 1]
            cos.append(tc * base_cos - ts * base_sin)
            sin.append(ts * base_cos + tc * base_sin)
        waves = halves(jnp.concatenate([jnp.concatenate(cos, 1), jnp.concatenate(sin, 1)]))
        acc = dot3(waves, z, NT)
        count = out_ref.shape[2]
        cos, sin = acc[:count], acc[count:]
        out_ref[i, 0] = cos[:, :height] + sin[:, height:]
        out_ref[i, 1] = cos[:, height:] - sin[:, :height]


def strips(column_start, source, waves, gs, cols_total, first=False):
    count = waves[0].shape[2]
    height, width = source.shape[1] // (1 if first else 2), source.shape[2]
    operands = ([column_start] if first else []) + [source, *waves]
    out = pl.pallas_call(
        functools.partial(strip_kernel, gs, cols_total, int(first)),
        in_specs=[VMEM] * len(operands),
        out_specs=[VMEM] * (3 if first else 1),
        out_shape=[jax.ShapeDtypeStruct((len(gs), 2, count, height), F32)]
        + ([jax.ShapeDtypeStruct((2, 2 * height, width), BF), jax.ShapeDtypeStruct((2, width), F32)] if first else []),
        compiler_params=LIMIT,
        cost_estimate=pl.CostEstimate(flops=10**9, bytes_accessed=2 << 20, transcendentals=0),
        name="strips",
    )(*operands)
    return out if first else out[0]


def pack_kernel(terms, *refs):
    weight_ref, row_ref, live_ref, out_ref = refs[terms:]
    count = refs[0].shape[2]
    strip = sum(ref[0] for ref in refs[:terms])
    out_ref[:count], out_ref[count : 2 * count] = strip[0], strip[1]
    width = out_ref.shape[1]
    weight = weight_ref[0]
    if count < width:
        weight = jnp.concatenate([weight, jnp.zeros((MAXB, width - count), F32)], 1)
    out_ref[2 * count : 2 * count + MAXB] = weight
    row = jnp.where(lanes(MAXB) < live_ref[0:1, 0:1], row_ref[...], -1).astype(F32)
    row = jnp.concatenate([row, jnp.zeros((1, width - MAXB), F32)], 1)
    out_ref[2 * count + MAXB :] = jnp.broadcast_to(row, (META, width))


def pack(terms, weight, row, live, count, height):
    return pl.pallas_call(
        functools.partial(pack_kernel, len(terms)),
        in_specs=[VMEM] * (len(terms) + 3),
        out_specs=VMEM,
        out_shape=jax.ShapeDtypeStruct((2 * count + MAXB + META, height), F32),
        compiler_params=LIMIT,
        name="pack",
    )(*terms, weight, row, live)


class Message:
    def __init__(self, starts, r, message, b_ref, roots_ref, height, count, rows_total):
        own = lax.axis_index("frow")
        mine, other = starts[own], starts[r]
        strip, rest = message[: 2 * count], message[2 * count :]
        pc, ps = unit(mine * (r * height + lanes(height)), rows_total, 1.0 / math.sqrt(rows_total))
        re, im = strip[:count], strip[count:]
        re, im = re * pc + im * ps, im * pc - re * ps
        high, low = halves(jnp.concatenate([jnp.concatenate([re, im], 1), jnp.concatenate([im, -re], 1)]))
        self.left = jnp.concatenate([high, low, high], 1)

        width = message.shape[1]
        flat = jnp.concatenate([rest, jnp.zeros((width - rest.shape[0], width), F32)])
        turned = jnp.transpose(flat)
        self.weight = jnp.concatenate(halves(turned[:count, :MAXB]), 1)
        row = turned[:MAXB, MAXB : MAXB + 1].astype(jnp.int32)
        self.place = jnp.where(row < 0, -1, (row + (other - mine)) & (rows_total - 1))
        self.away = mine - other
        self.turn = lax.rem(r - own + rows_total // height, rows_total // height)
        self.refs, self.count, self.rows_total = (b_ref, roots_ref), count, rows_total

    def chunk(self, begin, size):
        b_ref, roots_ref = self.refs
        part = lax.dot_general(self.left, b_ref[:, begin : begin + size], NN, preferred_element_type=F32)
        pc, ps = roots_ref[self.turn, 0:1, begin : begin + size], roots_ref[self.turn, 1:2, begin : begin + size]
        re, im = part[: self.count], part[self.count :]
        freq = begin + lanes(size)
        hot = (begin + lanes(size, MAXB) == self.place).astype(F32).astype(BF)
        gain = lax.dot_general(self.weight, jnp.concatenate([hot, hot]), NN, preferred_element_type=F32)
        seen = (((freq + self.away) & (self.rows_total - 1)) < SG).astype(F32)
        return re * pc + im * ps, im * pc - re * ps, gain + seen


def chunks(total, size=256):
    return [(begin, min(size, total - begin)) for begin in range(0, total, size)]


def gather_kernel(steps, rows, height, count, starts, b_ref, roots_ref, *refs):
    state_ref = None
    if len(refs) > len(steps) + 1:
        state_ref, refs = refs[0], refs[1:]
    at = ring_place(lax.axis_index("frow"), rows)
    found = [
        Message(starts, ring_block(at + step, rows), message[...], b_ref, roots_ref, height, count, rows * height)
        for step, message in zip(steps, refs)
    ]
    for begin, size in chunks(rows * height):
        terms = [message.chunk(begin, size) for message in found]
        for i in range(3):
            value = sum(term[i] for term in terms)
            if state_ref is not None:
                value = value + state_ref[i, :, begin : begin + size]
            refs[-1][i, :, begin : begin + size] = value


def gather_step(starts, table, roots, state, messages, steps, height):
    rows_total = table.shape[1]
    count = (messages[0].shape[0] - MAXB - META) // 2
    operands = [table, roots] + ([] if state is None else [state]) + list(messages)
    return pl.pallas_call(
        functools.partial(gather_kernel, steps, rows_total // height, height, count),
        in_specs=[SMEM] + [VMEM] * len(operands),
        out_specs=VMEM,
        out_shape=jax.ShapeDtypeStruct((3, count, rows_total), F32),
        compiler_params=LIMIT,
        cost_estimate=pl.CostEstimate(flops=10**9, bytes_accessed=4 << 20, transcendentals=0),
        name="gather_step",
    )(starts, *operands)


def back_kernel(rows, height, count, starts, b_ref, turned_ref, roots_ref, state_ref, message_ref, back_ref, sub_ref):
    rows_total = rows * height
    own = lax.axis_index("frow")
    r = ring_block(ring_place(own, rows) + rows // 2, rows)
    message = Message(starts, r, message_ref[...], b_ref, roots_ref, height, count, rows_total)
    acc = None
    for begin, size in chunks(rows_total):
        terms = message.chunk(begin, size)
        re, im, gain = [term + state_ref[i, :, begin : begin + size] for i, term in enumerate(terms)]
        if begin < SG:
            sub_ref[0, :, begin : begin + size] = re
            sub_ref[1, :, begin : begin + size] = im
        high, low = halves(jnp.concatenate([re * gain, im * gain]))
        table = turned_ref[begin : begin + size]
        part = lax.dot_general(high, table, NN, preferred_element_type=F32)
        part = part[:, : 2 * height] + (
            part[:, 2 * height :] + lax.dot_general(low, table[:, : 2 * height], NN, preferred_element_type=F32)
        )
        acc = part if acc is None else acc + part
    re = acc[:count, :height] - acc[count:, height:]
    im = acc[count:, :height] + acc[:count, height:]
    pc, ps = unit(starts[own] * (own * height + lanes(height)), rows_total, 1.0 / math.sqrt(rows_total))
    back_ref[0] = jnp.transpose(re * pc - im * ps)
    back_ref[1] = jnp.transpose(im * pc + re * ps)


def back_step(starts, table, turned, roots, state, message, height):
    count, rows_total = state.shape[1:]
    return pl.pallas_call(
        functools.partial(back_kernel, rows_total // height, height, count),
        in_specs=[SMEM] + [VMEM] * 5,
        out_specs=[VMEM] * 2,
        out_shape=[
            jax.ShapeDtypeStruct((2, height, count), F32),
            jax.ShapeDtypeStruct((2, count, SG), F32),
        ],
        compiler_params=LIMIT,
        name="back_step",
    )(starts, table, turned, roots, state, message)


def correct_kernel(sub_ref, gain_ref, roots_ref, out_ref):
    count = sub_ref.shape[1]
    pieces = SG // 128
    own = lax.axis_index("frow")
    pc, ps = roots_ref[own, 0:1, :SG], roots_ref[own, 1:2, :SG]
    re, im, gain = sub_ref[0], sub_ref[1], gain_ref[2, :, :SG]
    for part, value in enumerate([(re * pc + im * ps) * gain, (im * pc - re * ps) * gain]):
        for i in range(pieces):
            out_ref[pl.ds(2 * i + part, count, stride=2 * pieces), :] = value[:, 128 * i : 128 * (i + 1)]


def correct_step(sub, first_state, roots):
    count = sub.shape[1]
    out = pl.pallas_call(
        correct_kernel,
        in_specs=[VMEM] * 3,
        out_specs=VMEM,
        out_shape=jax.ShapeDtypeStruct((count * 2 * SG // 128, 128), F32),
        compiler_params=LIMIT,
        cost_estimate=pl.CostEstimate(flops=10**9, bytes_accessed=4 << 20, transcendentals=0),
        name="correct_step",
    )(sub, first_state, roots)
    out = out.reshape(count, SG // 128, 2, 128)
    return jnp.transpose(out, (0, 2, 1, 3)).reshape(1, count, 2, SG)


def image_kernel(gs, first, last, phase_ref, e_ref, *refs):
    backs, refs = refs[: len(gs)], refs[len(gs) :]
    acc_ref = None if first else refs[0]
    out_ref = refs[0 if first else 1]
    if last:
        scratch, sems = refs[-2:]
    width = e_ref.shape[-1]
    height, count = backs[0].shape[1:]
    own = lax.axis_index("fcol")
    left = []
    for back, g in zip(backs, gs):
        freq = (own ^ g) * count + lanes(count)
        pc, ps = unit(freq * (own * width), e_ref.shape[0] * width)
        re, im = back[0], back[1]
        re, im = re * pc - im * ps, im * pc + re * ps
        left.append(halves(jnp.concatenate([jnp.concatenate([re, -im], 1), jnp.concatenate([im, re], 1)])))
    copies = []
    for begin, size in chunks(width):
        columns = slice(begin, begin + size)
        acc = None if first else jnp.concatenate([acc_ref[0, :, columns], acc_ref[1, :, columns]])
        for (high, low), g in zip(left, gs):
            e = e_ref[own ^ g, 0:2, :, columns], e_ref[own ^ g, 2:4, :, columns]
            part = dot3((high, low), [value.reshape(2 * count, size) for value in e], NN)
            acc = part if acc is None else acc + part
        re, im = acc[:height], acc[height:]
        if last:
            pc, ps = phase_ref[0:1, columns], phase_ref[1:2, columns]
            scratch[0, :, columns] = re * pc - im * ps
            scratch[1, :, columns] = im * pc + re * ps
            copies.append(
                pltpu.make_async_copy(scratch.at[:, :, columns], out_ref.at[:, :, columns], sems.at[len(copies)])
            )
            copies[-1].start()
        else:
            out_ref[0, :, columns] = re
            out_ref[1, :, columns] = im
    for copy in copies:
        copy.wait()


def image_step(phase, table, gs, backs, acc, last):
    width = table.shape[-1]
    height = backs[0].shape[1]
    first = acc is None
    operands = list(backs) + ([] if first else [acc])
    return pl.pallas_call(
        functools.partial(image_kernel, tuple(gs), first, last),
        in_specs=[VMEM] * (2 + len(operands)),
        out_specs=pl.BlockSpec(memory_space=pl.ANY) if last else VMEM,
        out_shape=jax.ShapeDtypeStruct((2, height, width), F32),
        scratch_shapes=[pltpu.VMEM((2, height, width), F32), pltpu.SemaphoreType.DMA((len(chunks(width)),))] if last else [],
        compiler_params=LIMIT,
        cost_estimate=pl.CostEstimate(flops=10**9, bytes_accessed=4 << 20, transcendentals=0),
        name="image_step",
    )(phase, table, *operands)


def swap(value, axis, bit):
    return lax.ppermute(value, axis, [(i, i ^ bit) for i in range(lax.axis_size(axis))])


def per_device(facets, column_start, subgrid_start, vis_count, vis_row, vis_weight):
    rows = lax.axis_size("frow")
    cols = lax.axis_size("fcol")
    height, width = facets.shape[1:]
    rows_total, cols_total = height * rows, width * cols
    count = SG // cols
    assert vis_count.shape[0] == 1 and count <= height

    e_table = jnp.asarray(wave_table(SG, width, cols_total).reshape(4, cols, count, width).transpose(1, 0, 2, 3))
    b_table = wave_table(height, rows_total, rows_total)
    turned = jnp.asarray(b_table.reshape(4 * height, rows_total).T.copy())
    b_table = jnp.asarray(np.concatenate([b_table[:2], b_table]).reshape(6 * height, rows_total))
    angle = np.arange(rows)[:, None] * np.arange(rows_total)[None, :] % rows * (2.0 * np.pi / rows)
    roots = jnp.asarray(np.stack([np.cos(angle), np.sin(angle)], 1).astype(np.float32))

    top = cols // 2
    column_start = column_start.reshape(1, 1)
    waves = waves_of(count, width, cols_total)
    groups = [tuple(range(1, cols, 2)), tuple(range(top, cols, 2)), tuple(range(0, top, 2))]
    sent, z, phase = strips(column_start, facets, waves, groups[0], cols_total, first=True)
    far = strips(column_start, z, waves, groups[1], cols_total)
    got = swap(sent, "fcol", 1)
    far, got = lax.optimization_barrier((far + got[top // 2 :], got))
    terms = [strips(column_start, z, waves, groups[2], cols_total), got, swap(far, "fcol", top)]
    bit = 2
    while bit < top:
        terms[1] = terms[1][: terms[0].shape[0]]
        pairs = sum(terms).reshape((-1, 2) + far.shape[1:])
        terms = [pairs[:, 0], swap(pairs[:, 1], "fcol", bit)]
        bit *= 2

    own = pack(terms, vis_weight, vis_row, vis_count.reshape(1, 1), count, height)
    order = list(range(0, rows, 2)) + list(range(rows - 1, 0, -2))
    ahead = [(order[i], order[(i + 1) % rows]) for i in range(rows)]
    behind = [(b, a) for a, b in ahead]
    first_state = state = gather_step(subgrid_start, b_table, roots, None, [own], (0,), height)
    up = down = own
    for step in range(1, rows // 2):
        up = lax.ppermute(up, "frow", ahead)
        down = lax.ppermute(down, "frow", behind)
        up, state = lax.optimization_barrier((up, state))
        state = gather_step(subgrid_start, b_table, roots, state, [up, down], (-step, step), height)
    up = lax.ppermute(up, "frow", ahead)
    back, sub = back_step(subgrid_start, b_table, turned, roots, state, up, height)

    near, far = {0: back}, {top: swap(back, "fcol", top)}

    def spread(blocks, bit):
        return {g ^ bit: swap(b, "fcol", bit) for g, b in blocks.items()}

    def image(blocks, acc, last=False):
        return image_step(phase, e_table, blocks.keys(), list(blocks.values()), acc, last)

    bit = top // 2
    while bit >= 1:
        near |= spread(near, bit)
        bit //= 2
    acc = image(near, None)
    corrected = correct_step(sub, first_state, roots)
    far[top], acc, corrected = lax.optimization_barrier((far[top], acc, corrected))
    bit = top // 2
    while bit > 1:
        far |= spread(far, bit)
        bit //= 2
    rest = spread(far, 1)
    acc = image(far, acc)
    return corrected, image(rest, acc, last=True)


def solution(mesh):
    return jax.shard_map(
        per_device,
        mesh=mesh,
        in_specs=(
            P(None, "frow", "fcol"),
            P(),
            P(),
            P("frow"),
            P("frow", None),
            P("frow", None, "fcol"),
        ),
        out_specs=(P("frow", "fcol", None, None), P(None, "frow", "fcol")),
        check_vma=False,
    )
```

```python
import functools
import math

import jax
import jax.numpy as jnp
import ml_dtypes
import numpy as np
from jax import lax
from jax.experimental import pallas as pl
from jax.experimental.pallas import tpu as pltpu
from jax.sharding import PartitionSpec as P

SG = 512
MAXB = 64
META = 8

BF = jnp.bfloat16
F32 = jnp.float32
NN = (((1,), (0,)), ((), ()))
NT = (((1,), (1,)), ((), ()))
VMEM = pl.BlockSpec(memory_space=pltpu.VMEM)
SMEM = pl.BlockSpec(memory_space=pltpu.SMEM)
LIMIT = pltpu.CompilerParams(vmem_limit_bytes=32 << 20)


def halves(value):
    high = value.astype(BF)
    return high, (value - high.astype(F32)).astype(BF)


def dot3(left, right, dims):
    def dot(a, b):
        return lax.dot_general(a, b, dims, preferred_element_type=F32)
    return dot(left[0], right[0]) + (dot(left[0], right[1]) + dot(left[1], right[0]))


def unit(phase, modulus, scale=1.0):
    angle = (phase & (modulus - 1)).astype(F32) * F32(2.0 * math.pi / modulus)
    return jnp.cos(angle) * F32(scale), jnp.sin(angle) * F32(scale)


def lanes(count, rows=1):
    return lax.broadcasted_iota(jnp.int32, (rows, count), 1)


def wave_parts(rows, stride, cols, modulus):
    phase = np.arange(rows, dtype=np.int64)[:, None] * (stride * np.arange(cols, dtype=np.int64))[None, :] % modulus
    angle = phase * (2.0 * np.pi / modulus)
    return np.stack([np.cos(angle), np.sin(angle)])


def wave_table(rows, cols, modulus):
    parts = wave_parts(rows, 1, cols, modulus)
    high = parts.astype(ml_dtypes.bfloat16)
    low = (parts - high.astype(np.float64)).astype(ml_dtypes.bfloat16)
    return np.concatenate([high, low])


def ring_place(r, rows):
    return jnp.where(lax.rem(r, 2) == 0, r // 2, rows - 1 - r // 2)


def ring_block(place, rows):
    place = lax.rem(place + rows, rows)
    return jnp.where(place < rows // 2, 2 * place, 2 * (rows - 1 - place) + 1)


def wave_kernel(width, cols_total, base_ref, steps_ref):
    own = lax.axis_index("fcol")
    blocks, _, count, _ = base_ref.shape
    row = lax.broadcasted_iota(jnp.int32, (count, 128), 0)
    for ref, coord in ((base_ref, lanes(128)), (steps_ref, lanes(128) * 128 + own * width)):
        cos, sin = unit(row * coord, cols_total)
        for g in range(blocks):
            pc, ps = unit((own ^ g) * count * coord, cols_total)
            ref[g, 0] = cos * pc - sin * ps
            ref[g, 1] = sin * pc + cos * ps


def waves_of(count, width, cols_total):
    shape = jax.ShapeDtypeStruct((SG // count, 2, count, 128), F32)
    return pl.pallas_call(
        functools.partial(wave_kernel, width, cols_total),
        out_specs=[VMEM] * 2,
        out_shape=[shape] * 2,
        compiler_params=LIMIT,
        cost_estimate=pl.CostEstimate(flops=10**9, bytes_accessed=2 << 20, transcendentals=0),
        name="waves",
    )()


def strip_kernel(groups, cols_total, *refs):
    first = len(refs) == 6 + len(groups)
    source_ref, base_ref, steps_ref, out_refs = refs[0], refs[1], refs[2], refs[3 : 3 + len(groups)]
    if first:
        start_ref, (source_ref, base_ref, steps_ref), out_refs = refs[0], refs[1:4], refs[4 : 4 + len(groups)]
    width = source_ref.shape[-1]
    if first:
        own = lax.axis_index("fcol")
        pc, ps = unit(start_ref[0:1, 0:1] * (own * width + lanes(width)), cols_total, 1.0 / math.sqrt(cols_total))
        re, im = source_ref[0], source_ref[1]
        z = halves(jnp.concatenate([re * pc + im * ps, im * pc - re * ps]))
        z_ref, phase_ref = refs[-2:]
        z_ref[0], z_ref[1] = z
        phase_ref[0:1], phase_ref[1:2] = pc, ps
    else:
        z = source_ref[0], source_ref[1]
    for gs, out_ref in zip(groups, out_refs):
        count, height = out_ref.shape[-2:]
        for i, g in enumerate(gs):
            turn_cos, turn_sin, base_cos, base_sin = steps_ref[g, 0], steps_ref[g, 1], base_ref[g, 0], base_ref[g, 1]
            cos, sin = [], []
            for t in range(width // 128):
                tc, ts = turn_cos[:, t : t + 1], turn_sin[:, t : t + 1]
                cos.append(tc * base_cos - ts * base_sin)
                sin.append(ts * base_cos + tc * base_sin)
            waves = halves(jnp.concatenate([jnp.concatenate(cos, 1), jnp.concatenate(sin, 1)]))
            acc = dot3(waves, z, NT)
            cos, sin = acc[:count], acc[count:]
            out_ref[i, 0] = cos[:, :height] + sin[:, height:]
            out_ref[i, 1] = cos[:, height:] - sin[:, :height]


def strips(column_start, source, waves, *groups, first=False, cost=10**9):
    cols, _, count, _ = waves[0].shape
    height, width = source.shape[1] // (1 if first else 2), source.shape[2]
    operands = ([column_start] if first else []) + [source, *waves]
    return pl.pallas_call(
        functools.partial(strip_kernel, groups, cols * width),
        in_specs=[VMEM] * len(operands),
        out_specs=[VMEM] * (len(groups) + (2 if first else 0)),
        out_shape=[jax.ShapeDtypeStruct((len(gs), 2, count, height), F32) for gs in groups]
        + ([jax.ShapeDtypeStruct((2, 2 * height, width), BF), jax.ShapeDtypeStruct((2, width), F32)] if first else []),
        compiler_params=LIMIT,
        cost_estimate=pl.CostEstimate(flops=cost, bytes_accessed=2 << 20, transcendentals=0),
        name="strips",
    )(*operands)


def pack_kernel(terms, *refs):
    weight_ref, row_ref, live_ref, out_ref = refs[terms:]
    count = refs[0].shape[2]
    strip = sum(ref[0] for ref in refs[:terms])
    out_ref[:count], out_ref[count : 2 * count] = strip[0], strip[1]
    width = out_ref.shape[1]
    weight = weight_ref[0]
    if count < width:
        weight = jnp.concatenate([weight, jnp.zeros((MAXB, width - count), F32)], 1)
    out_ref[2 * count : 2 * count + MAXB] = weight
    row = jnp.where(lanes(MAXB) < live_ref[0:1, 0:1], row_ref[...], -1).astype(F32)
    row = jnp.concatenate([row, jnp.zeros((1, width - MAXB), F32)], 1)
    out_ref[2 * count + MAXB :] = jnp.broadcast_to(row, (META, width))


def pack(terms, weight, row, live, count, height):
    return pl.pallas_call(
        functools.partial(pack_kernel, len(terms)),
        in_specs=[VMEM] * (len(terms) + 3),
        out_specs=VMEM,
        out_shape=jax.ShapeDtypeStruct((2 * count + MAXB + META, height), F32),
        compiler_params=LIMIT,
        name="pack",
    )(*terms, weight, row, live)


class Message:
    def __init__(self, starts, r, message, b_ref, roots_ref, height, count, rows_total):
        own = lax.axis_index("frow")
        mine, other = starts[own], starts[r]
        strip, rest = message[: 2 * count], message[2 * count :]
        pc, ps = unit(mine * (r * height + lanes(height)), rows_total, 1.0 / math.sqrt(rows_total))
        re, im = strip[:count], strip[count:]
        re, im = re * pc + im * ps, im * pc - re * ps
        high, low = halves(jnp.concatenate([jnp.concatenate([re, im], 1), jnp.concatenate([im, -re], 1)]))
        self.left = jnp.concatenate([high, low, high], 1)

        width = message.shape[1]
        flat = jnp.concatenate([rest, jnp.zeros((width - rest.shape[0], width), F32)])
        turned = jnp.transpose(flat)
        self.weight = jnp.concatenate(halves(turned[:count, :MAXB]), 1)
        row = turned[:MAXB, MAXB : MAXB + 1].astype(jnp.int32)
        self.place = jnp.where(row < 0, -1, (row + (other - mine)) & (rows_total - 1))
        self.away = mine - other
        self.turn = lax.rem(r - own + rows_total // height, rows_total // height)
        self.refs, self.count, self.rows_total = (b_ref, roots_ref), count, rows_total

    def chunk(self, begin, size):
        b_ref, roots_ref = self.refs
        part = lax.dot_general(self.left, b_ref[:, begin : begin + size], NN, preferred_element_type=F32)
        pc, ps = roots_ref[self.turn, 0:1, begin : begin + size], roots_ref[self.turn, 1:2, begin : begin + size]
        re, im = part[: self.count], part[self.count :]
        freq = begin + lanes(size)
        hot = (begin + lanes(size, MAXB) == self.place).astype(F32).astype(BF)
        gain = lax.dot_general(self.weight, jnp.concatenate([hot, hot]), NN, preferred_element_type=F32)
        seen = (((freq + self.away) & (self.rows_total - 1)) < SG).astype(F32)
        return re * pc + im * ps, im * pc - re * ps, gain + seen


def chunks(total, size=256):
    return [(begin, min(size, total - begin)) for begin in range(0, total, size)]


def gather_kernel(steps, rows, height, count, starts, b_ref, roots_ref, *refs):
    state_ref = None
    if len(refs) > len(steps) + 1:
        state_ref, refs = refs[0], refs[1:]
    at = ring_place(lax.axis_index("frow"), rows)
    found = [
        Message(starts, ring_block(at + step, rows), message[...], b_ref, roots_ref, height, count, rows * height)
        for step, message in zip(steps, refs)
    ]
    for begin, size in chunks(rows * height):
        terms = [message.chunk(begin, size) for message in found]
        for i in range(3):
            value = sum(term[i] for term in terms)
            if state_ref is not None:
                value = value + state_ref[i, :, begin : begin + size]
            refs[-1][i, :, begin : begin + size] = value


def gather_step(starts, table, roots, state, messages, steps, height):
    rows_total = table.shape[1]
    count = (messages[0].shape[0] - MAXB - META) // 2
    operands = [table, roots] + ([] if state is None else [state]) + list(messages)
    return pl.pallas_call(
        functools.partial(gather_kernel, steps, rows_total // height, height, count),
        in_specs=[SMEM] + [VMEM] * len(operands),
        out_specs=VMEM,
        out_shape=jax.ShapeDtypeStruct((3, count, rows_total), F32),
        compiler_params=LIMIT,
        cost_estimate=pl.CostEstimate(flops=10**9, bytes_accessed=4 << 20, transcendentals=0),
        name="gather_step",
    )(starts, *operands)


def back_kernel(rows, height, count, starts, b_ref, turned_ref, roots_ref, state_ref, message_ref, back_ref, sub_ref):
    rows_total = rows * height
    own = lax.axis_index("frow")
    r = ring_block(ring_place(own, rows) + rows // 2, rows)
    message = Message(starts, r, message_ref[...], b_ref, roots_ref, height, count, rows_total)
    acc = None
    for begin, size in chunks(rows_total):
        terms = message.chunk(begin, size)
        re, im, gain = [term + state_ref[i, :, begin : begin + size] for i, term in enumerate(terms)]
        if begin < SG:
            sub_ref[0, :, begin : begin + size] = re
            sub_ref[1, :, begin : begin + size] = im
        high, low = halves(jnp.concatenate([re * gain, im * gain]))
        table = turned_ref[begin : begin + size]
        part = lax.dot_general(high, table, NN, preferred_element_type=F32)
        part = part[:, : 2 * height] + (
            part[:, 2 * height :] + lax.dot_general(low, table[:, : 2 * height], NN, preferred_element_type=F32)
        )
        acc = part if acc is None else acc + part
    re = acc[:count, :height] - acc[count:, height:]
    im = acc[count:, :height] + acc[:count, height:]
    pc, ps = unit(starts[own] * (own * height + lanes(height)), rows_total, 1.0 / math.sqrt(rows_total))
    back_ref[0] = jnp.transpose(re * pc - im * ps)
    back_ref[1] = jnp.transpose(im * pc + re * ps)


def back_step(starts, table, turned, roots, state, message, height):
    count, rows_total = state.shape[1:]
    return pl.pallas_call(
        functools.partial(back_kernel, rows_total // height, height, count),
        in_specs=[SMEM] + [VMEM] * 5,
        out_specs=[VMEM] * 2,
        out_shape=[
            jax.ShapeDtypeStruct((2, height, count), F32),
            jax.ShapeDtypeStruct((2, count, SG), F32),
        ],
        compiler_params=LIMIT,
        name="back_step",
    )(starts, table, turned, roots, state, message)


def correct_kernel(sub_ref, gain_ref, roots_ref, out_ref):
    count = sub_ref.shape[1]
    pieces = SG // 128
    own = lax.axis_index("frow")
    pc, ps = roots_ref[own, 0:1, :SG], roots_ref[own, 1:2, :SG]
    re, im, gain = sub_ref[0], sub_ref[1], gain_ref[2, :, :SG]
    for part, value in enumerate([(re * pc + im * ps) * gain, (im * pc - re * ps) * gain]):
        for i in range(pieces):
            out_ref[pl.ds(2 * i + part, count, stride=2 * pieces), :] = value[:, 128 * i : 128 * (i + 1)]


def correct_step(sub, first_state, roots):
    count = sub.shape[1]
    out = pl.pallas_call(
        correct_kernel,
        in_specs=[VMEM] * 3,
        out_specs=VMEM,
        out_shape=jax.ShapeDtypeStruct((count * 2 * SG // 128, 128), F32),
        compiler_params=LIMIT,
        cost_estimate=pl.CostEstimate(flops=4 * 10**9, bytes_accessed=4 << 20, transcendentals=0),
        name="correct_step",
    )(sub, first_state, roots)
    out = out.reshape(count, SG // 128, 2, 128)
    return jnp.transpose(out, (0, 2, 1, 3)).reshape(1, count, 2, SG)


def image_kernel(gs, first, last, phase_ref, e_ref, *refs):
    backs, refs = refs[: len(gs)], refs[len(gs) :]
    acc_ref = None if first else refs[0]
    out_ref = refs[0 if first else 1]
    if last:
        scratch, sems = refs[-2:]
    width = e_ref.shape[-1]
    height, count = backs[0].shape[1:]
    own = lax.axis_index("fcol")
    left = []
    for back, g in zip(backs, gs):
        freq = (own ^ g) * count + lanes(count)
        pc, ps = unit(freq * (own * width), e_ref.shape[0] * width)
        re, im = back[0], back[1]
        re, im = re * pc - im * ps, im * pc + re * ps
        left.append(halves(jnp.concatenate([jnp.concatenate([re, -im], 1), jnp.concatenate([im, re], 1)])))
    copies = []
    for begin, size in chunks(width):
        columns = slice(begin, begin + size)
        acc = None if first else jnp.concatenate([acc_ref[0, :, columns], acc_ref[1, :, columns]])
        for (high, low), g in zip(left, gs):
            e = e_ref[own ^ g, 0:2, :, columns], e_ref[own ^ g, 2:4, :, columns]
            part = dot3((high, low), [value.reshape(2 * count, size) for value in e], NN)
            acc = part if acc is None else acc + part
        re, im = acc[:height], acc[height:]
        if last:
            pc, ps = phase_ref[0:1, columns], phase_ref[1:2, columns]
            scratch[0, :, columns] = re * pc - im * ps
            scratch[1, :, columns] = im * pc + re * ps
            copies.append(
                pltpu.make_async_copy(scratch.at[:, :, columns], out_ref.at[:, :, columns], sems.at[len(copies)])
            )
            copies[-1].start()
        else:
            out_ref[0, :, columns] = re
            out_ref[1, :, columns] = im
    for copy in copies:
        copy.wait()


def image_step(phase, table, gs, backs, acc, last):
    width = table.shape[-1]
    height = backs[0].shape[1]
    first = acc is None
    operands = list(backs) + ([] if first else [acc])
    return pl.pallas_call(
        functools.partial(image_kernel, tuple(gs), first, last),
        in_specs=[VMEM] * (2 + len(operands)),
        out_specs=pl.BlockSpec(memory_space=pl.ANY) if last else VMEM,
        out_shape=jax.ShapeDtypeStruct((2, height, width), F32),
        scratch_shapes=[pltpu.VMEM((2, height, width), F32), pltpu.SemaphoreType.DMA((len(chunks(width)),))] if last else [],
        compiler_params=LIMIT,
        cost_estimate=pl.CostEstimate(flops=4 * 10**9, bytes_accessed=4 << 20, transcendentals=0),
        name="image_step",
    )(phase, table, *operands)


def swap(value, axis, bit):
    return lax.ppermute(value, axis, [(i, i ^ bit) for i in range(lax.axis_size(axis))])


def per_device(facets, column_start, subgrid_start, vis_count, vis_row, vis_weight):
    rows = lax.axis_size("frow")
    cols = lax.axis_size("fcol")
    height, width = facets.shape[1:]
    rows_total, cols_total = height * rows, width * cols
    count = SG // cols
    assert vis_count.shape[0] == 1 and count <= height

    e_table = jnp.asarray(wave_table(SG, width, cols_total).reshape(4, cols, count, width).transpose(1, 0, 2, 3))
    b_table = wave_table(height, rows_total, rows_total)
    turned = jnp.asarray(b_table.reshape(4 * height, rows_total).T.copy())
    b_table = jnp.asarray(np.concatenate([b_table[:2], b_table]).reshape(6 * height, rows_total))
    angle = np.arange(rows)[:, None] * np.arange(rows_total)[None, :] % rows * (2.0 * np.pi / rows)
    roots = jnp.asarray(np.stack([np.cos(angle), np.sin(angle)], 1).astype(np.float32))

    top = cols // 2
    column_start = column_start.reshape(1, 1)
    waves = waves_of(count, width, cols_total)
    sent, z, phase = strips(column_start, facets, waves, range(top + 1, cols, 2), first=True)
    far = strips(column_start, z, waves, range(top, cols, 2))[0] + swap(sent, "fcol", 1)
    far, z = lax.optimization_barrier((far, z))
    sent, near = strips(column_start, z, waves, range(1, top, 2), range(0, top, 2), cost=4 * 10**9)
    terms = [near + swap(far, "fcol", top), swap(sent, "fcol", 1)]
    bit = 2
    while bit < top:
        pairs = sum(terms).reshape((-1, 2) + far.shape[1:])
        terms = [pairs[:, 0], swap(pairs[:, 1], "fcol", bit)]
        bit *= 2

    own = pack(terms, vis_weight, vis_row, vis_count.reshape(1, 1), count, height)
    order = list(range(0, rows, 2)) + list(range(rows - 1, 0, -2))
    ahead = [(order[i], order[(i + 1) % rows]) for i in range(rows)]
    behind = [(b, a) for a, b in ahead]
    first_state = state = gather_step(subgrid_start, b_table, roots, None, [own], (0,), height)
    up = down = own
    for step in range(1, rows // 2):
        up = lax.ppermute(up, "frow", ahead)
        down = lax.ppermute(down, "frow", behind)
        up, state = lax.optimization_barrier((up, state))
        state = gather_step(subgrid_start, b_table, roots, state, [up, down], (-step, step), height)
    up = lax.ppermute(up, "frow", ahead)
    back, sub = back_step(subgrid_start, b_table, turned, roots, state, up, height)

    near, far = {0: back}, {top: swap(back, "fcol", top)}

    def spread(blocks, bit):
        return {g ^ bit: swap(b, "fcol", bit) for g, b in blocks.items()}

    def image(blocks, acc, last=False):
        return image_step(phase, e_table, blocks.keys(), list(blocks.values()), acc, last)

    acc = image(near, None)
    near[0], acc = lax.optimization_barrier((back, acc))
    bit = top // 2
    while bit >= 1:
        near |= spread(near, bit)
        bit //= 2
    del near[0]
    acc = image(near, acc)
    corrected = correct_step(sub, first_state, roots)
    far[top], acc, corrected = lax.optimization_barrier((far[top], acc, corrected))
    bit = top // 2
    while bit > 1:
        far |= spread(far, bit)
        bit //= 2
    rest = spread(far, 1)
    acc = image(far, acc)
    return corrected, image(rest, acc, last=True)


def solution(mesh):
    return jax.shard_map(
        per_device,
        mesh=mesh,
        in_specs=(
            P(None, "frow", "fcol"),
            P(),
            P(),
            P("frow"),
            P("frow", None),
            P("frow", None, "fcol"),
        ),
        out_specs=(P("frow", "fcol", None, None), P(None, "frow", "fcol")),
        check_vma=False,
    )
```

```python
import functools
import math

import jax
import jax.numpy as jnp
import ml_dtypes
import numpy as np
from jax import lax
from jax.experimental import pallas as pl
from jax.experimental.pallas import tpu as pltpu
from jax.sharding import PartitionSpec as P

SG = 512
MAXB = 64
META = 8

BF = jnp.bfloat16
F32 = jnp.float32
NN = (((1,), (0,)), ((), ()))
NT = (((1,), (1,)), ((), ()))
VMEM = pl.BlockSpec(memory_space=pltpu.VMEM)
SMEM = pl.BlockSpec(memory_space=pltpu.SMEM)
LIMIT = pltpu.CompilerParams(vmem_limit_bytes=32 << 20)


def halves(value):
    high = value.astype(BF)
    return high, (value - high.astype(F32)).astype(BF)


def dot3(left, right, dims):
    def dot(a, b):
        return lax.dot_general(a, b, dims, preferred_element_type=F32)
    return dot(left[0], right[0]) + (dot(left[0], right[1]) + dot(left[1], right[0]))


def unit(phase, modulus, scale=1.0):
    angle = (phase & (modulus - 1)).astype(F32) * F32(2.0 * math.pi / modulus)
    return jnp.cos(angle) * F32(scale), jnp.sin(angle) * F32(scale)


def lanes(count, rows=1):
    return lax.broadcasted_iota(jnp.int32, (rows, count), 1)


def wave_parts(rows, stride, cols, modulus):
    phase = np.arange(rows, dtype=np.int64)[:, None] * (stride * np.arange(cols, dtype=np.int64))[None, :] % modulus
    angle = phase * (2.0 * np.pi / modulus)
    return np.stack([np.cos(angle), np.sin(angle)])


def wave_table(rows, cols, modulus):
    parts = wave_parts(rows, 1, cols, modulus)
    high = parts.astype(ml_dtypes.bfloat16)
    low = (parts - high.astype(np.float64)).astype(ml_dtypes.bfloat16)
    return np.concatenate([high, low])


def ring_place(r, rows):
    return jnp.where(lax.rem(r, 2) == 0, r // 2, rows - 1 - r // 2)


def ring_block(place, rows):
    place = lax.rem(place + rows, rows)
    return jnp.where(place < rows // 2, 2 * place, 2 * (rows - 1 - place) + 1)


def wave_kernel(width, cols_total, base_ref, steps_ref):
    own = lax.axis_index("fcol")
    blocks, _, count, _ = base_ref.shape
    row = lax.broadcasted_iota(jnp.int32, (count, 128), 0)
    for ref, coord in ((base_ref, lanes(128)), (steps_ref, lanes(128) * 128 + own * width)):
        cos, sin = unit(row * coord, cols_total)
        for g in range(blocks):
            pc, ps = unit((own ^ g) * count * coord, cols_total)
            ref[g, 0] = cos * pc - sin * ps
            ref[g, 1] = sin * pc + cos * ps


def waves_of(count, width, cols_total):
    shape = jax.ShapeDtypeStruct((SG // count, 2, count, 128), F32)
    return pl.pallas_call(
        functools.partial(wave_kernel, width, cols_total),
        out_specs=[VMEM] * 2,
        out_shape=[shape] * 2,
        compiler_params=LIMIT,
        cost_estimate=pl.CostEstimate(flops=10**9, bytes_accessed=2 << 20, transcendentals=0),
        name="waves",
    )()


def strip_sums(gs, z_ref, base_ref, steps_ref, out_ref):
    count, height = out_ref.shape[-2:]
    z = z_ref[0], z_ref[1]
    for i, g in enumerate(gs):
        turn_cos, turn_sin, base_cos, base_sin = steps_ref[g, 0], steps_ref[g, 1], base_ref[g, 0], base_ref[g, 1]
        acc = None
        for begin, size in chunks(z_ref.shape[-1]):
            cos, sin = [], []
            for t in range(begin // 128, (begin + size) // 128):
                tc, ts = turn_cos[:, t : t + 1], turn_sin[:, t : t + 1]
                cos.append(tc * base_cos - ts * base_sin)
                sin.append(ts * base_cos + tc * base_sin)
            waves = halves(jnp.concatenate([jnp.concatenate(cos, 1), jnp.concatenate(sin, 1)]))
            part = dot3(waves, [value[:, begin : begin + size] for value in z], NT)
            acc = part if acc is None else acc + part
        cos, sin = acc[:count], acc[count:]
        out_ref[i, 0] = cos[:, :height] + sin[:, height:]
        out_ref[i, 1] = cos[:, height:] - sin[:, :height]


def first_strip_kernel(gs, cols_total, start_ref, x_ref, base_ref, steps_ref, out_ref, z_ref, phase_ref):
    own = lax.axis_index("fcol")
    width = x_ref.shape[-1]
    pc, ps = unit(start_ref[0:1, 0:1] * (own * width + lanes(width)), cols_total, 1.0 / math.sqrt(cols_total))
    re, im = x_ref[0], x_ref[1]
    z_ref[0], z_ref[1] = halves(jnp.concatenate([re * pc + im * ps, im * pc - re * ps]))
    phase_ref[0:1], phase_ref[1:2] = pc, ps
    strip_sums(gs, z_ref, base_ref, steps_ref, out_ref)


def first_strips(column_start, facets, waves, gs):
    cols, _, count, _ = waves[0].shape
    _, height, width = facets.shape
    return pl.pallas_call(
        functools.partial(first_strip_kernel, tuple(gs), cols * width),
        in_specs=[VMEM] * 4,
        out_specs=[VMEM] * 3,
        out_shape=[
            jax.ShapeDtypeStruct((len(gs), 2, count, height), F32),
            jax.ShapeDtypeStruct((2, 2 * height, width), BF),
            jax.ShapeDtypeStruct((2, width), F32),
        ],
        compiler_params=LIMIT,
        cost_estimate=pl.CostEstimate(flops=10**9, bytes_accessed=2 << 20, transcendentals=0),
        name="first_strips",
    )(column_start, facets, *waves)


def far_strip_kernel(gs, z_ref, base_ref, steps_ref, out_ref):
    strip_sums(gs, z_ref, base_ref, steps_ref, out_ref)


def far_strips(z, waves, gs):
    return pl.pallas_call(
        functools.partial(far_strip_kernel, tuple(gs)),
        in_specs=[VMEM] * 3,
        out_specs=VMEM,
        out_shape=jax.ShapeDtypeStruct((len(gs), 2, waves[0].shape[2], z.shape[1] // 2), F32),
        compiler_params=LIMIT,
        cost_estimate=pl.CostEstimate(flops=10**9, bytes_accessed=2 << 20, transcendentals=0),
        name="far_strips",
    )(z, *waves)


def near_strip_kernel(groups, starts_ref, z_ref, base_ref, steps_ref, *refs):
    out_refs, (turn_ref, away_ref, starts, sem) = refs[: len(groups)], refs[len(groups) :]
    copy = pltpu.make_async_copy(starts_ref, starts, sem)
    copy.start()
    for gs, out_ref in zip(groups, out_refs):
        strip_sums(gs, z_ref, base_ref, steps_ref, out_ref)
    copy.wait()
    rows, _, height = turn_ref.shape
    rows_total = rows * height
    mine = starts[lax.axis_index("frow")]
    for r in range(rows):
        turn_ref[r, 0:1], turn_ref[r, 1:2] = unit(mine * (r * height + lanes(height)), rows_total, 1.0 / math.sqrt(rows_total))
        away_ref[r] = jnp.full((1, 128), mine - starts[r], jnp.int32)


def near_strips(starts, z, waves, groups):
    rows, count, height = starts.shape[0], waves[0].shape[2], z.shape[1] // 2
    return pl.pallas_call(
        functools.partial(near_strip_kernel, groups),
        in_specs=[pl.BlockSpec(memory_space=pl.ANY)] + [VMEM] * 3,
        out_specs=[VMEM] * (len(groups) + 2),
        out_shape=[jax.ShapeDtypeStruct((len(gs), 2, count, height), F32) for gs in groups]
        + [jax.ShapeDtypeStruct((rows, 2, height), F32), jax.ShapeDtypeStruct((rows, 1, 128), jnp.int32)],
        scratch_shapes=[pltpu.SMEM((rows,), jnp.int32), pltpu.SemaphoreType.DMA],
        compiler_params=LIMIT,
        cost_estimate=pl.CostEstimate(flops=4 * 10**9, bytes_accessed=2 << 20, transcendentals=0),
        name="near_strips",
    )(starts, z, *waves)


def pack_kernel(terms, *refs):
    weight_ref, row_ref, live_ref, out_ref = refs[terms:]
    count = refs[0].shape[2]
    strip = sum(ref[0] for ref in refs[:terms])
    out_ref[:count], out_ref[count : 2 * count] = strip[0], strip[1]
    width = out_ref.shape[1]
    weight = weight_ref[0]
    if count < width:
        weight = jnp.concatenate([weight, jnp.zeros((MAXB, width - count), F32)], 1)
    out_ref[2 * count : 2 * count + MAXB] = weight
    row = jnp.where(lanes(MAXB) < live_ref[0:1, 0:1], row_ref[...], -1).astype(F32)
    row = jnp.concatenate([row, jnp.zeros((1, width - MAXB), F32)], 1)
    out_ref[2 * count + MAXB :] = jnp.broadcast_to(row, (META, width))


def pack(terms, weight, row, live, count, height):
    return pl.pallas_call(
        functools.partial(pack_kernel, len(terms)),
        in_specs=[VMEM] * (len(terms) + 3),
        out_specs=VMEM,
        out_shape=jax.ShapeDtypeStruct((2 * count + MAXB + META, height), F32),
        compiler_params=LIMIT,
        name="pack",
    )(*terms, weight, row, live)


class Message:
    def __init__(self, r, message, refs, height, count, rows_total):
        b_ref, roots_ref, turn_ref, away_ref = refs
        own = lax.axis_index("frow")
        strip, rest = message[: 2 * count], message[2 * count :]
        pc, ps = turn_ref[r, 0:1], turn_ref[r, 1:2]
        re, im = strip[:count], strip[count:]
        re, im = re * pc + im * ps, im * pc - re * ps
        high, low = halves(jnp.concatenate([jnp.concatenate([re, im], 1), jnp.concatenate([im, -re], 1)]))
        self.left = jnp.concatenate([high, low, high], 1)

        width = message.shape[1]
        flat = jnp.concatenate([rest, jnp.zeros((width - rest.shape[0], width), F32)])
        turned = jnp.transpose(flat)
        self.weight = jnp.concatenate(halves(turned[:count, :MAXB]), 1)
        row = turned[:MAXB, MAXB : MAXB + 1].astype(jnp.int32)
        self.away = away_ref[r][0:1, 0:1]
        self.place = jnp.where(row < 0, -1, (row - self.away) & (rows_total - 1))
        self.turn = lax.rem(r - own + rows_total // height, rows_total // height)
        self.refs, self.count, self.rows_total = (b_ref, roots_ref), count, rows_total

    def chunk(self, begin, size):
        b_ref, roots_ref = self.refs
        part = lax.dot_general(self.left, b_ref[:, begin : begin + size], NN, preferred_element_type=F32)
        pc, ps = roots_ref[self.turn, 0:1, begin : begin + size], roots_ref[self.turn, 1:2, begin : begin + size]
        re, im = part[: self.count], part[self.count :]
        freq = begin + lanes(size)
        hot = (begin + lanes(size, MAXB) == self.place).astype(F32).astype(BF)
        gain = lax.dot_general(self.weight, jnp.concatenate([hot, hot]), NN, preferred_element_type=F32)
        seen = (((freq + self.away) & (self.rows_total - 1)) < SG).astype(F32)
        return re * pc + im * ps, im * pc - re * ps, gain + seen


def chunks(total, size=256):
    return [(begin, min(size, total - begin)) for begin in range(0, total, size)]


def gather_kernel(steps, rows, height, count, *refs):
    tables, refs = refs[:4], refs[4:]
    state_ref = None
    if len(refs) > len(steps) + 1:
        state_ref, refs = refs[0], refs[1:]
    at = ring_place(lax.axis_index("frow"), rows)
    found = [
        Message(ring_block(at + step, rows), message[...], tables, height, count, rows * height)
        for step, message in zip(steps, refs)
    ]
    for begin, size in chunks(rows * height):
        terms = [message.chunk(begin, size) for message in found]
        for i in range(3):
            value = sum(term[i] for term in terms)
            if state_ref is not None:
                value = value + state_ref[i, :, begin : begin + size]
            refs[-1][i, :, begin : begin + size] = value


def gather_step(tables, state, messages, steps, height):
    rows_total = tables[0].shape[1]
    count = (messages[0].shape[0] - MAXB - META) // 2
    operands = [*tables] + ([] if state is None else [state]) + list(messages)
    return pl.pallas_call(
        functools.partial(gather_kernel, steps, rows_total // height, height, count),
        in_specs=[VMEM] * len(operands),
        out_specs=VMEM,
        out_shape=jax.ShapeDtypeStruct((3, count, rows_total), F32),
        compiler_params=LIMIT,
        cost_estimate=pl.CostEstimate(flops=10**9, bytes_accessed=4 << 20, transcendentals=0),
        name="gather_step",
    )(*operands)


def back_kernel(rows, height, count, *refs):
    tables, (turned_ref, state_ref, message_ref, back_ref, sub_ref) = refs[:4], refs[4:]
    rows_total = rows * height
    own = lax.axis_index("frow")
    r = ring_block(ring_place(own, rows) + rows // 2, rows)
    message = Message(r, message_ref[...], tables, height, count, rows_total)
    acc = None
    for begin, size in chunks(rows_total):
        terms = message.chunk(begin, size)
        re, im, gain = [term + state_ref[i, :, begin : begin + size] for i, term in enumerate(terms)]
        if begin < SG:
            sub_ref[0, :, begin : begin + size] = re
            sub_ref[1, :, begin : begin + size] = im
        high, low = halves(jnp.concatenate([re * gain, im * gain]))
        table = turned_ref[begin : begin + size]
        part = lax.dot_general(high, table, NN, preferred_element_type=F32)
        part = part[:, : 2 * height] + (
            part[:, 2 * height :] + lax.dot_general(low, table[:, : 2 * height], NN, preferred_element_type=F32)
        )
        acc = part if acc is None else acc + part
    re = acc[:count, :height] - acc[count:, height:]
    im = acc[count:, :height] + acc[:count, height:]
    pc, ps = tables[2][own, 0:1], tables[2][own, 1:2]
    back_ref[0] = jnp.transpose(re * pc - im * ps)
    back_ref[1] = jnp.transpose(im * pc + re * ps)


def back_step(tables, turned, state, message, height):
    count, rows_total = state.shape[1:]
    return pl.pallas_call(
        functools.partial(back_kernel, rows_total // height, height, count),
        in_specs=[VMEM] * 7,
        out_specs=[VMEM] * 2,
        out_shape=[
            jax.ShapeDtypeStruct((2, height, count), F32),
            jax.ShapeDtypeStruct((2, count, SG), F32),
        ],
        compiler_params=LIMIT,
        name="back_step",
    )(*tables, turned, state, message)


def correct_kernel(sub_ref, gain_ref, roots_ref, out_ref):
    count = sub_ref.shape[1]
    pieces = SG // 128
    own = lax.axis_index("frow")
    pc, ps = roots_ref[own, 0:1, :SG], roots_ref[own, 1:2, :SG]
    re, im, gain = sub_ref[0], sub_ref[1], gain_ref[2, :, :SG]
    for part, value in enumerate([(re * pc + im * ps) * gain, (im * pc - re * ps) * gain]):
        for i in range(pieces):
            out_ref[pl.ds(2 * i + part, count, stride=2 * pieces), :] = value[:, 128 * i : 128 * (i + 1)]


def correct_step(sub, first_state, roots):
    count = sub.shape[1]
    out = pl.pallas_call(
        correct_kernel,
        in_specs=[VMEM] * 3,
        out_specs=VMEM,
        out_shape=jax.ShapeDtypeStruct((count * 2 * SG // 128, 128), F32),
        compiler_params=LIMIT,
        cost_estimate=pl.CostEstimate(flops=4 * 10**9, bytes_accessed=4 << 20, transcendentals=0),
        name="correct_step",
    )(sub, first_state, roots)
    out = out.reshape(count, SG // 128, 2, 128)
    return jnp.transpose(out, (0, 2, 1, 3)).reshape(1, count, 2, SG)


def image_kernel(gs, first, last, phase_ref, e_ref, *refs):
    backs, refs = refs[: len(gs)], refs[len(gs) :]
    acc_ref = None if first else refs[0]
    out_ref = refs[0 if first else 1]
    if last:
        scratch, sems = refs[-2:]
    width = e_ref.shape[-1]
    height, count = backs[0].shape[1:]
    own = lax.axis_index("fcol")
    left = []
    for back, g in zip(backs, gs):
        freq = (own ^ g) * count + lanes(count)
        pc, ps = unit(freq * (own * width), e_ref.shape[0] * width)
        re, im = back[0], back[1]
        re, im = re * pc - im * ps, im * pc + re * ps
        left.append(halves(jnp.concatenate([jnp.concatenate([re, -im], 1), jnp.concatenate([im, re], 1)])))
    copies = []
    for begin, size in chunks(width):
        columns = slice(begin, begin + size)
        acc = None if first else jnp.concatenate([acc_ref[0, :, columns], acc_ref[1, :, columns]])
        for (high, low), g in zip(left, gs):
            e = e_ref[own ^ g, 0:2, :, columns], e_ref[own ^ g, 2:4, :, columns]
            part = dot3((high, low), [value.reshape(2 * count, size) for value in e], NN)
            acc = part if acc is None else acc + part
        re, im = acc[:height], acc[height:]
        if last:
            pc, ps = phase_ref[0:1, columns], phase_ref[1:2, columns]
            scratch[0, :, columns] = re * pc - im * ps
            scratch[1, :, columns] = im * pc + re * ps
            copies.append(
                pltpu.make_async_copy(scratch.at[:, :, columns], out_ref.at[:, :, columns], sems.at[len(copies)])
            )
            copies[-1].start()
        else:
            out_ref[0, :, columns] = re
            out_ref[1, :, columns] = im
    for copy in copies:
        copy.wait()


def image_step(phase, table, gs, backs, acc, last):
    width = table.shape[-1]
    height = backs[0].shape[1]
    first = acc is None
    operands = list(backs) + ([] if first else [acc])
    return pl.pallas_call(
        functools.partial(image_kernel, tuple(gs), first, last),
        in_specs=[VMEM] * (2 + len(operands)),
        out_specs=pl.BlockSpec(memory_space=pl.ANY) if last else VMEM,
        out_shape=jax.ShapeDtypeStruct((2, height, width), F32),
        scratch_shapes=[pltpu.VMEM((2, height, width), F32), pltpu.SemaphoreType.DMA((len(chunks(width)),))] if last else [],
        compiler_params=LIMIT,
        cost_estimate=pl.CostEstimate(flops=4 * 10**9, bytes_accessed=4 << 20, transcendentals=0),
        name="image_step",
    )(phase, table, *operands)


def swap(value, axis, bit):
    return lax.ppermute(value, axis, [(i, i ^ bit) for i in range(lax.axis_size(axis))])


def per_device(facets, column_start, subgrid_start, vis_count, vis_row, vis_weight):
    rows = lax.axis_size("frow")
    cols = lax.axis_size("fcol")
    height, width = facets.shape[1:]
    rows_total, cols_total = height * rows, width * cols
    count = SG // cols
    assert vis_count.shape[0] == 1 and count <= height

    e_table = jnp.asarray(wave_table(SG, width, cols_total).reshape(4, cols, count, width).transpose(1, 0, 2, 3))
    b_table = wave_table(height, rows_total, rows_total)
    turned = jnp.asarray(b_table.reshape(4 * height, rows_total).T.copy())
    b_table = jnp.asarray(np.concatenate([b_table[:2], b_table]).reshape(6 * height, rows_total))
    angle = np.arange(rows)[:, None] * np.arange(rows_total)[None, :] % rows * (2.0 * np.pi / rows)
    roots = jnp.asarray(np.stack([np.cos(angle), np.sin(angle)], 1).astype(np.float32))

    top = cols // 2
    column_start = column_start.reshape(1, 1)
    waves = waves_of(count, width, cols_total)
    sent, z, phase = first_strips(column_start, facets, waves, range(top + 1, cols, 2))
    far = far_strips(z, waves, range(top, cols, 2)) + swap(sent, "fcol", 1)
    far, z = lax.optimization_barrier((far, z))
    sent, near, *turns = near_strips(subgrid_start, z, waves, [tuple(range(1, top, 2)), tuple(range(0, top, 2))])
    terms = [near + swap(far, "fcol", top), swap(sent, "fcol", 1)]
    bit = 2
    while bit < top:
        pairs = sum(terms).reshape((-1, 2) + far.shape[1:])
        terms = [pairs[:, 0], swap(pairs[:, 1], "fcol", bit)]
        bit *= 2

    own = pack(terms, vis_weight, vis_row, vis_count.reshape(1, 1), count, height)
    tables = b_table, roots, *turns
    order = list(range(0, rows, 2)) + list(range(rows - 1, 0, -2))
    ahead = [(order[i], order[(i + 1) % rows]) for i in range(rows)]
    behind = [(b, a) for a, b in ahead]
    first_state = state = gather_step(tables, None, [own], (0,), height)
    up = down = own
    for step in range(1, rows // 2):
        up = lax.ppermute(up, "frow", ahead)
        down = lax.ppermute(down, "frow", behind)
        up, state = lax.optimization_barrier((up, state))
        state = gather_step(tables, state, [up, down], (-step, step), height)
    up = lax.ppermute(up, "frow", ahead)
    back, sub = back_step(tables, turned, state, up, height)

    near, far = {0: back}, {top: swap(back, "fcol", top)}

    def spread(blocks, bit):
        return {g ^ bit: swap(b, "fcol", bit) for g, b in blocks.items()}

    def image(blocks, acc, last=False):
        return image_step(phase, e_table, blocks.keys(), list(blocks.values()), acc, last)

    acc = image(near, None)
    near[0], acc = lax.optimization_barrier((back, acc))
    bit = top // 2
    while bit >= 1:
        near |= spread(near, bit)
        bit //= 2
    del near[0]
    acc = image(near, acc)
    corrected = correct_step(sub, first_state, roots)
    far[top], acc, corrected = lax.optimization_barrier((far[top], acc, corrected))
    bit = top // 2
    while bit > 1:
        far |= spread(far, bit)
        bit //= 2
    rest = spread(far, 1)
    acc = image(far, acc)
    return corrected, image(rest, acc, last=True)


def solution(mesh):
    return jax.shard_map(
        per_device,
        mesh=mesh,
        in_specs=(
            P(None, "frow", "fcol"),
            P(),
            P(),
            P("frow"),
            P("frow", None),
            P("frow", None, "fcol"),
        ),
        out_specs=(P("frow", "fcol", None, None), P(None, "frow", "fcol")),
        check_vma=False,
    )
```

```python
import functools
import math

import jax
import jax.numpy as jnp
import ml_dtypes
import numpy as np
from jax import lax
from jax.experimental import pallas as pl
from jax.experimental.pallas import tpu as pltpu
from jax.sharding import PartitionSpec as P

SG = 512
MAXB = 64
META = 8

BF = jnp.bfloat16
F32 = jnp.float32
NN = (((1,), (0,)), ((), ()))
NT = (((1,), (1,)), ((), ()))
VMEM = pl.BlockSpec(memory_space=pltpu.VMEM)
SMEM = pl.BlockSpec(memory_space=pltpu.SMEM)
LIMIT = pltpu.CompilerParams(vmem_limit_bytes=32 << 20)


def halves(value):
    high = value.astype(BF)
    return high, (value - high.astype(F32)).astype(BF)


def dot3(left, right, dims):
    def dot(a, b):
        return lax.dot_general(a, b, dims, preferred_element_type=F32)
    return dot(left[0], right[0]) + (dot(left[0], right[1]) + dot(left[1], right[0]))


def unit(phase, modulus, scale=1.0):
    angle = (phase & (modulus - 1)).astype(F32) * F32(2.0 * math.pi / modulus)
    return jnp.cos(angle) * F32(scale), jnp.sin(angle) * F32(scale)


def lanes(count, rows=1):
    return lax.broadcasted_iota(jnp.int32, (rows, count), 1)


def wave_parts(rows, stride, cols, modulus):
    phase = np.arange(rows, dtype=np.int64)[:, None] * (stride * np.arange(cols, dtype=np.int64))[None, :] % modulus
    angle = phase * (2.0 * np.pi / modulus)
    return np.stack([np.cos(angle), np.sin(angle)])


def wave_table(rows, cols, modulus):
    parts = wave_parts(rows, 1, cols, modulus)
    high = parts.astype(ml_dtypes.bfloat16)
    low = (parts - high.astype(np.float64)).astype(ml_dtypes.bfloat16)
    return np.concatenate([high, low])


def ring_place(r, rows):
    return jnp.where(lax.rem(r, 2) == 0, r // 2, rows - 1 - r // 2)


def ring_block(place, rows):
    place = lax.rem(place + rows, rows)
    return jnp.where(place < rows // 2, 2 * place, 2 * (rows - 1 - place) + 1)


def wave_kernel(width, cols_total, base_ref, steps_ref):
    own = lax.axis_index("fcol")
    blocks, _, count, _ = base_ref.shape
    row = lax.broadcasted_iota(jnp.int32, (count, 128), 0)
    for ref, coord in ((base_ref, lanes(128)), (steps_ref, lanes(128) * 128 + own * width)):
        cos, sin = unit(row * coord, cols_total)
        for g in range(blocks):
            pc, ps = unit((own ^ g) * count * coord, cols_total)
            ref[g, 0] = cos * pc - sin * ps
            ref[g, 1] = sin * pc + cos * ps


def waves_of(count, width, cols_total):
    shape = jax.ShapeDtypeStruct((SG // count, 2, count, 128), F32)
    return pl.pallas_call(
        functools.partial(wave_kernel, width, cols_total),
        out_specs=[VMEM] * 2,
        out_shape=[shape] * 2,
        compiler_params=LIMIT,
        cost_estimate=pl.CostEstimate(flops=10**9, bytes_accessed=2 << 20, transcendentals=0),
        name="waves",
    )()


def waves_in(base, turn, begin, size):
    cos, sin = [], []
    for t in range(begin // 128, (begin + size) // 128):
        tc, ts = turn[0][:, t : t + 1], turn[1][:, t : t + 1]
        cos.append(tc * base[0] - ts * base[1])
        sin.append(ts * base[0] + tc * base[1])
    return halves(jnp.concatenate([jnp.concatenate(cos, 1), jnp.concatenate(sin, 1)]))


def strip_sums(gs, z_ref, base_ref, steps_ref, out_ref):
    count, height = out_ref.shape[-2:]
    z = z_ref[0], z_ref[1]
    for i, g in enumerate(gs):
        base, turn = (base_ref[g, 0], base_ref[g, 1]), (steps_ref[g, 0], steps_ref[g, 1])
        acc = None
        for begin, size in chunks(z_ref.shape[-1]):
            waves = waves_in(base, turn, begin, size)
            part = dot3(waves, [value[:, begin : begin + size] for value in z], NT)
            acc = part if acc is None else acc + part
        cos, sin = acc[:count], acc[count:]
        out_ref[i, 0] = cos[:, :height] + sin[:, height:]
        out_ref[i, 1] = cos[:, height:] - sin[:, :height]


def first_strip_kernel(gs, cols_total, start_ref, x_ref, base_ref, steps_ref, out_ref, z_ref, tilt_ref):
    own = lax.axis_index("fcol")
    width = x_ref.shape[-1]
    start, scale = start_ref[0:1, 0:1], 1.0 / math.sqrt(cols_total)
    pc, ps = unit(start * (own * width + lanes(width)), cols_total, scale)
    re, im = x_ref[0], x_ref[1]
    z_ref[0], z_ref[1] = halves(jnp.concatenate([re * pc + im * ps, im * pc - re * ps]))
    tilt_ref[0:1], tilt_ref[1:2] = unit(start * lanes(128), cols_total)
    tilt_ref[2:3], tilt_ref[3:4] = unit(start * (own * width + 128 * lanes(128)), cols_total, scale)
    strip_sums(gs, z_ref, base_ref, steps_ref, out_ref)


def first_strips(column_start, facets, waves, gs):
    cols, _, count, _ = waves[0].shape
    _, height, width = facets.shape
    return pl.pallas_call(
        functools.partial(first_strip_kernel, tuple(gs), cols * width),
        in_specs=[VMEM] * 4,
        out_specs=[VMEM] * 3,
        out_shape=[
            jax.ShapeDtypeStruct((len(gs), 2, count, height), F32),
            jax.ShapeDtypeStruct((2, 2 * height, width), BF),
            jax.ShapeDtypeStruct((4, 128), F32),
        ],
        compiler_params=LIMIT,
        cost_estimate=pl.CostEstimate(flops=10**9, bytes_accessed=2 << 20, transcendentals=0),
        name="first_strips",
    )(column_start, facets, *waves)


def far_strip_kernel(gs, z_ref, base_ref, steps_ref, out_ref):
    strip_sums(gs, z_ref, base_ref, steps_ref, out_ref)


def far_strips(z, waves, gs):
    return pl.pallas_call(
        functools.partial(far_strip_kernel, tuple(gs)),
        in_specs=[VMEM] * 3,
        out_specs=VMEM,
        out_shape=jax.ShapeDtypeStruct((len(gs), 2, waves[0].shape[2], z.shape[1] // 2), F32),
        compiler_params=LIMIT,
        cost_estimate=pl.CostEstimate(flops=10**9, bytes_accessed=2 << 20, transcendentals=0),
        name="far_strips",
    )(z, *waves)


def near_strip_kernel(groups, starts_ref, z_ref, base_ref, steps_ref, *refs):
    out_refs, (turn_ref, away_ref, starts, sem) = refs[: len(groups)], refs[len(groups) :]
    copy = pltpu.make_async_copy(starts_ref, starts, sem)
    copy.start()
    for gs, out_ref in zip(groups, out_refs):
        strip_sums(gs, z_ref, base_ref, steps_ref, out_ref)
    copy.wait()
    rows, _, height = turn_ref.shape
    rows_total = rows * height
    mine = starts[lax.axis_index("frow")]
    for r in range(rows):
        turn_ref[r, 0:1], turn_ref[r, 1:2] = unit(mine * (r * height + lanes(height)), rows_total, 1.0 / math.sqrt(rows_total))
        away_ref[r] = jnp.full((1, 128), mine - starts[r], jnp.int32)


def near_strips(starts, z, waves, groups):
    rows, count, height = starts.shape[0], waves[0].shape[2], z.shape[1] // 2
    return pl.pallas_call(
        functools.partial(near_strip_kernel, groups),
        in_specs=[pl.BlockSpec(memory_space=pl.ANY)] + [VMEM] * 3,
        out_specs=[VMEM] * (len(groups) + 2),
        out_shape=[jax.ShapeDtypeStruct((len(gs), 2, count, height), F32) for gs in groups]
        + [jax.ShapeDtypeStruct((rows, 2, height), F32), jax.ShapeDtypeStruct((rows, 1, 128), jnp.int32)],
        scratch_shapes=[pltpu.SMEM((rows,), jnp.int32), pltpu.SemaphoreType.DMA],
        compiler_params=LIMIT,
        cost_estimate=pl.CostEstimate(flops=4 * 10**9, bytes_accessed=2 << 20, transcendentals=0),
        name="near_strips",
    )(starts, z, *waves)


def pack_kernel(terms, *refs):
    weight_ref, row_ref, live_ref, out_ref = refs[terms:]
    count = refs[0].shape[2]
    strip = sum(ref[0] for ref in refs[:terms])
    out_ref[:count], out_ref[count : 2 * count] = strip[0], strip[1]
    width = out_ref.shape[1]
    weight = weight_ref[0]
    if count < width:
        weight = jnp.concatenate([weight, jnp.zeros((MAXB, width - count), F32)], 1)
    out_ref[2 * count : 2 * count + MAXB] = weight
    row = jnp.where(lanes(MAXB) < live_ref[0:1, 0:1], row_ref[...], -1).astype(F32)
    row = jnp.concatenate([row, jnp.zeros((1, width - MAXB), F32)], 1)
    out_ref[2 * count + MAXB :] = jnp.broadcast_to(row, (META, width))


def pack(terms, weight, row, live, count, height):
    return pl.pallas_call(
        functools.partial(pack_kernel, len(terms)),
        in_specs=[VMEM] * (len(terms) + 3),
        out_specs=VMEM,
        out_shape=jax.ShapeDtypeStruct((2 * count + MAXB + META, height), F32),
        compiler_params=LIMIT,
        name="pack",
    )(*terms, weight, row, live)


class Message:
    def __init__(self, r, message, refs, height, count, rows_total):
        b_ref, roots_ref, turn_ref, away_ref = refs
        own = lax.axis_index("frow")
        strip, rest = message[: 2 * count], message[2 * count :]
        pc, ps = turn_ref[r, 0:1], turn_ref[r, 1:2]
        re, im = strip[:count], strip[count:]
        re, im = re * pc + im * ps, im * pc - re * ps
        high, low = halves(jnp.concatenate([jnp.concatenate([re, im], 1), jnp.concatenate([im, -re], 1)]))
        self.left = jnp.concatenate([high, low, high], 1)

        width = message.shape[1]
        flat = jnp.concatenate([rest, jnp.zeros((width - rest.shape[0], width), F32)])
        turned = jnp.transpose(flat)
        self.weight = jnp.concatenate(halves(turned[:count, :MAXB]), 1)
        row = turned[:MAXB, MAXB : MAXB + 1].astype(jnp.int32)
        self.away = away_ref[r][0:1, 0:1]
        self.place = jnp.where(row < 0, -1, (row - self.away) & (rows_total - 1))
        self.turn = lax.rem(r - own + rows_total // height, rows_total // height)
        self.refs, self.count, self.rows_total = (b_ref, roots_ref), count, rows_total

    def chunk(self, begin, size):
        b_ref, roots_ref = self.refs
        part = lax.dot_general(self.left, b_ref[:, begin : begin + size], NN, preferred_element_type=F32)
        pc, ps = roots_ref[self.turn, 0:1, begin : begin + size], roots_ref[self.turn, 1:2, begin : begin + size]
        re, im = part[: self.count], part[self.count :]
        freq = begin + lanes(size)
        hot = (begin + lanes(size, MAXB) == self.place).astype(F32).astype(BF)
        gain = lax.dot_general(self.weight, jnp.concatenate([hot, hot]), NN, preferred_element_type=F32)
        seen = (((freq + self.away) & (self.rows_total - 1)) < SG).astype(F32)
        return re * pc + im * ps, im * pc - re * ps, gain + seen


def chunks(total, size=256):
    return [(begin, min(size, total - begin)) for begin in range(0, total, size)]


def image_waves(base_ref, steps_ref, tilt_ref, out_ref):
    def tilted(cos, sin, row):
        pc, ps = tilt_ref[row : row + 1], tilt_ref[row + 1 : row + 2]
        return cos * pc - sin * ps, sin * pc + cos * ps

    for g in range(out_ref.shape[0]):
        base, turn = tilted(base_ref[g, 0], base_ref[g, 1], 0), tilted(steps_ref[g, 0], steps_ref[g, 1], 2)
        for begin, size in chunks(out_ref.shape[-1]):
            columns = slice(begin, begin + size)
            out_ref[g, 0, :, columns], out_ref[g, 1, :, columns] = waves_in(base, turn, begin, size)


def gather_kernel(kind, steps, rows, height, count, *refs):
    tables, refs = refs[:4], refs[4:]
    odd = lax.rem(lax.axis_index("fcol"), 2) == 1
    at = ring_place(lax.axis_index("frow"), rows)

    def add(state_ref, arrived, out_ref):
        found = [
            Message(ring_block(at + step, rows), message[...], tables, height, count, rows * height)
            for step, message in arrived
        ]
        for begin, size in chunks(rows * height):
            terms = [message.chunk(begin, size) for message in found]
            for i in range(3):
                value = sum(term[i] for term in terms)
                if state_ref is not None:
                    value = value + state_ref[i, :, begin : begin + size]
                out_ref[i, :, begin : begin + size] = value

    if kind == "first":
        add(None, zip(steps, refs), refs[-1])
    elif kind == "plain":
        add(refs[0], zip(steps, refs[1:]), refs[-1])
    elif kind == "skip":

        @pl.when(jnp.logical_not(odd))
        def _():
            add(refs[0], zip(steps, refs[1:]), refs[-1])

    elif kind == "late":
        state_ref, before_ref, early, now, waves, (out_ref, made_ref) = (
            refs[0], refs[1], refs[2:4], refs[4:6], refs[6:9], refs[9:]
        )

        @pl.when(jnp.logical_not(odd))
        def _():
            add(state_ref, zip(steps[2:], now), out_ref)

        @pl.when(odd)
        def _():
            add(before_ref, zip(steps, [*early, *now]), out_ref)
            image_waves(*waves, made_ref)

    else:
        state_ref, now, waves, made_ref, (out_ref, waves_ref) = refs[0], refs[1:3], refs[3:6], refs[6], refs[7:]
        add(state_ref, zip(steps, now), out_ref)

        @pl.when(odd)
        def _():
            waves_ref[...] = made_ref[...]

        @pl.when(jnp.logical_not(odd))
        def _():
            image_waves(*waves, waves_ref)


def gather_step(kind, tables, operands, steps, count, made=None):
    height, rows_total = tables[2].shape[2], tables[0].shape[1]
    shapes = [jax.ShapeDtypeStruct((3, count, rows_total), F32)] + ([made] if made else [])
    out = pl.pallas_call(
        functools.partial(gather_kernel, kind, steps, rows_total // height, height, count),
        in_specs=[VMEM] * (len(tables) + len(operands)),
        out_specs=[VMEM] * len(shapes),
        out_shape=shapes,
        compiler_params=LIMIT,
        cost_estimate=pl.CostEstimate(flops=10**9, bytes_accessed=4 << 20, transcendentals=0),
        name="gather_step",
    )(*tables, *operands)
    return out if made else out[0]


def back_kernel(rows, height, count, *refs):
    tables, (turned_ref, state_ref, message_ref, back_ref, sub_ref) = refs[:4], refs[4:]
    rows_total = rows * height
    own = lax.axis_index("frow")
    r = ring_block(ring_place(own, rows) + rows // 2, rows)
    message = Message(r, message_ref[...], tables, height, count, rows_total)
    acc = None
    for begin, size in chunks(rows_total):
        terms = message.chunk(begin, size)
        re, im, gain = [term + state_ref[i, :, begin : begin + size] for i, term in enumerate(terms)]
        if begin < SG:
            sub_ref[0, :, begin : begin + size] = re
            sub_ref[1, :, begin : begin + size] = im
        high, low = halves(jnp.concatenate([re * gain, im * gain]))
        table = turned_ref[begin : begin + size]
        part = lax.dot_general(high, table, NN, preferred_element_type=F32)
        part = part[:, : 2 * height] + (
            part[:, 2 * height :] + lax.dot_general(low, table[:, : 2 * height], NN, preferred_element_type=F32)
        )
        acc = part if acc is None else acc + part
    re = acc[:count, :height] - acc[count:, height:]
    im = acc[count:, :height] + acc[:count, height:]
    pc, ps = tables[2][own, 0:1], tables[2][own, 1:2]
    back_ref[0] = jnp.transpose(re * pc - im * ps)
    back_ref[1] = jnp.transpose(im * pc + re * ps)


def back_step(tables, turned, state, message, height):
    count, rows_total = state.shape[1:]
    return pl.pallas_call(
        functools.partial(back_kernel, rows_total // height, height, count),
        in_specs=[VMEM] * 7,
        out_specs=[VMEM] * 2,
        out_shape=[
            jax.ShapeDtypeStruct((2, height, count), F32),
            jax.ShapeDtypeStruct((2, count, SG), F32),
        ],
        compiler_params=LIMIT,
        name="back_step",
    )(*tables, turned, state, message)


def correct_kernel(sub_ref, gain_ref, roots_ref, out_ref):
    count = sub_ref.shape[1]
    pieces = SG // 128
    own = lax.axis_index("frow")
    pc, ps = roots_ref[own, 0:1, :SG], roots_ref[own, 1:2, :SG]
    re, im, gain = sub_ref[0], sub_ref[1], gain_ref[2, :, :SG]
    for part, value in enumerate([(re * pc + im * ps) * gain, (im * pc - re * ps) * gain]):
        for i in range(pieces):
            out_ref[pl.ds(2 * i + part, count, stride=2 * pieces), :] = value[:, 128 * i : 128 * (i + 1)]


def correct_step(sub, first_state, roots):
    count = sub.shape[1]
    out = pl.pallas_call(
        correct_kernel,
        in_specs=[VMEM] * 3,
        out_specs=VMEM,
        out_shape=jax.ShapeDtypeStruct((count * 2 * SG // 128, 128), F32),
        compiler_params=LIMIT,
        cost_estimate=pl.CostEstimate(flops=4 * 10**9, bytes_accessed=4 << 20, transcendentals=0),
        name="correct_step",
    )(sub, first_state, roots)
    out = out.reshape(count, SG // 128, 2, 128)
    return jnp.transpose(out, (0, 2, 1, 3)).reshape(1, count, 2, SG)


def image_kernel(gs, first, last, e_ref, *refs):
    backs, refs = refs[: len(gs)], refs[len(gs) :]
    acc_ref = None if first else refs[0]
    out_ref = refs[0 if first else 1]
    if last:
        scratch, sems = refs[-2:]
    width = e_ref.shape[-1]
    height = backs[0].shape[1]
    left = []
    for back in backs:
        re, im = back[0], back[1]
        left.append(halves(jnp.concatenate([jnp.concatenate([re, -im], 1), jnp.concatenate([im, re], 1)])))
    copies = []
    for begin, size in chunks(width):
        columns = slice(begin, begin + size)
        acc = None if first else jnp.concatenate([acc_ref[0, :, columns], acc_ref[1, :, columns]])
        for (high, low), g in zip(left, gs):
            part = dot3((high, low), (e_ref[g, 0, :, columns], e_ref[g, 1, :, columns]), NN)
            acc = part if acc is None else acc + part
        re, im = acc[:height], acc[height:]
        if last:
            scratch[0, :, columns] = re
            scratch[1, :, columns] = im
            copies.append(
                pltpu.make_async_copy(scratch.at[:, :, columns], out_ref.at[:, :, columns], sems.at[len(copies)])
            )
            copies[-1].start()
        else:
            out_ref[0, :, columns] = re
            out_ref[1, :, columns] = im
    for copy in copies:
        copy.wait()


def image_step(table, gs, backs, acc, last):
    width = table.shape[-1]
    height = backs[0].shape[1]
    first = acc is None
    operands = list(backs) + ([] if first else [acc])
    return pl.pallas_call(
        functools.partial(image_kernel, tuple(gs), first, last),
        in_specs=[VMEM] * (1 + len(operands)),
        out_specs=pl.BlockSpec(memory_space=pl.ANY) if last else VMEM,
        out_shape=jax.ShapeDtypeStruct((2, height, width), F32),
        scratch_shapes=[pltpu.VMEM((2, height, width), F32), pltpu.SemaphoreType.DMA((len(chunks(width)),))] if last else [],
        compiler_params=LIMIT,
        cost_estimate=pl.CostEstimate(flops=4 * 10**9, bytes_accessed=4 << 20, transcendentals=0),
        name="image_step",
    )(table, *operands)


def swap(value, axis, bit):
    return lax.ppermute(value, axis, [(i, i ^ bit) for i in range(lax.axis_size(axis))])


def per_device(facets, column_start, subgrid_start, vis_count, vis_row, vis_weight):
    rows = lax.axis_size("frow")
    cols = lax.axis_size("fcol")
    height, width = facets.shape[1:]
    rows_total, cols_total = height * rows, width * cols
    count = SG // cols
    assert vis_count.shape[0] == 1 and count <= height

    b_table = wave_table(height, rows_total, rows_total)
    turned = jnp.asarray(b_table.reshape(4 * height, rows_total).T.copy())
    b_table = jnp.asarray(np.concatenate([b_table[:2], b_table]).reshape(6 * height, rows_total))
    angle = np.arange(rows)[:, None] * np.arange(rows_total)[None, :] % rows * (2.0 * np.pi / rows)
    roots = jnp.asarray(np.stack([np.cos(angle), np.sin(angle)], 1).astype(np.float32))

    top = cols // 2
    column_start = column_start.reshape(1, 1)
    waves = waves_of(count, width, cols_total)
    sent, z, tilt = first_strips(column_start, facets, waves, range(top + 1, cols, 2))
    far = far_strips(z, waves, range(top, cols, 2)) + swap(sent, "fcol", 1)
    far, z = lax.optimization_barrier((far, z))
    sent, near, *turns = near_strips(subgrid_start, z, waves, [tuple(range(1, top, 2)), tuple(range(0, top, 2))])
    terms = [near + swap(far, "fcol", top), swap(sent, "fcol", 1)]
    bit = 2
    while bit < top:
        pairs = sum(terms).reshape((-1, 2) + far.shape[1:])
        terms = [pairs[:, 0], swap(pairs[:, 1], "fcol", bit)]
        bit *= 2

    own = pack(terms, vis_weight, vis_row, vis_count.reshape(1, 1), count, height)
    tables = b_table, roots, *turns
    order = list(range(0, rows, 2)) + list(range(rows - 1, 0, -2))
    ahead = [(order[i], order[(i + 1) % rows]) for i in range(rows)]
    behind = [(b, a) for a, b in ahead]
    first_state = state = gather_step("first", tables, [own], (0,), count)
    last = rows // 2 - 1
    assert last >= 3
    made = jax.ShapeDtypeStruct((cols, 2, 2 * count, width), BF)
    up = down = own
    for step in range(1, last + 1):
        up = lax.ppermute(up, "frow", ahead)
        down = lax.ppermute(down, "frow", behind)
        up, state = lax.optimization_barrier((up, state))
        if step == last - 2:
            before, early = state, [up, down]
            state = gather_step("skip", tables, [state, up, down], (-step, step), count)
        elif step == last - 1:
            steps = (1 - step, step - 1, -step, step)
            operands = [state, before, *early, up, down, *waves, tilt]
            state, image_table = gather_step("late", tables, operands, steps, count, made)
        elif step == last:
            operands = [state, up, down, *waves, tilt, image_table]
            state, image_table = gather_step("last", tables, operands, (-step, step), count, made)
        else:
            state = gather_step("plain", tables, [state, up, down], (-step, step), count)
    up = lax.ppermute(up, "frow", ahead)
    back, sub = back_step(tables, turned, state, up, height)

    near, far = {0: back}, {top: swap(back, "fcol", top)}

    def spread(blocks, bit):
        return {g ^ bit: swap(b, "fcol", bit) for g, b in blocks.items()}

    def image(blocks, acc, last=False):
        return image_step(image_table, blocks.keys(), list(blocks.values()), acc, last)

    acc = image(near, None)
    near[0], acc = lax.optimization_barrier((back, acc))
    bit = top // 2
    while bit >= 1:
        near |= spread(near, bit)
        bit //= 2
    del near[0]
    acc = image(near, acc)
    corrected = correct_step(sub, first_state, roots)
    far[top], acc, corrected = lax.optimization_barrier((far[top], acc, corrected))
    bit = top // 2
    while bit > 1:
        far |= spread(far, bit)
        bit //= 2
    rest = spread(far, 1)
    acc = image(far, acc)
    return corrected, image(rest, acc, last=True)


def solution(mesh):
    return jax.shard_map(
        per_device,
        mesh=mesh,
        in_specs=(
            P(None, "frow", "fcol"),
            P(),
            P(),
            P("frow"),
            P("frow", None),
            P("frow", None, "fcol"),
        ),
        out_specs=(P("frow", "fcol", None, None), P(None, "frow", "fcol")),
        check_vma=False,
    )
```

```python
import functools
import math

import jax
import jax.numpy as jnp
import ml_dtypes
import numpy as np
from jax import lax
from jax.experimental import pallas as pl
from jax.experimental.pallas import tpu as pltpu
from jax.sharding import PartitionSpec as P

SG = 512
MAXB = 64
META = 8

BF = jnp.bfloat16
F32 = jnp.float32
NN = (((1,), (0,)), ((), ()))
NT = (((1,), (1,)), ((), ()))
VMEM = pl.BlockSpec(memory_space=pltpu.VMEM)
SMEM = pl.BlockSpec(memory_space=pltpu.SMEM)
LIMIT = pltpu.CompilerParams(vmem_limit_bytes=32 << 20)


def halves(value):
    high = value.astype(BF)
    return high, (value - high.astype(F32)).astype(BF)


def dot3(left, right, dims):
    def dot(a, b):
        return lax.dot_general(a, b, dims, preferred_element_type=F32)
    return dot(left[0], right[0]) + (dot(left[0], right[1]) + dot(left[1], right[0]))


def unit(phase, modulus, scale=1.0):
    angle = (phase & (modulus - 1)).astype(F32) * F32(2.0 * math.pi / modulus)
    return jnp.cos(angle) * F32(scale), jnp.sin(angle) * F32(scale)


def lanes(count, rows=1):
    return lax.broadcasted_iota(jnp.int32, (rows, count), 1)


def wave_parts(rows, stride, cols, modulus):
    phase = np.arange(rows, dtype=np.int64)[:, None] * (stride * np.arange(cols, dtype=np.int64))[None, :] % modulus
    angle = phase * (2.0 * np.pi / modulus)
    return np.stack([np.cos(angle), np.sin(angle)])


def wave_table(rows, cols, modulus):
    parts = wave_parts(rows, 1, cols, modulus)
    high = parts.astype(ml_dtypes.bfloat16)
    low = (parts - high.astype(np.float64)).astype(ml_dtypes.bfloat16)
    return np.concatenate([high, low])


def ring_place(r, rows):
    return jnp.where(lax.rem(r, 2) == 0, r // 2, rows - 1 - r // 2)


def ring_block(place, rows):
    place = lax.rem(place + rows, rows)
    return jnp.where(place < rows // 2, 2 * place, 2 * (rows - 1 - place) + 1)


def wave_kernel(width, cols_total, base_ref, steps_ref):
    own = lax.axis_index("fcol")
    blocks, _, count, _ = base_ref.shape
    row = lax.broadcasted_iota(jnp.int32, (count, 128), 0)
    for ref, coord in ((base_ref, lanes(128)), (steps_ref, lanes(128) * 128 + own * width)):
        cos, sin = unit(row * coord, cols_total)
        for g in range(blocks):
            pc, ps = unit((own ^ g) * count * coord, cols_total)
            ref[g, 0] = cos * pc - sin * ps
            ref[g, 1] = sin * pc + cos * ps


def waves_of(count, width, cols_total):
    shape = jax.ShapeDtypeStruct((SG // count, 2, count, 128), F32)
    return pl.pallas_call(
        functools.partial(wave_kernel, width, cols_total),
        out_specs=[VMEM] * 2,
        out_shape=[shape] * 2,
        compiler_params=LIMIT,
        cost_estimate=pl.CostEstimate(flops=10**9, bytes_accessed=2 << 20, transcendentals=0),
        name="waves",
    )()


def waves_in(base, turn, begin, size):
    cos, sin = [], []
    for t in range(begin // 128, (begin + size) // 128):
        tc, ts = turn[0][:, t : t + 1], turn[1][:, t : t + 1]
        cos.append(tc * base[0] - ts * base[1])
        sin.append(ts * base[0] + tc * base[1])
    return halves(jnp.concatenate([jnp.concatenate(cos, 1), jnp.concatenate(sin, 1)]))


def strip_sums(gs, z_ref, base_ref, steps_ref, out_ref):
    count, height = out_ref.shape[-2:]
    z = z_ref[0], z_ref[1]
    for i, g in enumerate(gs):
        base, turn = (base_ref[g, 0], base_ref[g, 1]), (steps_ref[g, 0], steps_ref[g, 1])
        acc = None
        for begin, size in chunks(z_ref.shape[-1]):
            waves = waves_in(base, turn, begin, size)
            part = dot3(waves, [value[:, begin : begin + size] for value in z], NT)
            acc = part if acc is None else acc + part
        cos, sin = acc[:count], acc[count:]
        out_ref[i, 0] = cos[:, :height] + sin[:, height:]
        out_ref[i, 1] = cos[:, height:] - sin[:, :height]


def first_strip_kernel(gs, cols_total, start_ref, x_ref, base_ref, steps_ref, out_ref, z_ref, tilt_ref):
    own = lax.axis_index("fcol")
    width = x_ref.shape[-1]
    start, scale = start_ref[0:1, 0:1], 1.0 / math.sqrt(cols_total)
    pc, ps = unit(start * (own * width + lanes(width)), cols_total, scale)
    re, im = x_ref[0], x_ref[1]
    z_ref[0], z_ref[1] = halves(jnp.concatenate([re * pc + im * ps, im * pc - re * ps]))
    tilt_ref[0:1], tilt_ref[1:2] = unit(start * lanes(128), cols_total)
    tilt_ref[2:3], tilt_ref[3:4] = unit(start * (own * width + 128 * lanes(128)), cols_total, scale)
    strip_sums(gs, z_ref, base_ref, steps_ref, out_ref)


def first_strips(column_start, facets, waves, gs):
    cols, _, count, _ = waves[0].shape
    _, height, width = facets.shape
    return pl.pallas_call(
        functools.partial(first_strip_kernel, tuple(gs), cols * width),
        in_specs=[VMEM] * 4,
        out_specs=[VMEM] * 3,
        out_shape=[
            jax.ShapeDtypeStruct((len(gs), 2, count, height), F32),
            jax.ShapeDtypeStruct((2, 2 * height, width), BF),
            jax.ShapeDtypeStruct((4, 128), F32),
        ],
        compiler_params=LIMIT,
        cost_estimate=pl.CostEstimate(flops=10**9, bytes_accessed=2 << 20, transcendentals=0),
        name="first_strips",
    )(column_start, facets, *waves)


def far_strip_kernel(gs, z_ref, base_ref, steps_ref, out_ref):
    strip_sums(gs, z_ref, base_ref, steps_ref, out_ref)


def far_strips(z, waves, gs):
    return pl.pallas_call(
        functools.partial(far_strip_kernel, tuple(gs)),
        in_specs=[VMEM] * 3,
        out_specs=VMEM,
        out_shape=jax.ShapeDtypeStruct((len(gs), 2, waves[0].shape[2], z.shape[1] // 2), F32),
        compiler_params=LIMIT,
        cost_estimate=pl.CostEstimate(flops=10**9, bytes_accessed=2 << 20, transcendentals=0),
        name="far_strips",
    )(z, *waves)


def near_strip_kernel(groups, starts_ref, z_ref, base_ref, steps_ref, *refs):
    out_refs, (turn_ref, away_ref, starts, sem) = refs[: len(groups)], refs[len(groups) :]
    copy = pltpu.make_async_copy(starts_ref, starts, sem)
    copy.start()
    for gs, out_ref in zip(groups, out_refs):
        strip_sums(gs, z_ref, base_ref, steps_ref, out_ref)
    copy.wait()
    rows, _, height = turn_ref.shape
    rows_total = rows * height
    mine = starts[lax.axis_index("frow")]
    for r in range(rows):
        turn_ref[r, 0:1], turn_ref[r, 1:2] = unit(mine * (r * height + lanes(height)), rows_total, 1.0 / math.sqrt(rows_total))
        away_ref[r] = jnp.full((1, 128), mine - starts[r], jnp.int32)


def near_strips(starts, z, waves, groups):
    rows, count, height = starts.shape[0], waves[0].shape[2], z.shape[1] // 2
    return pl.pallas_call(
        functools.partial(near_strip_kernel, groups),
        in_specs=[pl.BlockSpec(memory_space=pl.ANY)] + [VMEM] * 3,
        out_specs=[VMEM] * (len(groups) + 2),
        out_shape=[jax.ShapeDtypeStruct((len(gs), 2, count, height), F32) for gs in groups]
        + [jax.ShapeDtypeStruct((rows, 2, height), F32), jax.ShapeDtypeStruct((rows, 1, 128), jnp.int32)],
        scratch_shapes=[pltpu.SMEM((rows,), jnp.int32), pltpu.SemaphoreType.DMA],
        compiler_params=LIMIT,
        cost_estimate=pl.CostEstimate(flops=4 * 10**9, bytes_accessed=2 << 20, transcendentals=0),
        name="near_strips",
    )(starts, z, *waves)


def pack_kernel(terms, *refs):
    weight_ref, row_ref, live_ref, out_ref = refs[terms:]
    count = refs[0].shape[2]
    strip = sum(ref[0] for ref in refs[:terms])
    out_ref[:count], out_ref[count : 2 * count] = strip[0], strip[1]
    width = out_ref.shape[1]
    weight = weight_ref[0]
    if count < width:
        weight = jnp.concatenate([weight, jnp.zeros((MAXB, width - count), F32)], 1)
    out_ref[2 * count : 2 * count + MAXB] = weight
    row = jnp.where(lanes(MAXB) < live_ref[0:1, 0:1], row_ref[...], -1).astype(F32)
    row = jnp.concatenate([row, jnp.zeros((1, width - MAXB), F32)], 1)
    out_ref[2 * count + MAXB :] = jnp.broadcast_to(row, (META, width))


def pack(terms, weight, row, live, count, height):
    return pl.pallas_call(
        functools.partial(pack_kernel, len(terms)),
        in_specs=[VMEM] * (len(terms) + 3),
        out_specs=VMEM,
        out_shape=jax.ShapeDtypeStruct((2 * count + MAXB + META, height), F32),
        compiler_params=LIMIT,
        name="pack",
    )(*terms, weight, row, live)


class Message:
    def __init__(self, r, message, refs, height, count, rows_total):
        b_ref, roots_ref, turn_ref, away_ref = refs
        own = lax.axis_index("frow")
        strip, rest = message[: 2 * count], message[2 * count :]
        pc, ps = turn_ref[r, 0:1], turn_ref[r, 1:2]
        re, im = strip[:count], strip[count:]
        re, im = re * pc + im * ps, im * pc - re * ps
        high, low = halves(jnp.concatenate([jnp.concatenate([re, im], 1), jnp.concatenate([im, -re], 1)]))
        self.left = jnp.concatenate([high, low, high], 1)

        width = message.shape[1]
        flat = jnp.concatenate([rest, jnp.zeros((width - rest.shape[0], width), F32)])
        turned = jnp.transpose(flat)
        self.weight = jnp.concatenate(halves(turned[:count, :MAXB]), 1)
        row = turned[:MAXB, MAXB : MAXB + 1].astype(jnp.int32)
        self.away = away_ref[r][0:1, 0:1]
        self.place = jnp.where(row < 0, -1, (row - self.away) & (rows_total - 1))
        self.turn = lax.rem(r - own + rows_total // height, rows_total // height)
        self.refs, self.count, self.rows_total = (b_ref, roots_ref), count, rows_total

    def chunk(self, begin, size):
        b_ref, roots_ref = self.refs
        part = lax.dot_general(self.left, b_ref[:, begin : begin + size], NN, preferred_element_type=F32)
        pc, ps = roots_ref[self.turn, 0:1, begin : begin + size], roots_ref[self.turn, 1:2, begin : begin + size]
        re, im = part[: self.count], part[self.count :]
        freq = begin + lanes(size)
        hot = (begin + lanes(size, MAXB) == self.place).astype(F32).astype(BF)
        gain = lax.dot_general(self.weight, jnp.concatenate([hot, hot]), NN, preferred_element_type=F32)
        seen = (((freq + self.away) & (self.rows_total - 1)) < SG).astype(F32)
        return re * pc + im * ps, im * pc - re * ps, gain + seen


def chunks(total, size=256):
    return [(begin, min(size, total - begin)) for begin in range(0, total, size)]


def image_waves(base_ref, steps_ref, tilt_ref, out_ref):
    def tilted(cos, sin, row):
        pc, ps = tilt_ref[row : row + 1], tilt_ref[row + 1 : row + 2]
        return cos * pc - sin * ps, sin * pc + cos * ps

    for g in range(out_ref.shape[0]):
        base, turn = tilted(base_ref[g, 0], base_ref[g, 1], 0), tilted(steps_ref[g, 0], steps_ref[g, 1], 2)
        for begin, size in chunks(out_ref.shape[-1]):
            columns = slice(begin, begin + size)
            out_ref[g, 0, :, columns], out_ref[g, 1, :, columns] = waves_in(base, turn, begin, size)


def gather_kernel(kind, steps, rows, height, count, *refs):
    tables, refs = refs[:4], refs[4:]
    odd = lax.rem(lax.axis_index("fcol"), 2) == 1
    at = ring_place(lax.axis_index("frow"), rows)

    def add(state_ref, arrived, out_ref, gain_ref=None):
        found = [
            Message(ring_block(at + step, rows), message[...], tables, height, count, rows * height)
            for step, message in arrived
        ]
        for begin, size in chunks(rows * height):
            terms = [message.chunk(begin, size) for message in found]
            if gain_ref is not None and begin < SG:
                gain_ref[:, begin : begin + size] = terms[0][2]
            for i in range(3):
                value = sum(term[i] for term in terms)
                if state_ref is not None:
                    value = value + state_ref[i, :, begin : begin + size]
                out_ref[i, :, begin : begin + size] = value

    if kind == "first":
        add(None, zip(steps, refs), refs[-1])
    elif kind == "plain":
        add(refs[0], zip(steps, refs[1:]), refs[-1])
    elif kind == "own":

        @pl.when(jnp.logical_not(odd))
        def _():
            add(None, zip(steps, refs), refs[-1])

    elif kind == "skip":

        @pl.when(jnp.logical_not(odd))
        def _():
            add(refs[0], zip(steps, refs[1:]), refs[-1])

    elif kind in ("late", "late own"):
        whole = kind == "late own"
        state_ref, before_ref, early, now, waves, (out_ref, made_ref, gain_ref) = (
            refs[0], refs[1], refs[2:4], refs[4:6], refs[6:9], refs[9:]
        )

        @pl.when(jnp.logical_not(odd))
        def _():
            add(state_ref, zip(steps[2:], now), out_ref)

        @pl.when(odd)
        def _():
            if whole:
                add(None, zip((0, *steps), [before_ref, *early, *now]), out_ref, gain_ref)
            else:
                add(before_ref, zip(steps, [*early, *now]), out_ref)
            image_waves(*waves, made_ref)

    else:
        state_ref, now, waves, made_ref, (out_ref, waves_ref) = refs[0], refs[1:3], refs[3:6], refs[6], refs[7:]
        add(state_ref, zip(steps, now), out_ref)

        @pl.when(odd)
        def _():
            waves_ref[...] = made_ref[...]

        @pl.when(jnp.logical_not(odd))
        def _():
            image_waves(*waves, waves_ref)


def gather_step(kind, tables, operands, steps, count, *more):
    height, rows_total = tables[2].shape[2], tables[0].shape[1]
    shapes = [jax.ShapeDtypeStruct((3, count, rows_total), F32), *more]
    out = pl.pallas_call(
        functools.partial(gather_kernel, kind, steps, rows_total // height, height, count),
        in_specs=[VMEM] * (len(tables) + len(operands)),
        out_specs=[VMEM] * len(shapes),
        out_shape=shapes,
        compiler_params=LIMIT,
        cost_estimate=pl.CostEstimate(flops=10**9, bytes_accessed=4 << 20, transcendentals=0),
        name="gather_step",
    )(*tables, *operands)
    return out if more else out[0]


def back_kernel(rows, height, count, *refs):
    tables, (turned_ref, state_ref, message_ref, back_ref, sub_ref) = refs[:4], refs[4:]
    rows_total = rows * height
    own = lax.axis_index("frow")
    r = ring_block(ring_place(own, rows) + rows // 2, rows)
    message = Message(r, message_ref[...], tables, height, count, rows_total)
    acc = None
    for begin, size in chunks(rows_total):
        terms = message.chunk(begin, size)
        re, im, gain = [term + state_ref[i, :, begin : begin + size] for i, term in enumerate(terms)]
        if begin < SG:
            sub_ref[0, :, begin : begin + size] = re
            sub_ref[1, :, begin : begin + size] = im
        high, low = halves(jnp.concatenate([re * gain, im * gain]))
        table = turned_ref[begin : begin + size]
        part = lax.dot_general(high, table, NN, preferred_element_type=F32)
        part = part[:, : 2 * height] + (
            part[:, 2 * height :] + lax.dot_general(low, table[:, : 2 * height], NN, preferred_element_type=F32)
        )
        acc = part if acc is None else acc + part
    re = acc[:count, :height] - acc[count:, height:]
    im = acc[count:, :height] + acc[:count, height:]
    pc, ps = tables[2][own, 0:1], tables[2][own, 1:2]
    back_ref[0] = jnp.transpose(re * pc - im * ps)
    back_ref[1] = jnp.transpose(im * pc + re * ps)


def back_step(tables, turned, state, message, height):
    count, rows_total = state.shape[1:]
    return pl.pallas_call(
        functools.partial(back_kernel, rows_total // height, height, count),
        in_specs=[VMEM] * 7,
        out_specs=[VMEM] * 2,
        out_shape=[
            jax.ShapeDtypeStruct((2, height, count), F32),
            jax.ShapeDtypeStruct((2, count, SG), F32),
        ],
        compiler_params=LIMIT,
        name="back_step",
    )(*tables, turned, state, message)


def correct_kernel(whole, sub_ref, gain_ref, late_ref, roots_ref, out_ref):
    count = sub_ref.shape[1]
    pieces = SG // 128
    own = lax.axis_index("frow")
    pc, ps = roots_ref[own, 0:1, :SG], roots_ref[own, 1:2, :SG]
    re, im, gain = sub_ref[0], sub_ref[1], gain_ref[2, :, :SG]
    if whole:
        gain = jnp.where(lax.rem(lax.axis_index("fcol"), 2) == 1, late_ref[...], gain)
    for part, value in enumerate([(re * pc + im * ps) * gain, (im * pc - re * ps) * gain]):
        for i in range(pieces):
            out_ref[pl.ds(2 * i + part, count, stride=2 * pieces), :] = value[:, 128 * i : 128 * (i + 1)]


def correct_step(whole, sub, first_state, own_gain, roots):
    count = sub.shape[1]
    out = pl.pallas_call(
        functools.partial(correct_kernel, whole),
        in_specs=[VMEM] * 4,
        out_specs=VMEM,
        out_shape=jax.ShapeDtypeStruct((count * 2 * SG // 128, 128), F32),
        compiler_params=LIMIT,
        cost_estimate=pl.CostEstimate(flops=4 * 10**9, bytes_accessed=4 << 20, transcendentals=0),
        name="correct_step",
    )(sub, first_state, own_gain, roots)
    out = out.reshape(count, SG // 128, 2, 128)
    return jnp.transpose(out, (0, 2, 1, 3)).reshape(1, count, 2, SG)


def image_kernel(gs, first, last, e_ref, *refs):
    backs, refs = refs[: len(gs)], refs[len(gs) :]
    acc_ref = None if first else refs[0]
    out_ref = refs[0 if first else 1]
    if last:
        scratch, sems = refs[-2:]
    width = e_ref.shape[-1]
    height = backs[0].shape[1]
    left = []
    for back in backs:
        re, im = back[0], back[1]
        left.append(halves(jnp.concatenate([jnp.concatenate([re, -im], 1), jnp.concatenate([im, re], 1)])))
    copies = []
    for begin, size in chunks(width):
        columns = slice(begin, begin + size)
        acc = None if first else jnp.concatenate([acc_ref[0, :, columns], acc_ref[1, :, columns]])
        for (high, low), g in zip(left, gs):
            part = dot3((high, low), (e_ref[g, 0, :, columns], e_ref[g, 1, :, columns]), NN)
            acc = part if acc is None else acc + part
        re, im = acc[:height], acc[height:]
        if last:
            scratch[0, :, columns] = re
            scratch[1, :, columns] = im
            copies.append(
                pltpu.make_async_copy(scratch.at[:, :, columns], out_ref.at[:, :, columns], sems.at[len(copies)])
            )
            copies[-1].start()
        else:
            out_ref[0, :, columns] = re
            out_ref[1, :, columns] = im
    for copy in copies:
        copy.wait()


def image_step(table, gs, backs, acc, last):
    width = table.shape[-1]
    height = backs[0].shape[1]
    first = acc is None
    operands = list(backs) + ([] if first else [acc])
    return pl.pallas_call(
        functools.partial(image_kernel, tuple(gs), first, last),
        in_specs=[VMEM] * (1 + len(operands)),
        out_specs=pl.BlockSpec(memory_space=pl.ANY) if last else VMEM,
        out_shape=jax.ShapeDtypeStruct((2, height, width), F32),
        scratch_shapes=[pltpu.VMEM((2, height, width), F32), pltpu.SemaphoreType.DMA((len(chunks(width)),))] if last else [],
        compiler_params=LIMIT,
        cost_estimate=pl.CostEstimate(flops=4 * 10**9, bytes_accessed=4 << 20, transcendentals=0),
        name="image_step",
    )(table, *operands)


def swap(value, axis, bit):
    return lax.ppermute(value, axis, [(i, i ^ bit) for i in range(lax.axis_size(axis))])


def per_device(facets, column_start, subgrid_start, vis_count, vis_row, vis_weight):
    rows = lax.axis_size("frow")
    cols = lax.axis_size("fcol")
    height, width = facets.shape[1:]
    rows_total, cols_total = height * rows, width * cols
    count = SG // cols
    assert vis_count.shape[0] == 1 and count <= height

    b_table = wave_table(height, rows_total, rows_total)
    turned = jnp.asarray(b_table.reshape(4 * height, rows_total).T.copy())
    b_table = jnp.asarray(np.concatenate([b_table[:2], b_table]).reshape(6 * height, rows_total))
    angle = np.arange(rows)[:, None] * np.arange(rows_total)[None, :] % rows * (2.0 * np.pi / rows)
    roots = jnp.asarray(np.stack([np.cos(angle), np.sin(angle)], 1).astype(np.float32))

    top = cols // 2
    column_start = column_start.reshape(1, 1)
    waves = waves_of(count, width, cols_total)
    sent, z, tilt = first_strips(column_start, facets, waves, range(top + 1, cols, 2))
    far = far_strips(z, waves, range(top, cols, 2)) + swap(sent, "fcol", 1)
    far, z = lax.optimization_barrier((far, z))
    sent, near, *turns = near_strips(subgrid_start, z, waves, [tuple(range(1, top, 2)), tuple(range(0, top, 2))])
    terms = [near + swap(far, "fcol", top), swap(sent, "fcol", 1)]
    bit = 2
    while bit < top:
        pairs = sum(terms).reshape((-1, 2) + far.shape[1:])
        terms = [pairs[:, 0], swap(pairs[:, 1], "fcol", bit)]
        bit *= 2

    own = pack(terms, vis_weight, vis_row, vis_count.reshape(1, 1), count, height)
    tables = b_table, roots, *turns
    order = list(range(0, rows, 2)) + list(range(rows - 1, 0, -2))
    ahead = [(order[i], order[(i + 1) % rows]) for i in range(rows)]
    behind = [(b, a) for a, b in ahead]
    last = rows // 2 - 1
    assert last >= 3
    whole = last == 3
    first_state = state = gather_step("own" if whole else "first", tables, [own], (0,), count)
    made = jax.ShapeDtypeStruct((cols, 2, 2 * count, width), BF)
    up = down = own
    for step in range(1, last + 1):
        up = lax.ppermute(up, "frow", ahead)
        down = lax.ppermute(down, "frow", behind)
        up, state = lax.optimization_barrier((up, state))
        if step == last - 2:
            before, early = state, [up, down]
            state = gather_step("skip", tables, [state, up, down], (-step, step), count)
        elif step == last - 1:
            steps = (1 - step, step - 1, -step, step)
            operands = [state, own if whole else before, *early, up, down, *waves, tilt]
            own_gain = jax.ShapeDtypeStruct((count, SG), F32)
            kind = "late own" if whole else "late"
            state, image_table, own_gain = gather_step(kind, tables, operands, steps, count, made, own_gain)
        elif step == last:
            operands = [state, up, down, *waves, tilt, image_table]
            state, image_table = gather_step("last", tables, operands, (-step, step), count, made)
        else:
            state = gather_step("plain", tables, [state, up, down], (-step, step), count)
    up = lax.ppermute(up, "frow", ahead)
    back, sub = back_step(tables, turned, state, up, height)

    near, far = {0: back}, {top: swap(back, "fcol", top)}

    def spread(blocks, bit):
        return {g ^ bit: swap(b, "fcol", bit) for g, b in blocks.items()}

    def image(blocks, acc, last=False):
        return image_step(image_table, blocks.keys(), list(blocks.values()), acc, last)

    acc = image(near, None)
    near[0], acc = lax.optimization_barrier((back, acc))
    bit = top // 2
    while bit >= 1:
        near |= spread(near, bit)
        bit //= 2
    del near[0]
    acc = image(near, acc)
    corrected = correct_step(whole, sub, first_state, own_gain, roots)
    far[top], acc, corrected = lax.optimization_barrier((far[top], acc, corrected))
    bit = top // 2
    while bit > 1:
        far |= spread(far, bit)
        bit //= 2
    rest = spread(far, 1)
    acc = image(far, acc)
    return corrected, image(rest, acc, last=True)


def solution(mesh):
    return jax.shard_map(
        per_device,
        mesh=mesh,
        in_specs=(
            P(None, "frow", "fcol"),
            P(),
            P(),
            P("frow"),
            P("frow", None),
            P("frow", None, "fcol"),
        ),
        out_specs=(P("frow", "fcol", None, None), P(None, "frow", "fcol")),
        check_vma=False,
    )
```

```python
import functools
import math

import jax
import jax.numpy as jnp
import ml_dtypes
import numpy as np
from jax import lax
from jax.experimental import pallas as pl
from jax.experimental.pallas import tpu as pltpu
from jax.sharding import PartitionSpec as P

SG = 512
MAXB = 64
META = 8

BF = jnp.bfloat16
F32 = jnp.float32
NN = (((1,), (0,)), ((), ()))
NT = (((1,), (1,)), ((), ()))
VMEM = pl.BlockSpec(memory_space=pltpu.VMEM)
SMEM = pl.BlockSpec(memory_space=pltpu.SMEM)
LIMIT = pltpu.CompilerParams(vmem_limit_bytes=32 << 20)


def halves(value):
    high = value.astype(BF)
    return high, (value - high.astype(F32)).astype(BF)


def dot3(left, right, dims):
    def dot(a, b):
        return lax.dot_general(a, b, dims, preferred_element_type=F32)
    return dot(left[0], right[0]) + (dot(left[0], right[1]) + dot(left[1], right[0]))


def unit(phase, modulus, scale=1.0):
    angle = (phase & (modulus - 1)).astype(F32) * F32(2.0 * math.pi / modulus)
    return jnp.cos(angle) * F32(scale), jnp.sin(angle) * F32(scale)


def lanes(count, rows=1):
    return lax.broadcasted_iota(jnp.int32, (rows, count), 1)


def wave_parts(rows, stride, cols, modulus):
    phase = np.arange(rows, dtype=np.int64)[:, None] * (stride * np.arange(cols, dtype=np.int64))[None, :] % modulus
    angle = phase * (2.0 * np.pi / modulus)
    return np.stack([np.cos(angle), np.sin(angle)])


def wave_table(rows, cols, modulus):
    parts = wave_parts(rows, 1, cols, modulus)
    high = parts.astype(ml_dtypes.bfloat16)
    low = (parts - high.astype(np.float64)).astype(ml_dtypes.bfloat16)
    return np.concatenate([high, low])


def ring_place(r, rows):
    return jnp.where(lax.rem(r, 2) == 0, r // 2, rows - 1 - r // 2)


def ring_block(place, rows):
    place = lax.rem(place + rows, rows)
    return jnp.where(place < rows // 2, 2 * place, 2 * (rows - 1 - place) + 1)


def wave_kernel(width, cols_total, base_ref, steps_ref):
    own = lax.axis_index("fcol")
    blocks, _, count, _ = base_ref.shape
    down = lax.broadcasted_iota(jnp.int32, (count, 128), 0)
    cos, sin = unit(down * lanes(128), cols_total)
    tiles = width // 128
    every = own * width + 128 * lax.broadcasted_iota(jnp.int32, (tiles, 128), 0)
    for g in range(blocks):
        first = (own ^ g) * count
        pc, ps = unit(first * lanes(128), cols_total)
        base_ref[g, 0] = cos * pc - sin * ps
        base_ref[g, 1] = sin * pc + cos * ps
        for part, value in enumerate(unit((first + lanes(128, tiles)) * every, cols_total)):
            steps_ref[g, part, :, :tiles] = jnp.transpose(value)[:count]


def waves_of(count, width, cols_total):
    shape = jax.ShapeDtypeStruct((SG // count, 2, count, 128), F32)
    return pl.pallas_call(
        functools.partial(wave_kernel, width, cols_total),
        out_specs=[VMEM] * 2,
        out_shape=[shape] * 2,
        compiler_params=LIMIT,
        cost_estimate=pl.CostEstimate(flops=10**9, bytes_accessed=2 << 20, transcendentals=0),
        name="waves",
    )()


def waves_in(base, turn, begin, size):
    cos, sin = [], []
    for t in range(begin // 128, (begin + size) // 128):
        tc, ts = turn[0][:, t : t + 1], turn[1][:, t : t + 1]
        cos.append(tc * base[0] - ts * base[1])
        sin.append(ts * base[0] + tc * base[1])
    return halves(jnp.concatenate([jnp.concatenate(cos, 1), jnp.concatenate(sin, 1)]))


def strip_sums(gs, z_of, width, base_ref, steps_ref, out_ref):
    count, height = out_ref.shape[-2:]
    for i, g in enumerate(gs):
        base, turn = (base_ref[g, 0], base_ref[g, 1]), (steps_ref[g, 0], steps_ref[g, 1])
        acc = None
        for begin, size in chunks(width):
            part = dot3(waves_in(base, turn, begin, size), z_of(begin, size), NT)
            acc = part if acc is None else acc + part
        cos, sin = acc[:count], acc[count:]
        out_ref[i, 0] = cos[:, :height] + sin[:, height:]
        out_ref[i, 1] = cos[:, height:] - sin[:, :height]


def first_strip_kernel(gs, cols_total, start_ref, x_ref, base_ref, steps_ref, out_ref, z_ref, tilt_ref):
    own = lax.axis_index("fcol")
    width = x_ref.shape[-1]
    start, scale = start_ref[0:1, 0:1], 1.0 / math.sqrt(cols_total)
    made = {}

    def z_of(begin, size):
        if begin not in made:
            columns = slice(begin, begin + size)
            pc, ps = unit(start * (own * width + begin + lanes(size)), cols_total, scale)
            re, im = x_ref[0, :, columns], x_ref[1, :, columns]
            made[begin] = halves(jnp.concatenate([re * pc + im * ps, im * pc - re * ps]))
            z_ref[0, :, columns], z_ref[1, :, columns] = made[begin]
        return made[begin]

    tilt_ref[0:1], tilt_ref[1:2] = unit(start * lanes(128), cols_total)
    tilt_ref[2:3], tilt_ref[3:4] = unit(start * (own * width + 128 * lanes(128)), cols_total, scale)
    strip_sums(gs, z_of, width, base_ref, steps_ref, out_ref)


def first_strips(column_start, facets, waves, gs):
    cols, _, count, _ = waves[0].shape
    _, height, width = facets.shape
    return pl.pallas_call(
        functools.partial(first_strip_kernel, tuple(gs), cols * width),
        in_specs=[VMEM] * 4,
        out_specs=[VMEM] * 3,
        out_shape=[
            jax.ShapeDtypeStruct((len(gs), 2, count, height), F32),
            jax.ShapeDtypeStruct((2, 2 * height, width), BF),
            jax.ShapeDtypeStruct((4, 128), F32),
        ],
        compiler_params=LIMIT,
        cost_estimate=pl.CostEstimate(flops=10**9, bytes_accessed=2 << 20, transcendentals=0),
        name="first_strips",
    )(column_start, facets, *waves)


def columns_of(z_ref):
    return lambda begin, size: (z_ref[0, :, begin : begin + size], z_ref[1, :, begin : begin + size])


def far_strip_kernel(gs, z_ref, base_ref, steps_ref, out_ref):
    strip_sums(gs, columns_of(z_ref), z_ref.shape[-1], base_ref, steps_ref, out_ref)


def far_strips(z, waves, gs):
    return pl.pallas_call(
        functools.partial(far_strip_kernel, tuple(gs)),
        in_specs=[VMEM] * 3,
        out_specs=VMEM,
        out_shape=jax.ShapeDtypeStruct((len(gs), 2, waves[0].shape[2], z.shape[1] // 2), F32),
        compiler_params=LIMIT,
        cost_estimate=pl.CostEstimate(flops=10**9, bytes_accessed=2 << 20, transcendentals=0),
        name="far_strips",
    )(z, *waves)


def near_strip_kernel(groups, starts_ref, z_ref, base_ref, steps_ref, *refs):
    out_refs, (turn_ref, away_ref, starts, sem) = refs[: len(groups)], refs[len(groups) :]
    copy = pltpu.make_async_copy(starts_ref, starts, sem)
    copy.start()
    for gs, out_ref in zip(groups, out_refs):
        strip_sums(gs, columns_of(z_ref), z_ref.shape[-1], base_ref, steps_ref, out_ref)
    copy.wait()
    rows, _, height = turn_ref.shape
    rows_total = rows * height
    mine = starts[lax.axis_index("frow")]
    for r in range(rows):
        turn_ref[r, 0:1], turn_ref[r, 1:2] = unit(mine * (r * height + lanes(height)), rows_total, 1.0 / math.sqrt(rows_total))
        away_ref[r] = jnp.full((1, 128), mine - starts[r], jnp.int32)


def near_strips(starts, z, waves, groups):
    rows, count, height = starts.shape[0], waves[0].shape[2], z.shape[1] // 2
    return pl.pallas_call(
        functools.partial(near_strip_kernel, groups),
        in_specs=[pl.BlockSpec(memory_space=pl.ANY)] + [VMEM] * 3,
        out_specs=[VMEM] * (len(groups) + 2),
        out_shape=[jax.ShapeDtypeStruct((len(gs), 2, count, height), F32) for gs in groups]
        + [jax.ShapeDtypeStruct((rows, 2, height), F32), jax.ShapeDtypeStruct((rows, 1, 128), jnp.int32)],
        scratch_shapes=[pltpu.SMEM((rows,), jnp.int32), pltpu.SemaphoreType.DMA],
        compiler_params=LIMIT,
        cost_estimate=pl.CostEstimate(flops=4 * 10**9, bytes_accessed=2 << 20, transcendentals=0),
        name="near_strips",
    )(starts, z, *waves)


def pack_kernel(terms, *refs):
    weight_ref, row_ref, live_ref, out_ref = refs[terms:]
    count = refs[0].shape[2]
    strip = sum(ref[0] for ref in refs[:terms])
    out_ref[:count], out_ref[count : 2 * count] = strip[0], strip[1]
    width = out_ref.shape[1]
    weight = weight_ref[0]
    if count < width:
        weight = jnp.concatenate([weight, jnp.zeros((MAXB, width - count), F32)], 1)
    out_ref[2 * count : 2 * count + MAXB] = weight
    row = jnp.where(lanes(MAXB) < live_ref[0:1, 0:1], row_ref[...], -1).astype(F32)
    row = jnp.concatenate([row, jnp.zeros((1, width - MAXB), F32)], 1)
    out_ref[2 * count + MAXB :] = jnp.broadcast_to(row, (META, width))


def pack(terms, weight, row, live, count, height):
    return pl.pallas_call(
        functools.partial(pack_kernel, len(terms)),
        in_specs=[VMEM] * (len(terms) + 3),
        out_specs=VMEM,
        out_shape=jax.ShapeDtypeStruct((2 * count + MAXB + META, height), F32),
        compiler_params=LIMIT,
        name="pack",
    )(*terms, weight, row, live)


class Message:
    def __init__(self, r, message, refs, height, count, rows_total):
        b_ref, roots_ref, turn_ref, away_ref = refs
        own = lax.axis_index("frow")
        strip, rest = message[: 2 * count], message[2 * count :]
        pc, ps = turn_ref[r, 0:1], turn_ref[r, 1:2]
        re, im = strip[:count], strip[count:]
        re, im = re * pc + im * ps, im * pc - re * ps
        high, low = halves(jnp.concatenate([jnp.concatenate([re, im], 1), jnp.concatenate([im, -re], 1)]))
        self.left = jnp.concatenate([high, low, high], 1)

        width = message.shape[1]
        flat = jnp.concatenate([rest, jnp.zeros((width - rest.shape[0], width), F32)])
        turned = jnp.transpose(flat)
        self.weight = jnp.concatenate(halves(turned[:count, :MAXB]), 1)
        row = turned[:MAXB, MAXB : MAXB + 1].astype(jnp.int32)
        self.away = away_ref[r][0:1, 0:1]
        self.place = jnp.where(row < 0, -1, (row - self.away) & (rows_total - 1))
        self.turn = lax.rem(r - own + rows_total // height, rows_total // height)
        self.refs, self.count, self.rows_total = (b_ref, roots_ref), count, rows_total

    def chunk(self, begin, size):
        b_ref, roots_ref = self.refs
        part = lax.dot_general(self.left, b_ref[:, begin : begin + size], NN, preferred_element_type=F32)
        pc, ps = roots_ref[self.turn, 0:1, begin : begin + size], roots_ref[self.turn, 1:2, begin : begin + size]
        re, im = part[: self.count], part[self.count :]
        freq = begin + lanes(size)
        hot = (begin + lanes(size, MAXB) == self.place).astype(F32).astype(BF)
        gain = lax.dot_general(self.weight, jnp.concatenate([hot, hot]), NN, preferred_element_type=F32)
        seen = (((freq + self.away) & (self.rows_total - 1)) < SG).astype(F32)
        return re * pc + im * ps, im * pc - re * ps, gain + seen


def chunks(total, size=256):
    return [(begin, min(size, total - begin)) for begin in range(0, total, size)]


def image_waves(base_ref, steps_ref, tilt_ref, out_ref):
    def tilted(cos, sin, row):
        pc, ps = tilt_ref[row : row + 1], tilt_ref[row + 1 : row + 2]
        return cos * pc - sin * ps, sin * pc + cos * ps

    for g in range(out_ref.shape[0]):
        base, turn = tilted(base_ref[g, 0], base_ref[g, 1], 0), tilted(steps_ref[g, 0], steps_ref[g, 1], 2)
        for begin, size in chunks(out_ref.shape[-1]):
            columns = slice(begin, begin + size)
            out_ref[g, 0, :, columns], out_ref[g, 1, :, columns] = waves_in(base, turn, begin, size)


def last_chunks(total):
    return [(0, total // 2), (total // 2, total // 2)]


def gather_kernel(kind, steps, rows, height, count, *refs):
    tables, refs = refs[:4], refs[4:]
    odd = lax.rem(lax.axis_index("fcol"), 2) == 1
    at = ring_place(lax.axis_index("frow"), rows)

    def add(state_ref, arrived, out_ref, gain_ref=None):
        found = [
            Message(ring_block(at + step, rows), message[...], tables, height, count, rows * height)
            for step, message in arrived
        ]
        for begin, size in chunks(rows * height):
            terms = [message.chunk(begin, size) for message in found]
            if gain_ref is not None and begin < SG:
                gain_ref[:, begin : begin + size] = terms[0][2]
            for i in range(3):
                value = sum(term[i] for term in terms)
                if state_ref is not None:
                    value = value + state_ref[i, :, begin : begin + size]
                out_ref[i, :, begin : begin + size] = value

    if kind == "first":
        add(None, zip(steps, refs), refs[-1])
    elif kind == "plain":
        add(refs[0], zip(steps, refs[1:]), refs[-1])
    elif kind == "own":

        @pl.when(jnp.logical_not(odd))
        def _():
            add(None, zip(steps, refs), refs[-1])

    elif kind == "skip":

        @pl.when(jnp.logical_not(odd))
        def _():
            add(refs[0], zip(steps, refs[1:]), refs[-1])

    elif kind in ("late", "late own"):
        whole = kind == "late own"
        state_ref, before_ref, early, now, waves, (out_ref, made_ref, gain_ref) = (
            refs[0], refs[1], refs[2:4], refs[4:6], refs[6:9], refs[9:]
        )

        @pl.when(jnp.logical_not(odd))
        def _():
            add(state_ref, zip(steps[2:], now), out_ref)

        @pl.when(odd)
        def _():
            if whole:
                add(None, zip((0, *steps), [before_ref, *early, *now]), out_ref, gain_ref)
            else:
                add(before_ref, zip(steps, [*early, *now]), out_ref)
            image_waves(*waves, made_ref)

    else:
        state_ref, now, waves, made_ref, (out_ref, waves_ref) = refs[0], refs[1:3], refs[3:6], refs[6], refs[7:]
        add(state_ref, zip(steps, now), out_ref)

        @pl.when(odd)
        def _():
            waves_ref[...] = made_ref[...]

        @pl.when(jnp.logical_not(odd))
        def _():
            image_waves(*waves, waves_ref)


def gather_step(kind, tables, operands, steps, count, *more):
    height, rows_total = tables[2].shape[2], tables[0].shape[1]
    shapes = [jax.ShapeDtypeStruct((3, count, rows_total), F32), *more]
    out = pl.pallas_call(
        functools.partial(gather_kernel, kind, steps, rows_total // height, height, count),
        in_specs=[VMEM] * (len(tables) + len(operands)),
        out_specs=[VMEM] * len(shapes),
        out_shape=shapes,
        compiler_params=LIMIT,
        cost_estimate=pl.CostEstimate(flops=10**9, bytes_accessed=4 << 20, transcendentals=0),
        name="gather_step",
    )(*tables, *operands)
    return out if more else out[0]


def back_kernel(rows, height, count, *refs):
    tables, (turned_ref, state_ref, message_ref, back_ref, sub_ref) = refs[:4], refs[4:]
    rows_total = rows * height
    own = lax.axis_index("frow")
    r = ring_block(ring_place(own, rows) + rows // 2, rows)
    message = Message(r, message_ref[...], tables, height, count, rows_total)
    acc = None
    for begin, size in chunks(rows_total):
        terms = message.chunk(begin, size)
        re, im, gain = [term + state_ref[i, :, begin : begin + size] for i, term in enumerate(terms)]
        if begin < SG:
            sub_ref[0, :, begin : begin + size] = re
            sub_ref[1, :, begin : begin + size] = im
        high, low = halves(jnp.concatenate([re * gain, im * gain]))
        table = turned_ref[begin : begin + size]
        part = lax.dot_general(high, table, NN, preferred_element_type=F32)
        part = part[:, : 2 * height] + (
            part[:, 2 * height :] + lax.dot_general(low, table[:, : 2 * height], NN, preferred_element_type=F32)
        )
        acc = part if acc is None else acc + part
    re = acc[:count, :height] - acc[count:, height:]
    im = acc[count:, :height] + acc[:count, height:]
    pc, ps = tables[2][own, 0:1], tables[2][own, 1:2]
    back_ref[0] = jnp.transpose(re * pc - im * ps)
    back_ref[1] = jnp.transpose(im * pc + re * ps)


def back_step(tables, turned, state, message, height):
    count, rows_total = state.shape[1:]
    return pl.pallas_call(
        functools.partial(back_kernel, rows_total // height, height, count),
        in_specs=[VMEM] * 7,
        out_specs=[VMEM] * 2,
        out_shape=[
            jax.ShapeDtypeStruct((2, height, count), F32),
            jax.ShapeDtypeStruct((2, count, SG), F32),
        ],
        compiler_params=LIMIT,
        name="back_step",
    )(*tables, turned, state, message)


def correct_kernel(whole, sub_ref, gain_ref, late_ref, roots_ref, out_ref):
    count = sub_ref.shape[1]
    pieces = SG // 128
    own = lax.axis_index("frow")
    pc, ps = roots_ref[own, 0:1, :SG], roots_ref[own, 1:2, :SG]
    re, im, gain = sub_ref[0], sub_ref[1], gain_ref[2, :, :SG]
    if whole:
        gain = jnp.where(lax.rem(lax.axis_index("fcol"), 2) == 1, late_ref[...], gain)
    for part, value in enumerate([(re * pc + im * ps) * gain, (im * pc - re * ps) * gain]):
        for i in range(pieces):
            out_ref[pl.ds(2 * i + part, count, stride=2 * pieces), :] = value[:, 128 * i : 128 * (i + 1)]


def correct_step(whole, sub, first_state, own_gain, roots):
    count = sub.shape[1]
    out = pl.pallas_call(
        functools.partial(correct_kernel, whole),
        in_specs=[VMEM] * 4,
        out_specs=VMEM,
        out_shape=jax.ShapeDtypeStruct((count * 2 * SG // 128, 128), F32),
        compiler_params=LIMIT,
        cost_estimate=pl.CostEstimate(flops=4 * 10**9, bytes_accessed=4 << 20, transcendentals=0),
        name="correct_step",
    )(sub, first_state, own_gain, roots)
    out = out.reshape(count, SG // 128, 2, 128)
    return jnp.transpose(out, (0, 2, 1, 3)).reshape(1, count, 2, SG)


def image_kernel(gs, first, last, e_ref, *refs):
    backs, refs = refs[: len(gs)], refs[len(gs) :]
    acc_ref = None if first else refs[0]
    out_ref = refs[0 if first else 1]
    if last:
        scratch, sems = refs[-2:]
    width = e_ref.shape[-1]
    height = backs[0].shape[1]
    left = []
    for back in backs:
        re, im = back[0], back[1]
        left.append(halves(jnp.concatenate([jnp.concatenate([re, -im], 1), jnp.concatenate([im, re], 1)])))
    copies = []
    for begin, size in (last_chunks(width) if last else chunks(width)):
        columns = slice(begin, begin + size)
        acc = None if first else jnp.concatenate([acc_ref[0, :, columns], acc_ref[1, :, columns]])
        for (high, low), g in zip(left, gs):
            part = dot3((high, low), (e_ref[g, 0, :, columns], e_ref[g, 1, :, columns]), NN)
            acc = part if acc is None else acc + part
        re, im = acc[:height], acc[height:]
        if last:
            scratch[0, :, columns] = re
            scratch[1, :, columns] = im
            copies.append(
                pltpu.make_async_copy(scratch.at[:, :, columns], out_ref.at[:, :, columns], sems.at[len(copies)])
            )
            copies[-1].start()
        else:
            out_ref[0, :, columns] = re
            out_ref[1, :, columns] = im
    for copy in copies:
        copy.wait()


def image_step(table, gs, backs, acc, last):
    width = table.shape[-1]
    height = backs[0].shape[1]
    first = acc is None
    operands = list(backs) + ([] if first else [acc])
    return pl.pallas_call(
        functools.partial(image_kernel, tuple(gs), first, last),
        in_specs=[VMEM] * (1 + len(operands)),
        out_specs=pl.BlockSpec(memory_space=pl.ANY) if last else VMEM,
        out_shape=jax.ShapeDtypeStruct((2, height, width), F32),
        scratch_shapes=[pltpu.VMEM((2, height, width), F32), pltpu.SemaphoreType.DMA((len(last_chunks(width)),))] if last else [],
        compiler_params=LIMIT,
        cost_estimate=pl.CostEstimate(flops=4 * 10**9, bytes_accessed=4 << 20, transcendentals=0),
        name="image_step",
    )(table, *operands)


def swap(value, axis, bit):
    return lax.ppermute(value, axis, [(i, i ^ bit) for i in range(lax.axis_size(axis))])


def per_device(facets, column_start, subgrid_start, vis_count, vis_row, vis_weight):
    rows = lax.axis_size("frow")
    cols = lax.axis_size("fcol")
    height, width = facets.shape[1:]
    rows_total, cols_total = height * rows, width * cols
    count = SG // cols
    assert vis_count.shape[0] == 1 and count <= height

    b_table = wave_table(height, rows_total, rows_total)
    turned = jnp.asarray(b_table.reshape(4 * height, rows_total).T.copy())
    b_table = jnp.asarray(np.concatenate([b_table[:2], b_table]).reshape(6 * height, rows_total))
    angle = np.arange(rows)[:, None] * np.arange(rows_total)[None, :] % rows * (2.0 * np.pi / rows)
    roots = jnp.asarray(np.stack([np.cos(angle), np.sin(angle)], 1).astype(np.float32))

    top = cols // 2
    column_start = column_start.reshape(1, 1)
    waves = waves_of(count, width, cols_total)
    sent, z, tilt = first_strips(column_start, facets, waves, range(top + 1, cols, 2))
    far = far_strips(z, waves, range(top, cols, 2)) + swap(sent, "fcol", 1)
    far, z = lax.optimization_barrier((far, z))
    sent, near, *turns = near_strips(subgrid_start, z, waves, [tuple(range(1, top, 2)), tuple(range(0, top, 2))])
    terms = [near + swap(far, "fcol", top), swap(sent, "fcol", 1)]
    bit = 2
    while bit < top:
        pairs = sum(terms).reshape((-1, 2) + far.shape[1:])
        terms = [pairs[:, 0], swap(pairs[:, 1], "fcol", bit)]
        bit *= 2

    own = pack(terms, vis_weight, vis_row, vis_count.reshape(1, 1), count, height)
    tables = b_table, roots, *turns
    order = list(range(0, rows, 2)) + list(range(rows - 1, 0, -2))
    ahead = [(order[i], order[(i + 1) % rows]) for i in range(rows)]
    behind = [(b, a) for a, b in ahead]
    last = rows // 2 - 1
    assert last >= 3
    whole = last == 3
    first_state = state = gather_step("own" if whole else "first", tables, [own], (0,), count)
    made = jax.ShapeDtypeStruct((cols, 2, 2 * count, width), BF)
    up = down = own
    for step in range(1, last + 1):
        up = lax.ppermute(up, "frow", ahead)
        down = lax.ppermute(down, "frow", behind)
        up, state = lax.optimization_barrier((up, state))
        if step == last - 2:
            before, early = state, [up, down]
            state = gather_step("skip", tables, [state, up, down], (-step, step), count)
        elif step == last - 1:
            steps = (1 - step, step - 1, -step, step)
            operands = [state, own if whole else before, *early, up, down, *waves, tilt]
            own_gain = jax.ShapeDtypeStruct((count, SG), F32)
            kind = "late own" if whole else "late"
            state, image_table, own_gain = gather_step(kind, tables, operands, steps, count, made, own_gain)
        elif step == last:
            operands = [state, up, down, *waves, tilt, image_table]
            state, image_table = gather_step("last", tables, operands, (-step, step), count, made)
        else:
            state = gather_step("plain", tables, [state, up, down], (-step, step), count)
    up = lax.ppermute(up, "frow", ahead)
    back, sub = back_step(tables, turned, state, up, height)

    near, far = {0: back}, {top: swap(back, "fcol", top)}

    def spread(blocks, bit):
        return {g ^ bit: swap(b, "fcol", bit) for g, b in blocks.items()}

    def image(blocks, acc, last=False):
        return image_step(image_table, blocks.keys(), list(blocks.values()), acc, last)

    acc = image(near, None)
    near[0], acc = lax.optimization_barrier((back, acc))
    bit = top // 2
    while bit >= 1:
        near |= spread(near, bit)
        bit //= 2
    del near[0]
    acc = image(near, acc)
    corrected = correct_step(whole, sub, first_state, own_gain, roots)
    far[top], acc, corrected = lax.optimization_barrier((far[top], acc, corrected))
    bit = top // 2
    while bit > 1:
        far |= spread(far, bit)
        bit //= 2
    rest = spread(far, 1)
    acc = image(far, acc)
    return corrected, image(rest, acc, last=True)


def solution(mesh):
    return jax.shard_map(
        per_device,
        mesh=mesh,
        in_specs=(
            P(None, "frow", "fcol"),
            P(),
            P(),
            P("frow"),
            P("frow", None),
            P("frow", None, "fcol"),
        ),
        out_specs=(P("frow", "fcol", None, None), P(None, "frow", "fcol")),
        check_vma=False,
    )
```

```python
import functools
import math

import jax
import jax.numpy as jnp
import ml_dtypes
import numpy as np
from jax import lax
from jax.experimental import pallas as pl
from jax.experimental.pallas import tpu as pltpu
from jax.sharding import PartitionSpec as P

SG = 512
MAXB = 64
META = 8

BF = jnp.bfloat16
F32 = jnp.float32
NN = (((1,), (0,)), ((), ()))
NT = (((1,), (1,)), ((), ()))
VMEM = pl.BlockSpec(memory_space=pltpu.VMEM)
SMEM = pl.BlockSpec(memory_space=pltpu.SMEM)
LIMIT = pltpu.CompilerParams(vmem_limit_bytes=32 << 20)


def halves(value):
    high = value.astype(BF)
    return high, (value - high.astype(F32)).astype(BF)


def dot3(left, right, dims):
    def dot(a, b):
        return lax.dot_general(a, b, dims, preferred_element_type=F32)
    return dot(left[0], right[0]) + (dot(left[0], right[1]) + dot(left[1], right[0]))


def unit(phase, modulus, scale=1.0):
    angle = (phase & (modulus - 1)).astype(F32) * F32(2.0 * math.pi / modulus)
    return jnp.cos(angle) * F32(scale), jnp.sin(angle) * F32(scale)


def lanes(count, rows=1):
    return lax.broadcasted_iota(jnp.int32, (rows, count), 1)


def wave_parts(rows, stride, cols, modulus):
    phase = np.arange(rows, dtype=np.int64)[:, None] * (stride * np.arange(cols, dtype=np.int64))[None, :] % modulus
    angle = phase * (2.0 * np.pi / modulus)
    return np.stack([np.cos(angle), np.sin(angle)])


def wave_table(rows, cols, modulus):
    parts = wave_parts(rows, 1, cols, modulus)
    high = parts.astype(ml_dtypes.bfloat16)
    low = (parts - high.astype(np.float64)).astype(ml_dtypes.bfloat16)
    return np.concatenate([high, low])


def ring_place(r, rows):
    return jnp.where(lax.rem(r, 2) == 0, r // 2, rows - 1 - r // 2)


def ring_block(place, rows):
    place = lax.rem(place + rows, rows)
    return jnp.where(place < rows // 2, 2 * place, 2 * (rows - 1 - place) + 1)


def wave_kernel(width, cols_total, base_ref, steps_ref):
    own = lax.axis_index("fcol")
    blocks, _, count, _ = base_ref.shape
    down = lax.broadcasted_iota(jnp.int32, (count, 128), 0)
    cos, sin = unit(down * lanes(128), cols_total)
    tiles = width // 128
    every = own * width + 128 * lax.broadcasted_iota(jnp.int32, (tiles, 128), 0)
    for g in range(blocks):
        first = (own ^ g) * count
        pc, ps = unit(first * lanes(128), cols_total)
        base_ref[g, 0] = cos * pc - sin * ps
        base_ref[g, 1] = sin * pc + cos * ps
        for part, value in enumerate(unit((first + lanes(128, tiles)) * every, cols_total)):
            steps_ref[g, part, :, :tiles] = jnp.transpose(value)[:count]


def waves_of(count, width, cols_total):
    shape = jax.ShapeDtypeStruct((SG // count, 2, count, 128), F32)
    return pl.pallas_call(
        functools.partial(wave_kernel, width, cols_total),
        out_specs=[VMEM] * 2,
        out_shape=[shape] * 2,
        compiler_params=LIMIT,
        cost_estimate=pl.CostEstimate(flops=10**9, bytes_accessed=2 << 20, transcendentals=0),
        name="waves",
    )()


def waves_in(base, turn, begin, size):
    cos, sin = [], []
    for t in range(begin // 128, (begin + size) // 128):
        tc, ts = turn[0][:, t : t + 1], turn[1][:, t : t + 1]
        cos.append(tc * base[0] - ts * base[1])
        sin.append(ts * base[0] + tc * base[1])
    return halves(jnp.concatenate([jnp.concatenate(cos, 1), jnp.concatenate(sin, 1)]))


def tilted(waves, tilt_ref, row):
    (cos, sin), (pc, ps) = waves, (tilt_ref[row : row + 1], tilt_ref[row + 1 : row + 2])
    return cos * pc - sin * ps, sin * pc + cos * ps


def strip_sums(gs, z_of, width, base_ref, steps_ref, tilt_ref, out_ref):
    count, height = out_ref.shape[-2:]
    for i, g in enumerate(gs):
        base = tilted((base_ref[g, 0], base_ref[g, 1]), tilt_ref, 0)
        turn = tilted((steps_ref[g, 0], steps_ref[g, 1]), tilt_ref, 2)
        acc = None
        for begin, size in chunks(width):
            part = dot3(waves_in(base, turn, begin, size), z_of(begin, size), NT)
            acc = part if acc is None else acc + part
        cos, sin = acc[:count], acc[count:]
        out_ref[i, 0] = cos[:, :height] + sin[:, height:]
        out_ref[i, 1] = cos[:, height:] - sin[:, :height]


def first_strip_kernel(gs, cols_total, start_ref, x_ref, base_ref, steps_ref, out_ref, z_ref, tilt_ref):
    start, begin = start_ref[0:1, 0:1], lax.axis_index("fcol") * x_ref.shape[-1]
    tilt_ref[0:1], tilt_ref[1:2] = unit(start * lanes(128), cols_total)
    tilt_ref[2:3], tilt_ref[3:4] = unit(start * (begin + 128 * lanes(128)), cols_total, 1.0 / math.sqrt(cols_total))
    made = {}

    def z_of(begin, size):
        if begin not in made:
            columns = slice(begin, begin + size)
            made[begin] = halves(jnp.concatenate([x_ref[0, :, columns], x_ref[1, :, columns]]))
            z_ref[0, :, columns], z_ref[1, :, columns] = made[begin]
        return made[begin]

    strip_sums(gs, z_of, x_ref.shape[-1], base_ref, steps_ref, tilt_ref, out_ref)


def first_strips(column_start, facets, waves, gs):
    cols, _, count, _ = waves[0].shape
    _, height, width = facets.shape
    return pl.pallas_call(
        functools.partial(first_strip_kernel, tuple(gs), cols * width),
        in_specs=[VMEM] * 4,
        out_specs=[VMEM] * 3,
        out_shape=[
            jax.ShapeDtypeStruct((len(gs), 2, count, height), F32),
            jax.ShapeDtypeStruct((2, 2 * height, width), BF),
            jax.ShapeDtypeStruct((4, 128), F32),
        ],
        compiler_params=LIMIT,
        cost_estimate=pl.CostEstimate(flops=10**9, bytes_accessed=2 << 20, transcendentals=0),
        name="first_strips",
    )(column_start, facets, *waves)


def columns_of(z_ref):
    return lambda begin, size: (z_ref[0, :, begin : begin + size], z_ref[1, :, begin : begin + size])


def far_strip_kernel(gs, z_ref, base_ref, steps_ref, tilt_ref, out_ref):
    strip_sums(gs, columns_of(z_ref), z_ref.shape[-1], base_ref, steps_ref, tilt_ref, out_ref)


def far_strips(z, waves, gs):
    return pl.pallas_call(
        functools.partial(far_strip_kernel, tuple(gs)),
        in_specs=[VMEM] * 4,
        out_specs=VMEM,
        out_shape=jax.ShapeDtypeStruct((len(gs), 2, waves[0].shape[2], z.shape[1] // 2), F32),
        compiler_params=LIMIT,
        cost_estimate=pl.CostEstimate(flops=10**9, bytes_accessed=2 << 20, transcendentals=0),
        name="far_strips",
    )(z, *waves)


def near_strip_kernel(groups, starts_ref, z_ref, base_ref, steps_ref, tilt_ref, *refs):
    out_refs, (turn_ref, away_ref, starts, sem) = refs[: len(groups)], refs[len(groups) :]
    copy = pltpu.make_async_copy(starts_ref, starts, sem)
    copy.start()
    for gs, out_ref in zip(groups, out_refs):
        strip_sums(gs, columns_of(z_ref), z_ref.shape[-1], base_ref, steps_ref, tilt_ref, out_ref)
    copy.wait()
    rows, _, height = turn_ref.shape
    rows_total = rows * height
    mine = starts[lax.axis_index("frow")]
    for r in range(rows):
        turn_ref[r, 0:1], turn_ref[r, 1:2] = unit(mine * (r * height + lanes(height)), rows_total, 1.0 / math.sqrt(rows_total))
        away_ref[r] = jnp.full((1, 128), mine - starts[r], jnp.int32)


def near_strips(starts, z, waves, groups):
    rows, count, height = starts.shape[0], waves[0].shape[2], z.shape[1] // 2
    return pl.pallas_call(
        functools.partial(near_strip_kernel, groups),
        in_specs=[pl.BlockSpec(memory_space=pl.ANY)] + [VMEM] * 4,
        out_specs=[VMEM] * (len(groups) + 2),
        out_shape=[jax.ShapeDtypeStruct((len(gs), 2, count, height), F32) for gs in groups]
        + [jax.ShapeDtypeStruct((rows, 2, height), F32), jax.ShapeDtypeStruct((rows, 1, 128), jnp.int32)],
        scratch_shapes=[pltpu.SMEM((rows,), jnp.int32), pltpu.SemaphoreType.DMA],
        compiler_params=LIMIT,
        cost_estimate=pl.CostEstimate(flops=4 * 10**9, bytes_accessed=2 << 20, transcendentals=0),
        name="near_strips",
    )(starts, z, *waves)


def pack_kernel(terms, *refs):
    weight_ref, row_ref, live_ref, out_ref = refs[terms:]
    count = refs[0].shape[2]
    strip = sum(ref[0] for ref in refs[:terms])
    out_ref[:count], out_ref[count : 2 * count] = strip[0], strip[1]
    width = out_ref.shape[1]
    weight = weight_ref[0]
    if count < width:
        weight = jnp.concatenate([weight, jnp.zeros((MAXB, width - count), F32)], 1)
    out_ref[2 * count : 2 * count + MAXB] = weight
    row = jnp.where(lanes(MAXB) < live_ref[0:1, 0:1], row_ref[...], -1).astype(F32)
    row = jnp.concatenate([row, jnp.zeros((1, width - MAXB), F32)], 1)
    out_ref[2 * count + MAXB :] = jnp.broadcast_to(row, (META, width))


def pack(terms, weight, row, live, count, height):
    return pl.pallas_call(
        functools.partial(pack_kernel, len(terms)),
        in_specs=[VMEM] * (len(terms) + 3),
        out_specs=VMEM,
        out_shape=jax.ShapeDtypeStruct((2 * count + MAXB + META, height), F32),
        compiler_params=LIMIT,
        name="pack",
    )(*terms, weight, row, live)


class Message:
    def __init__(self, r, message, refs, height, count, rows_total):
        b_ref, roots_ref, turn_ref, away_ref = refs
        own = lax.axis_index("frow")
        strip, rest = message[: 2 * count], message[2 * count :]
        pc, ps = turn_ref[r, 0:1], turn_ref[r, 1:2]
        re, im = strip[:count], strip[count:]
        re, im = re * pc + im * ps, im * pc - re * ps
        high, low = halves(jnp.concatenate([jnp.concatenate([re, im], 1), jnp.concatenate([im, -re], 1)]))
        self.left = jnp.concatenate([high, low, high], 1)

        width = message.shape[1]
        flat = jnp.concatenate([rest, jnp.zeros((width - rest.shape[0], width), F32)])
        turned = jnp.transpose(flat)
        self.weight = jnp.concatenate(halves(turned[:count, :MAXB]), 1)
        row = turned[:MAXB, MAXB : MAXB + 1].astype(jnp.int32)
        self.away = away_ref[r][0:1, 0:1]
        self.place = jnp.where(row < 0, -1, (row - self.away) & (rows_total - 1))
        self.turn = lax.rem(r - own + rows_total // height, rows_total // height)
        self.refs, self.count, self.rows_total = (b_ref, roots_ref), count, rows_total

    def chunk(self, begin, size):
        b_ref, roots_ref = self.refs
        part = lax.dot_general(self.left, b_ref[:, begin : begin + size], NN, preferred_element_type=F32)
        pc, ps = roots_ref[self.turn, 0:1, begin : begin + size], roots_ref[self.turn, 1:2, begin : begin + size]
        re, im = part[: self.count], part[self.count :]
        freq = begin + lanes(size)
        hot = (begin + lanes(size, MAXB) == self.place).astype(F32).astype(BF)
        gain = lax.dot_general(self.weight, jnp.concatenate([hot, hot]), NN, preferred_element_type=F32)
        seen = (((freq + self.away) & (self.rows_total - 1)) < SG).astype(F32)
        return re * pc + im * ps, im * pc - re * ps, gain + seen


def chunks(total, size=256):
    return [(begin, min(size, total - begin)) for begin in range(0, total, size)]


def image_waves(base_ref, steps_ref, tilt_ref, out_ref):
    for g in range(out_ref.shape[0]):
        base = tilted((base_ref[g, 0], base_ref[g, 1]), tilt_ref, 0)
        turn = tilted((steps_ref[g, 0], steps_ref[g, 1]), tilt_ref, 2)
        for begin, size in chunks(out_ref.shape[-1]):
            columns = slice(begin, begin + size)
            out_ref[g, 0, :, columns], out_ref[g, 1, :, columns] = waves_in(base, turn, begin, size)


def last_chunks(total):
    return [(0, total // 2), (total // 2, total // 2)]


def gather_kernel(kind, steps, rows, height, count, *refs):
    tables, refs = refs[:4], refs[4:]
    odd = lax.rem(lax.axis_index("fcol"), 2) == 1
    at = ring_place(lax.axis_index("frow"), rows)

    def add(state_ref, arrived, out_ref, gain_ref=None):
        found = [
            Message(ring_block(at + step, rows), message[...], tables, height, count, rows * height)
            for step, message in arrived
        ]
        for begin, size in chunks(rows * height):
            terms = [message.chunk(begin, size) for message in found]
            if gain_ref is not None and begin < SG:
                gain_ref[:, begin : begin + size] = terms[0][2]
            for i in range(3):
                value = sum(term[i] for term in terms)
                if state_ref is not None:
                    value = value + state_ref[i, :, begin : begin + size]
                out_ref[i, :, begin : begin + size] = value

    if kind == "first":
        add(None, zip(steps, refs), refs[-1])
    elif kind == "plain":
        add(refs[0], zip(steps, refs[1:]), refs[-1])
    elif kind == "own":

        @pl.when(jnp.logical_not(odd))
        def _():
            add(None, zip(steps, refs), refs[-1])

    elif kind == "skip":

        @pl.when(jnp.logical_not(odd))
        def _():
            add(refs[0], zip(steps, refs[1:]), refs[-1])

    elif kind in ("late", "late own"):
        whole = kind == "late own"
        state_ref, before_ref, early, now, waves, (out_ref, made_ref, gain_ref) = (
            refs[0], refs[1], refs[2:4], refs[4:6], refs[6:9], refs[9:]
        )

        @pl.when(jnp.logical_not(odd))
        def _():
            add(state_ref, zip(steps[2:], now), out_ref)

        @pl.when(odd)
        def _():
            if whole:
                add(None, zip((0, *steps), [before_ref, *early, *now]), out_ref, gain_ref)
            else:
                add(before_ref, zip(steps, [*early, *now]), out_ref)
            image_waves(*waves, made_ref)

    else:
        state_ref, now, waves, made_ref, (out_ref, waves_ref) = refs[0], refs[1:3], refs[3:6], refs[6], refs[7:]
        add(state_ref, zip(steps, now), out_ref)

        @pl.when(odd)
        def _():
            waves_ref[...] = made_ref[...]

        @pl.when(jnp.logical_not(odd))
        def _():
            image_waves(*waves, waves_ref)


def gather_step(kind, tables, operands, steps, count, *more):
    height, rows_total = tables[2].shape[2], tables[0].shape[1]
    shapes = [jax.ShapeDtypeStruct((3, count, rows_total), F32), *more]
    out = pl.pallas_call(
        functools.partial(gather_kernel, kind, steps, rows_total // height, height, count),
        in_specs=[VMEM] * (len(tables) + len(operands)),
        out_specs=[VMEM] * len(shapes),
        out_shape=shapes,
        compiler_params=LIMIT,
        cost_estimate=pl.CostEstimate(flops=10**9, bytes_accessed=4 << 20, transcendentals=0),
        name="gather_step",
    )(*tables, *operands)
    return out if more else out[0]


def back_kernel(rows, height, count, *refs):
    tables, (turned_ref, state_ref, message_ref, back_ref, sub_ref) = refs[:4], refs[4:]
    rows_total = rows * height
    own = lax.axis_index("frow")
    r = ring_block(ring_place(own, rows) + rows // 2, rows)
    message = Message(r, message_ref[...], tables, height, count, rows_total)
    acc = None
    for begin, size in chunks(rows_total):
        terms = message.chunk(begin, size)
        re, im, gain = [term + state_ref[i, :, begin : begin + size] for i, term in enumerate(terms)]
        if begin < SG:
            sub_ref[0, :, begin : begin + size] = re
            sub_ref[1, :, begin : begin + size] = im
        high, low = halves(jnp.concatenate([re * gain, im * gain]))
        table = turned_ref[begin : begin + size]
        part = lax.dot_general(high, table, NN, preferred_element_type=F32)
        part = part[:, : 2 * height] + (
            part[:, 2 * height :] + lax.dot_general(low, table[:, : 2 * height], NN, preferred_element_type=F32)
        )
        acc = part if acc is None else acc + part
    re = acc[:count, :height] - acc[count:, height:]
    im = acc[count:, :height] + acc[:count, height:]
    pc, ps = tables[2][own, 0:1], tables[2][own, 1:2]
    back_ref[0] = jnp.transpose(re * pc - im * ps)
    back_ref[1] = jnp.transpose(im * pc + re * ps)


def back_step(tables, turned, state, message, height):
    count, rows_total = state.shape[1:]
    return pl.pallas_call(
        functools.partial(back_kernel, rows_total // height, height, count),
        in_specs=[VMEM] * 7,
        out_specs=[VMEM] * 2,
        out_shape=[
            jax.ShapeDtypeStruct((2, height, count), F32),
            jax.ShapeDtypeStruct((2, count, SG), F32),
        ],
        compiler_params=LIMIT,
        name="back_step",
    )(*tables, turned, state, message)


def correct_kernel(whole, sub_ref, gain_ref, late_ref, roots_ref, out_ref):
    count = sub_ref.shape[1]
    pieces = SG // 128
    own = lax.axis_index("frow")
    pc, ps = roots_ref[own, 0:1, :SG], roots_ref[own, 1:2, :SG]
    re, im, gain = sub_ref[0], sub_ref[1], gain_ref[2, :, :SG]
    if whole:
        gain = jnp.where(lax.rem(lax.axis_index("fcol"), 2) == 1, late_ref[...], gain)
    for part, value in enumerate([(re * pc + im * ps) * gain, (im * pc - re * ps) * gain]):
        for i in range(pieces):
            out_ref[pl.ds(2 * i + part, count, stride=2 * pieces), :] = value[:, 128 * i : 128 * (i + 1)]


def correct_step(whole, sub, first_state, own_gain, roots):
    count = sub.shape[1]
    out = pl.pallas_call(
        functools.partial(correct_kernel, whole),
        in_specs=[VMEM] * 4,
        out_specs=VMEM,
        out_shape=jax.ShapeDtypeStruct((count * 2 * SG // 128, 128), F32),
        compiler_params=LIMIT,
        cost_estimate=pl.CostEstimate(flops=4 * 10**9, bytes_accessed=4 << 20, transcendentals=0),
        name="correct_step",
    )(sub, first_state, own_gain, roots)
    out = out.reshape(count, SG // 128, 2, 128)
    return jnp.transpose(out, (0, 2, 1, 3)).reshape(1, count, 2, SG)


def image_kernel(gs, first, last, e_ref, *refs):
    backs, refs = refs[: len(gs)], refs[len(gs) :]
    acc_ref = None if first else refs[0]
    out_ref = refs[0 if first else 1]
    if last:
        scratch, sems = refs[-2:]
    width = e_ref.shape[-1]
    height = backs[0].shape[1]
    left = []
    for back in backs:
        re, im = back[0], back[1]
        left.append(halves(jnp.concatenate([jnp.concatenate([re, -im], 1), jnp.concatenate([im, re], 1)])))
    copies = []
    for begin, size in (last_chunks(width) if last else chunks(width)):
        columns = slice(begin, begin + size)
        acc = None if first else jnp.concatenate([acc_ref[0, :, columns], acc_ref[1, :, columns]])
        for (high, low), g in zip(left, gs):
            part = dot3((high, low), (e_ref[g, 0, :, columns], e_ref[g, 1, :, columns]), NN)
            acc = part if acc is None else acc + part
        re, im = acc[:height], acc[height:]
        if last:
            scratch[0, :, columns] = re
            scratch[1, :, columns] = im
            copies.append(
                pltpu.make_async_copy(scratch.at[:, :, columns], out_ref.at[:, :, columns], sems.at[len(copies)])
            )
            copies[-1].start()
        else:
            out_ref[0, :, columns] = re
            out_ref[1, :, columns] = im
    for copy in copies:
        copy.wait()


def image_step(table, gs, backs, acc, last):
    width = table.shape[-1]
    height = backs[0].shape[1]
    first = acc is None
    operands = list(backs) + ([] if first else [acc])
    return pl.pallas_call(
        functools.partial(image_kernel, tuple(gs), first, last),
        in_specs=[VMEM] * (1 + len(operands)),
        out_specs=pl.BlockSpec(memory_space=pl.ANY) if last else VMEM,
        out_shape=jax.ShapeDtypeStruct((2, height, width), F32),
        scratch_shapes=[pltpu.VMEM((2, height, width), F32), pltpu.SemaphoreType.DMA((len(last_chunks(width)),))] if last else [],
        compiler_params=LIMIT,
        cost_estimate=pl.CostEstimate(flops=4 * 10**9, bytes_accessed=4 << 20, transcendentals=0),
        name="image_step",
    )(table, *operands)


def swap(value, axis, bit):
    return lax.ppermute(value, axis, [(i, i ^ bit) for i in range(lax.axis_size(axis))])


def per_device(facets, column_start, subgrid_start, vis_count, vis_row, vis_weight):
    rows = lax.axis_size("frow")
    cols = lax.axis_size("fcol")
    height, width = facets.shape[1:]
    rows_total, cols_total = height * rows, width * cols
    count = SG // cols
    assert vis_count.shape[0] == 1 and count <= height

    b_table = wave_table(height, rows_total, rows_total)
    turned = jnp.asarray(b_table.reshape(4 * height, rows_total).T.copy())
    b_table = jnp.asarray(np.concatenate([b_table[:2], b_table]).reshape(6 * height, rows_total))
    angle = np.arange(rows)[:, None] * np.arange(rows_total)[None, :] % rows * (2.0 * np.pi / rows)
    roots = jnp.asarray(np.stack([np.cos(angle), np.sin(angle)], 1).astype(np.float32))

    top = cols // 2
    column_start = column_start.reshape(1, 1)
    waves = waves_of(count, width, cols_total)
    sent, z, tilt = first_strips(column_start, facets, waves, range(top + 1, cols, 2))
    waves = *waves, tilt
    far = far_strips(z, waves, range(top, cols, 2)) + swap(sent, "fcol", 1)
    far, z = lax.optimization_barrier((far, z))
    sent, near, *turns = near_strips(subgrid_start, z, waves, [tuple(range(1, top, 2)), tuple(range(0, top, 2))])
    terms = [near + swap(far, "fcol", top), swap(sent, "fcol", 1)]
    bit = 2
    while bit < top:
        pairs = sum(terms).reshape((-1, 2) + far.shape[1:])
        terms = [pairs[:, 0], swap(pairs[:, 1], "fcol", bit)]
        bit *= 2

    own = pack(terms, vis_weight, vis_row, vis_count.reshape(1, 1), count, height)
    tables = b_table, roots, *turns
    order = list(range(0, rows, 2)) + list(range(rows - 1, 0, -2))
    ahead = [(order[i], order[(i + 1) % rows]) for i in range(rows)]
    behind = [(b, a) for a, b in ahead]
    last = rows // 2 - 1
    assert last >= 3
    whole = last == 3
    first_state = state = gather_step("own" if whole else "first", tables, [own], (0,), count)
    made = jax.ShapeDtypeStruct((cols, 2, 2 * count, width), BF)
    up = down = own
    for step in range(1, last + 1):
        up = lax.ppermute(up, "frow", ahead)
        down = lax.ppermute(down, "frow", behind)
        up, state = lax.optimization_barrier((up, state))
        if step == last - 2:
            before, early = state, [up, down]
            state = gather_step("skip", tables, [state, up, down], (-step, step), count)
        elif step == last - 1:
            steps = (1 - step, step - 1, -step, step)
            operands = [state, own if whole else before, *early, up, down, *waves]
            own_gain = jax.ShapeDtypeStruct((count, SG), F32)
            kind = "late own" if whole else "late"
            state, image_table, own_gain = gather_step(kind, tables, operands, steps, count, made, own_gain)
        elif step == last:
            operands = [state, up, down, *waves, image_table]
            state, image_table = gather_step("last", tables, operands, (-step, step), count, made)
        else:
            state = gather_step("plain", tables, [state, up, down], (-step, step), count)
    up = lax.ppermute(up, "frow", ahead)
    back, sub = back_step(tables, turned, state, up, height)

    near, far = {0: back}, {top: swap(back, "fcol", top)}

    def spread(blocks, bit):
        return {g ^ bit: swap(b, "fcol", bit) for g, b in blocks.items()}

    def image(blocks, acc, last=False):
        return image_step(image_table, blocks.keys(), list(blocks.values()), acc, last)

    acc = image(near, None)
    near[0], acc = lax.optimization_barrier((back, acc))
    bit = top // 2
    while bit >= 1:
        near |= spread(near, bit)
        bit //= 2
    del near[0]
    acc = image(near, acc)
    corrected = correct_step(whole, sub, first_state, own_gain, roots)
    far[top], acc, corrected = lax.optimization_barrier((far[top], acc, corrected))
    bit = top // 2
    while bit > 1:
        far |= spread(far, bit)
        bit //= 2
    rest = spread(far, 1)
    acc = image(far, acc)
    return corrected, image(rest, acc, last=True)


def solution(mesh):
    return jax.shard_map(
        per_device,
        mesh=mesh,
        in_specs=(
            P(None, "frow", "fcol"),
            P(),
            P(),
            P("frow"),
            P("frow", None),
            P("frow", None, "fcol"),
        ),
        out_specs=(P("frow", "fcol", None, None), P(None, "frow", "fcol")),
        check_vma=False,
    )
```

```python
import functools
import math

import jax
import jax.numpy as jnp
import ml_dtypes
import numpy as np
from jax import lax
from jax.experimental import pallas as pl
from jax.experimental.pallas import tpu as pltpu
from jax.sharding import PartitionSpec as P

SG = 512
MAXB = 64
META = 8

BF = jnp.bfloat16
F32 = jnp.float32
NN = (((1,), (0,)), ((), ()))
NT = (((1,), (1,)), ((), ()))
VMEM = pl.BlockSpec(memory_space=pltpu.VMEM)
SMEM = pl.BlockSpec(memory_space=pltpu.SMEM)
LIMIT = pltpu.CompilerParams(vmem_limit_bytes=20 << 20)


def halves(value):
    high = value.astype(BF)
    return high, (value - high.astype(F32)).astype(BF)


def dot3(left, right, dims):
    def dot(a, b):
        return lax.dot_general(a, b, dims, preferred_element_type=F32)
    return dot(left[0], right[0]) + (dot(left[0], right[1]) + dot(left[1], right[0]))


def unit(phase, modulus, scale=1.0):
    angle = (phase & (modulus - 1)).astype(F32) * F32(2.0 * math.pi / modulus)
    return jnp.cos(angle) * F32(scale), jnp.sin(angle) * F32(scale)


def lanes(count, rows=1):
    return lax.broadcasted_iota(jnp.int32, (rows, count), 1)


def wave_parts(rows, stride, cols, modulus):
    phase = np.arange(rows, dtype=np.int64)[:, None] * (stride * np.arange(cols, dtype=np.int64))[None, :] % modulus
    angle = phase * (2.0 * np.pi / modulus)
    return np.stack([np.cos(angle), np.sin(angle)])


def wave_table(rows, cols, modulus):
    parts = wave_parts(rows, 1, cols, modulus)
    high = parts.astype(ml_dtypes.bfloat16)
    low = (parts - high.astype(np.float64)).astype(ml_dtypes.bfloat16)
    return np.concatenate([high, low])


def ring_place(r, rows):
    return jnp.where(lax.rem(r, 2) == 0, r // 2, rows - 1 - r // 2)


def ring_block(place, rows):
    place = lax.rem(place + rows, rows)
    return jnp.where(place < rows // 2, 2 * place, 2 * (rows - 1 - place) + 1)


def wave_kernel(width, cols_total, base_ref, steps_ref):
    own = lax.axis_index("fcol")
    blocks, _, count, _ = base_ref.shape
    down = lax.broadcasted_iota(jnp.int32, (count, 128), 0)
    cos, sin = unit(down * lanes(128), cols_total)
    tiles = width // 128
    every = own * width + 128 * lax.broadcasted_iota(jnp.int32, (tiles, 128), 0)
    for g in range(blocks):
        first = (own ^ g) * count
        pc, ps = unit(first * lanes(128), cols_total)
        base_ref[g, 0] = cos * pc - sin * ps
        base_ref[g, 1] = sin * pc + cos * ps
        for part, value in enumerate(unit((first + lanes(128, tiles)) * every, cols_total)):
            steps_ref[g, part, :, :tiles] = jnp.transpose(value)[:count]


def waves_of(count, width, cols_total):
    shape = jax.ShapeDtypeStruct((SG // count, 2, count, 128), F32)
    return pl.pallas_call(
        functools.partial(wave_kernel, width, cols_total),
        out_specs=[VMEM] * 2,
        out_shape=[shape] * 2,
        compiler_params=LIMIT,
        cost_estimate=pl.CostEstimate(flops=10**9, bytes_accessed=2 << 20, transcendentals=0),
        name="waves",
    )()


def waves_in(base, turn, begin, size):
    cos, sin = [], []
    for t in range(begin // 128, (begin + size) // 128):
        tc, ts = turn[0][:, t : t + 1], turn[1][:, t : t + 1]
        cos.append(tc * base[0] - ts * base[1])
        sin.append(ts * base[0] + tc * base[1])
    return halves(jnp.concatenate([jnp.concatenate(cos, 1), jnp.concatenate(sin, 1)]))


def tilted(waves, tilt_ref, row):
    (cos, sin), (pc, ps) = waves, (tilt_ref[row : row + 1], tilt_ref[row + 1 : row + 2])
    return cos * pc - sin * ps, sin * pc + cos * ps


def strip_sums(gs, z_of, width, base_ref, steps_ref, tilt_ref, out_ref):
    count, height = out_ref.shape[-2:]
    for i, g in enumerate(gs):
        base = tilted((base_ref[g, 0], base_ref[g, 1]), tilt_ref, 0)
        turn = tilted((steps_ref[g, 0], steps_ref[g, 1]), tilt_ref, 2)
        acc = None
        for begin, size in chunks(width):
            part = dot3(waves_in(base, turn, begin, size), z_of(begin, size), NT)
            acc = part if acc is None else acc + part
        cos, sin = acc[:count], acc[count:]
        out_ref[i, 0] = cos[:, :height] + sin[:, height:]
        out_ref[i, 1] = cos[:, height:] - sin[:, :height]


def first_strip_kernel(gs, cols_total, start_ref, x_ref, base_ref, steps_ref, out_ref, z_ref, tilt_ref):
    start, begin = start_ref[0:1, 0:1], lax.axis_index("fcol") * x_ref.shape[-1]
    tilt_ref[0:1], tilt_ref[1:2] = unit(start * lanes(128), cols_total)
    tilt_ref[2:3], tilt_ref[3:4] = unit(start * (begin + 128 * lanes(128)), cols_total, 1.0 / math.sqrt(cols_total))
    made = {}

    def z_of(begin, size):
        if begin not in made:
            columns = slice(begin, begin + size)
            made[begin] = halves(jnp.concatenate([x_ref[0, :, columns], x_ref[1, :, columns]]))
            z_ref[0, :, columns], z_ref[1, :, columns] = made[begin]
        return made[begin]

    strip_sums(gs, z_of, x_ref.shape[-1], base_ref, steps_ref, tilt_ref, out_ref)


def first_strips(column_start, facets, waves, gs):
    cols, _, count, _ = waves[0].shape
    _, height, width = facets.shape
    return pl.pallas_call(
        functools.partial(first_strip_kernel, tuple(gs), cols * width),
        in_specs=[VMEM] * 4,
        out_specs=[VMEM] * 3,
        out_shape=[
            jax.ShapeDtypeStruct((len(gs), 2, count, height), F32),
            jax.ShapeDtypeStruct((2, 2 * height, width), BF),
            jax.ShapeDtypeStruct((4, 128), F32),
        ],
        compiler_params=LIMIT,
        cost_estimate=pl.CostEstimate(flops=10**9, bytes_accessed=2 << 20, transcendentals=0),
        name="first_strips",
    )(column_start, facets, *waves)


def columns_of(z_ref):
    return lambda begin, size: (z_ref[0, :, begin : begin + size], z_ref[1, :, begin : begin + size])


def far_strip_kernel(gs, z_ref, base_ref, steps_ref, tilt_ref, out_ref):
    strip_sums(gs, columns_of(z_ref), z_ref.shape[-1], base_ref, steps_ref, tilt_ref, out_ref)


def far_strips(z, waves, gs):
    return pl.pallas_call(
        functools.partial(far_strip_kernel, tuple(gs)),
        in_specs=[VMEM] * 4,
        out_specs=VMEM,
        out_shape=jax.ShapeDtypeStruct((len(gs), 2, waves[0].shape[2], z.shape[1] // 2), F32),
        compiler_params=LIMIT,
        cost_estimate=pl.CostEstimate(flops=10**9, bytes_accessed=2 << 20, transcendentals=0),
        name="far_strips",
    )(z, *waves)


def near_strip_kernel(groups, starts_ref, z_ref, base_ref, steps_ref, tilt_ref, *refs):
    out_refs, (turn_ref, away_ref, starts, sem) = refs[: len(groups)], refs[len(groups) :]
    copy = pltpu.make_async_copy(starts_ref, starts, sem)
    copy.start()
    for gs, out_ref in zip(groups, out_refs):
        strip_sums(gs, columns_of(z_ref), z_ref.shape[-1], base_ref, steps_ref, tilt_ref, out_ref)
    copy.wait()
    rows, _, height = turn_ref.shape
    rows_total = rows * height
    mine = starts[lax.axis_index("frow")]
    for r in range(rows):
        turn_ref[r, 0:1], turn_ref[r, 1:2] = unit(mine * (r * height + lanes(height)), rows_total, 1.0 / math.sqrt(rows_total))
        away_ref[r] = jnp.full((1, 128), mine - starts[r], jnp.int32)


def near_strips(starts, z, waves, groups):
    rows, count, height = starts.shape[0], waves[0].shape[2], z.shape[1] // 2
    return pl.pallas_call(
        functools.partial(near_strip_kernel, groups),
        in_specs=[pl.BlockSpec(memory_space=pl.ANY)] + [VMEM] * 4,
        out_specs=[VMEM] * (len(groups) + 2),
        out_shape=[jax.ShapeDtypeStruct((len(gs), 2, count, height), F32) for gs in groups]
        + [jax.ShapeDtypeStruct((rows, 2, height), F32), jax.ShapeDtypeStruct((rows, 1, 128), jnp.int32)],
        scratch_shapes=[pltpu.SMEM((rows,), jnp.int32), pltpu.SemaphoreType.DMA],
        compiler_params=LIMIT,
        cost_estimate=pl.CostEstimate(flops=4 * 10**9, bytes_accessed=2 << 20, transcendentals=0),
        name="near_strips",
    )(starts, z, *waves)


def pack_kernel(terms, *refs):
    weight_ref, row_ref, live_ref, out_ref = refs[terms:]
    count = refs[0].shape[2]
    strip = sum(ref[0] for ref in refs[:terms])
    out_ref[:count], out_ref[count : 2 * count] = strip[0], strip[1]
    width = out_ref.shape[1]
    weight = weight_ref[0]
    if count < width:
        weight = jnp.concatenate([weight, jnp.zeros((MAXB, width - count), F32)], 1)
    out_ref[2 * count : 2 * count + MAXB] = weight
    row = jnp.where(lanes(MAXB) < live_ref[0:1, 0:1], row_ref[...], -1).astype(F32)
    row = jnp.concatenate([row, jnp.zeros((1, width - MAXB), F32)], 1)
    out_ref[2 * count + MAXB :] = jnp.broadcast_to(row, (META, width))


def pack(terms, weight, row, live, count, height):
    return pl.pallas_call(
        functools.partial(pack_kernel, len(terms)),
        in_specs=[VMEM] * (len(terms) + 3),
        out_specs=VMEM,
        out_shape=jax.ShapeDtypeStruct((2 * count + MAXB + META, height), F32),
        compiler_params=LIMIT,
        name="pack",
    )(*terms, weight, row, live)


class Message:
    def __init__(self, r, message, refs, height, count, rows_total):
        b_ref, roots_ref, turn_ref, away_ref = refs
        own = lax.axis_index("frow")
        strip, rest = message[: 2 * count], message[2 * count :]
        pc, ps = turn_ref[r, 0:1], turn_ref[r, 1:2]
        re, im = strip[:count], strip[count:]
        re, im = re * pc + im * ps, im * pc - re * ps
        high, low = halves(jnp.concatenate([jnp.concatenate([re, im], 1), jnp.concatenate([im, -re], 1)]))
        self.left = jnp.concatenate([high, low, high], 1)

        width = message.shape[1]
        flat = jnp.concatenate([rest, jnp.zeros((width - rest.shape[0], width), F32)])
        turned = jnp.transpose(flat)
        self.weight = jnp.concatenate(halves(turned[:count, :MAXB]), 1)
        row = turned[:MAXB, MAXB : MAXB + 1].astype(jnp.int32)
        self.away = away_ref[r][0:1, 0:1]
        self.place = jnp.where(row < 0, -1, (row - self.away) & (rows_total - 1))
        self.turn = lax.rem(r - own + rows_total // height, rows_total // height)
        self.refs, self.count, self.rows_total = (b_ref, roots_ref), count, rows_total

    def chunk(self, begin, size):
        b_ref, roots_ref = self.refs
        part = lax.dot_general(self.left, b_ref[:, begin : begin + size], NN, preferred_element_type=F32)
        pc, ps = roots_ref[self.turn, 0:1, begin : begin + size], roots_ref[self.turn, 1:2, begin : begin + size]
        re, im = part[: self.count], part[self.count :]
        freq = begin + lanes(size)
        hot = (begin + lanes(size, MAXB) == self.place).astype(F32).astype(BF)
        gain = lax.dot_general(self.weight, jnp.concatenate([hot, hot]), NN, preferred_element_type=F32)
        seen = (((freq + self.away) & (self.rows_total - 1)) < SG).astype(F32)
        return re * pc + im * ps, im * pc - re * ps, gain + seen


def chunks(total, size=256):
    return [(begin, min(size, total - begin)) for begin in range(0, total, size)]


def image_waves(base_ref, steps_ref, tilt_ref, out_ref):
    for g in range(out_ref.shape[0]):
        base = tilted((base_ref[g, 0], base_ref[g, 1]), tilt_ref, 0)
        turn = tilted((steps_ref[g, 0], steps_ref[g, 1]), tilt_ref, 2)
        for begin, size in chunks(out_ref.shape[-1]):
            columns = slice(begin, begin + size)
            out_ref[g, 0, :, columns], out_ref[g, 1, :, columns] = waves_in(base, turn, begin, size)


def last_chunks(total):
    return [(0, total // 2), (total // 2, total // 2)]


def gather_kernel(kind, steps, rows, height, count, *refs):
    tables, refs = refs[:4], refs[4:]
    odd = lax.rem(lax.axis_index("fcol"), 2) == 1
    at = ring_place(lax.axis_index("frow"), rows)

    def add(state_ref, arrived, out_ref, gain_ref=None):
        found = [
            Message(ring_block(at + step, rows), message[...], tables, height, count, rows * height)
            for step, message in arrived
        ]
        for begin, size in chunks(rows * height):
            terms = [message.chunk(begin, size) for message in found]
            if gain_ref is not None and begin < SG:
                gain_ref[:, begin : begin + size] = terms[0][2]
            for i in range(3):
                value = sum(term[i] for term in terms)
                if state_ref is not None:
                    value = value + state_ref[i, :, begin : begin + size]
                out_ref[i, :, begin : begin + size] = value

    if kind == "first":
        add(None, zip(steps, refs), refs[-1])
    elif kind == "plain":
        add(refs[0], zip(steps, refs[1:]), refs[-1])
    elif kind == "own":

        @pl.when(jnp.logical_not(odd))
        def _():
            add(None, zip(steps, refs), refs[-1])

    elif kind == "skip":

        @pl.when(jnp.logical_not(odd))
        def _():
            add(refs[0], zip(steps, refs[1:]), refs[-1])

    elif kind in ("late", "late own"):
        whole = kind == "late own"
        state_ref, before_ref, early, now, waves, (out_ref, made_ref, gain_ref) = (
            refs[0], refs[1], refs[2:4], refs[4:6], refs[6:9], refs[9:]
        )

        @pl.when(jnp.logical_not(odd))
        def _():
            add(state_ref, zip(steps[2:], now), out_ref)

        @pl.when(odd)
        def _():
            if whole:
                add(None, zip((0, *steps), [before_ref, *early, *now]), out_ref, gain_ref)
            else:
                add(before_ref, zip(steps, [*early, *now]), out_ref)
            image_waves(*waves, made_ref)

    else:
        state_ref, now, waves, made_ref, (out_ref, waves_ref) = refs[0], refs[1:3], refs[3:6], refs[6], refs[7:]
        add(state_ref, zip(steps, now), out_ref)

        @pl.when(odd)
        def _():
            waves_ref[...] = made_ref[...]

        @pl.when(jnp.logical_not(odd))
        def _():
            image_waves(*waves, waves_ref)


def gather_step(kind, tables, operands, steps, count, *more):
    height, rows_total = tables[2].shape[2], tables[0].shape[1]
    shapes = [jax.ShapeDtypeStruct((3, count, rows_total), F32), *more]
    out = pl.pallas_call(
        functools.partial(gather_kernel, kind, steps, rows_total // height, height, count),
        in_specs=[VMEM] * (len(tables) + len(operands)),
        out_specs=[VMEM] * len(shapes),
        out_shape=shapes,
        compiler_params=LIMIT,
        cost_estimate=pl.CostEstimate(flops=10**9, bytes_accessed=4 << 20, transcendentals=0),
        name="gather_step",
    )(*tables, *operands)
    return out if more else out[0]


def back_kernel(rows, height, count, *refs):
    tables, (turned_ref, state_ref, message_ref, back_ref, sub_ref) = refs[:4], refs[4:]
    rows_total = rows * height
    own = lax.axis_index("frow")
    r = ring_block(ring_place(own, rows) + rows // 2, rows)
    message = Message(r, message_ref[...], tables, height, count, rows_total)
    acc = None
    for begin, size in chunks(rows_total):
        terms = message.chunk(begin, size)
        re, im, gain = [term + state_ref[i, :, begin : begin + size] for i, term in enumerate(terms)]
        if begin < SG:
            sub_ref[0, :, begin : begin + size] = re
            sub_ref[1, :, begin : begin + size] = im
        high, low = halves(jnp.concatenate([re * gain, im * gain]))
        table = turned_ref[begin : begin + size]
        part = lax.dot_general(high, table, NN, preferred_element_type=F32)
        part = part[:, : 2 * height] + (
            part[:, 2 * height :] + lax.dot_general(low, table[:, : 2 * height], NN, preferred_element_type=F32)
        )
        acc = part if acc is None else acc + part
    re = acc[:count, :height] - acc[count:, height:]
    im = acc[count:, :height] + acc[:count, height:]
    pc, ps = tables[2][own, 0:1], tables[2][own, 1:2]
    back_ref[0] = jnp.transpose(re * pc - im * ps)
    back_ref[1] = jnp.transpose(im * pc + re * ps)


def back_step(tables, turned, state, message, height):
    count, rows_total = state.shape[1:]
    return pl.pallas_call(
        functools.partial(back_kernel, rows_total // height, height, count),
        in_specs=[VMEM] * 7,
        out_specs=[VMEM] * 2,
        out_shape=[
            jax.ShapeDtypeStruct((2, height, count), F32),
            jax.ShapeDtypeStruct((2, count, SG), F32),
        ],
        compiler_params=LIMIT,
        name="back_step",
    )(*tables, turned, state, message)


def correct_kernel(whole, sub_ref, gain_ref, late_ref, roots_ref, out_ref):
    count = sub_ref.shape[1]
    pieces = SG // 128
    own = lax.axis_index("frow")
    pc, ps = roots_ref[own, 0:1, :SG], roots_ref[own, 1:2, :SG]
    re, im, gain = sub_ref[0], sub_ref[1], gain_ref[2, :, :SG]
    if whole:
        gain = jnp.where(lax.rem(lax.axis_index("fcol"), 2) == 1, late_ref[...], gain)
    for part, value in enumerate([(re * pc + im * ps) * gain, (im * pc - re * ps) * gain]):
        for i in range(pieces):
            out_ref[pl.ds(2 * i + part, count, stride=2 * pieces), :] = value[:, 128 * i : 128 * (i + 1)]


def correct_step(whole, sub, first_state, own_gain, roots):
    count = sub.shape[1]
    out = pl.pallas_call(
        functools.partial(correct_kernel, whole),
        in_specs=[VMEM] * 4,
        out_specs=VMEM,
        out_shape=jax.ShapeDtypeStruct((count * 2 * SG // 128, 128), F32),
        compiler_params=LIMIT,
        cost_estimate=pl.CostEstimate(flops=4 * 10**9, bytes_accessed=4 << 20, transcendentals=0),
        name="correct_step",
    )(sub, first_state, own_gain, roots)
    out = out.reshape(count, SG // 128, 2, 128)
    return jnp.transpose(out, (0, 2, 1, 3)).reshape(1, count, 2, SG)


def image_kernel(gs, first, last, e_ref, *refs):
    backs, refs = refs[: len(gs)], refs[len(gs) :]
    acc_ref = None if first else refs[0]
    out_ref = refs[0 if first else 1]
    if last:
        scratch, sems = refs[-2:]
    width = e_ref.shape[-1]
    height = backs[0].shape[1]
    left = []
    for back in backs:
        re, im = back[0], back[1]
        left.append(halves(jnp.concatenate([jnp.concatenate([re, -im], 1), jnp.concatenate([im, re], 1)])))
    copies = []
    for begin, size in (last_chunks(width) if last else chunks(width)):
        columns = slice(begin, begin + size)
        acc = None if first else jnp.concatenate([acc_ref[0, :, columns], acc_ref[1, :, columns]])
        for (high, low), g in zip(left, gs):
            part = dot3((high, low), (e_ref[g, 0, :, columns], e_ref[g, 1, :, columns]), NN)
            acc = part if acc is None else acc + part
        re, im = acc[:height], acc[height:]
        if last:
            scratch[0, :, columns] = re
            scratch[1, :, columns] = im
            copies.append(
                pltpu.make_async_copy(scratch.at[:, :, columns], out_ref.at[:, :, columns], sems.at[len(copies)])
            )
            copies[-1].start()
        else:
            out_ref[0, :, columns] = re
            out_ref[1, :, columns] = im
    for copy in copies:
        copy.wait()


def image_step(table, gs, backs, acc, last):
    width = table.shape[-1]
    height = backs[0].shape[1]
    first = acc is None
    operands = list(backs) + ([] if first else [acc])
    return pl.pallas_call(
        functools.partial(image_kernel, tuple(gs), first, last),
        in_specs=[VMEM] * (1 + len(operands)),
        out_specs=pl.BlockSpec(memory_space=pl.ANY) if last else VMEM,
        out_shape=jax.ShapeDtypeStruct((2, height, width), F32),
        scratch_shapes=[pltpu.VMEM((2, height, width), F32), pltpu.SemaphoreType.DMA((len(last_chunks(width)),))] if last else [],
        compiler_params=LIMIT,
        cost_estimate=pl.CostEstimate(flops=4 * 10**9, bytes_accessed=4 << 20, transcendentals=0),
        name="image_step",
    )(table, *operands)


def swap(value, axis, bit):
    return lax.ppermute(value, axis, [(i, i ^ bit) for i in range(lax.axis_size(axis))])


def per_device(facets, column_start, subgrid_start, vis_count, vis_row, vis_weight):
    rows = lax.axis_size("frow")
    cols = lax.axis_size("fcol")
    height, width = facets.shape[1:]
    rows_total, cols_total = height * rows, width * cols
    count = SG // cols
    assert vis_count.shape[0] == 1 and count <= height

    b_table = wave_table(height, rows_total, rows_total)
    turned = jnp.asarray(b_table.reshape(4 * height, rows_total).T.copy())
    b_table = jnp.asarray(np.concatenate([b_table[:2], b_table]).reshape(6 * height, rows_total))
    angle = np.arange(rows)[:, None] * np.arange(rows_total)[None, :] % rows * (2.0 * np.pi / rows)
    roots = jnp.asarray(np.stack([np.cos(angle), np.sin(angle)], 1).astype(np.float32))

    top = cols // 2
    column_start = column_start.reshape(1, 1)
    waves = waves_of(count, width, cols_total)
    sent, z, tilt = first_strips(column_start, facets, waves, range(top + 1, cols, 2))
    waves = *waves, tilt
    far = far_strips(z, waves, range(top, cols, 2)) + swap(sent, "fcol", 1)
    far, z = lax.optimization_barrier((far, z))
    sent, near, *turns = near_strips(subgrid_start, z, waves, [tuple(range(1, top, 2)), tuple(range(0, top, 2))])
    terms = [near + swap(far, "fcol", top), swap(sent, "fcol", 1)]
    bit = 2
    while bit < top:
        pairs = sum(terms).reshape((-1, 2) + far.shape[1:])
        terms = [pairs[:, 0], swap(pairs[:, 1], "fcol", bit)]
        bit *= 2

    own = pack(terms, vis_weight, vis_row, vis_count.reshape(1, 1), count, height)
    tables = b_table, roots, *turns
    order = list(range(0, rows, 2)) + list(range(rows - 1, 0, -2))
    ahead = [(order[i], order[(i + 1) % rows]) for i in range(rows)]
    behind = [(b, a) for a, b in ahead]
    last = rows // 2 - 1
    assert last >= 3
    whole = last == 3
    first_state = state = gather_step("own" if whole else "first", tables, [own], (0,), count)
    made = jax.ShapeDtypeStruct((cols, 2, 2 * count, width), BF)
    up = down = own
    for step in range(1, last + 1):
        up = lax.ppermute(up, "frow", ahead)
        down = lax.ppermute(down, "frow", behind)
        up, state = lax.optimization_barrier((up, state))
        if step == last - 2:
            before, early = state, [up, down]
            state = gather_step("skip", tables, [state, up, down], (-step, step), count)
        elif step == last - 1:
            steps = (1 - step, step - 1, -step, step)
            operands = [state, own if whole else before, *early, up, down, *waves]
            own_gain = jax.ShapeDtypeStruct((count, SG), F32)
            kind = "late own" if whole else "late"
            state, image_table, own_gain = gather_step(kind, tables, operands, steps, count, made, own_gain)
        elif step == last:
            operands = [state, up, down, *waves, image_table]
            state, image_table = gather_step("last", tables, operands, (-step, step), count, made)
        else:
            state = gather_step("plain", tables, [state, up, down], (-step, step), count)
    up = lax.ppermute(up, "frow", ahead)
    back, sub = back_step(tables, turned, state, up, height)

    near, far = {0: back}, {top: swap(back, "fcol", top)}

    def spread(blocks, bit):
        return {g ^ bit: swap(b, "fcol", bit) for g, b in blocks.items()}

    def image(blocks, acc, last=False):
        return image_step(image_table, blocks.keys(), list(blocks.values()), acc, last)

    acc = image(near, None)
    near[0], acc = lax.optimization_barrier((back, acc))
    bit = top // 2
    while bit >= 1:
        near |= spread(near, bit)
        bit //= 2
    del near[0]
    acc = image(near, acc)
    corrected = correct_step(whole, sub, first_state, own_gain, roots)
    far[top], acc, corrected = lax.optimization_barrier((far[top], acc, corrected))
    bit = top // 2
    while bit > 1:
        far |= spread(far, bit)
        bit //= 2
    rest = spread(far, 1)
    acc = image(far, acc)
    return corrected, image(rest, acc, last=True)


def solution(mesh):
    return jax.shard_map(
        per_device,
        mesh=mesh,
        in_specs=(
            P(None, "frow", "fcol"),
            P(),
            P(),
            P("frow"),
            P("frow", None),
            P("frow", None, "fcol"),
        ),
        out_specs=(P("frow", "fcol", None, None), P(None, "frow", "fcol")),
        check_vma=False,
    )
```

```python
import functools
import math

import jax
import jax.numpy as jnp
import ml_dtypes
import numpy as np
from jax import lax
from jax.experimental import pallas as pl
from jax.experimental.pallas import tpu as pltpu
from jax.sharding import PartitionSpec as P

SG = 512
MAXB = 64
META = 8

BF = jnp.bfloat16
F32 = jnp.float32
NN = (((1,), (0,)), ((), ()))
NT = (((1,), (1,)), ((), ()))
VMEM = pl.BlockSpec(memory_space=pltpu.VMEM)
SMEM = pl.BlockSpec(memory_space=pltpu.SMEM)
LIMIT = pltpu.CompilerParams(vmem_limit_bytes=32 << 20)


def halves(value):
    high = value.astype(BF)
    return high, (value - high.astype(F32)).astype(BF)


def dot3(left, right, dims):
    def dot(a, b):
        return lax.dot_general(a, b, dims, preferred_element_type=F32)
    return dot(left[0], right[0]) + (dot(left[0], right[1]) + dot(left[1], right[0]))


def unit(phase, modulus, scale=1.0):
    angle = (phase & (modulus - 1)).astype(F32) * F32(2.0 * math.pi / modulus)
    return jnp.cos(angle) * F32(scale), jnp.sin(angle) * F32(scale)


def lanes(count, rows=1):
    return lax.broadcasted_iota(jnp.int32, (rows, count), 1)


def wave_parts(rows, stride, cols, modulus):
    phase = np.arange(rows, dtype=np.int64)[:, None] * (stride * np.arange(cols, dtype=np.int64))[None, :] % modulus
    angle = phase * (2.0 * np.pi / modulus)
    return np.stack([np.cos(angle), np.sin(angle)])


def wave_table(rows, cols, modulus):
    parts = wave_parts(rows, 1, cols, modulus)
    high = parts.astype(ml_dtypes.bfloat16)
    low = (parts - high.astype(np.float64)).astype(ml_dtypes.bfloat16)
    return np.concatenate([high, low])


def ring_place(r, rows):
    return jnp.where(lax.rem(r, 2) == 0, r // 2, rows - 1 - r // 2)


def ring_block(place, rows):
    place = lax.rem(place + rows, rows)
    return jnp.where(place < rows // 2, 2 * place, 2 * (rows - 1 - place) + 1)


def wave_kernel(width, cols_total, base_ref, steps_ref):
    own = lax.axis_index("fcol")
    blocks, _, count, _ = base_ref.shape
    down = lax.broadcasted_iota(jnp.int32, (count, 128), 0)
    cos, sin = unit(down * lanes(128), cols_total)
    tiles = width // 128
    every = own * width + 128 * lax.broadcasted_iota(jnp.int32, (tiles, 128), 0)
    for g in range(blocks):
        first = (own ^ g) * count
        pc, ps = unit(first * lanes(128), cols_total)
        base_ref[g, 0] = cos * pc - sin * ps
        base_ref[g, 1] = sin * pc + cos * ps
        for part, value in enumerate(unit((first + lanes(128, tiles)) * every, cols_total)):
            steps_ref[g, part, :, :tiles] = jnp.transpose(value)[:count]


def waves_of(count, width, cols_total):
    shape = jax.ShapeDtypeStruct((SG // count, 2, count, 128), F32)
    return pl.pallas_call(
        functools.partial(wave_kernel, width, cols_total),
        out_specs=[VMEM] * 2,
        out_shape=[shape] * 2,
        compiler_params=LIMIT,
        cost_estimate=pl.CostEstimate(flops=10**9, bytes_accessed=2 << 20, transcendentals=0),
        name="waves",
    )()


def waves_in(base, turn, begin, size):
    cos, sin = [], []
    for t in range(begin // 128, (begin + size) // 128):
        tc, ts = turn[0][:, t : t + 1], turn[1][:, t : t + 1]
        cos.append(tc * base[0] - ts * base[1])
        sin.append(ts * base[0] + tc * base[1])
    return halves(jnp.concatenate([jnp.concatenate(cos, 1), jnp.concatenate(sin, 1)]))


def tilted(waves, tilt_ref, row):
    (cos, sin), (pc, ps) = waves, (tilt_ref[row : row + 1], tilt_ref[row + 1 : row + 2])
    return cos * pc - sin * ps, sin * pc + cos * ps


def strip_sums(gs, z_of, width, base_ref, steps_ref, tilt_ref, out_ref):
    count, height = out_ref.shape[-2:]
    for i, g in enumerate(gs):
        base = tilted((base_ref[g, 0], base_ref[g, 1]), tilt_ref, 0)
        turn = tilted((steps_ref[g, 0], steps_ref[g, 1]), tilt_ref, 2)
        acc = None
        for begin, size in chunks(width):
            part = dot3(waves_in(base, turn, begin, size), z_of(begin, size), NT)
            acc = part if acc is None else acc + part
        cos, sin = acc[:count], acc[count:]
        out_ref[i, 0] = cos[:, :height] + sin[:, height:]
        out_ref[i, 1] = cos[:, height:] - sin[:, :height]


def first_strip_kernel(gs, cols_total, start_ref, x_ref, base_ref, steps_ref, out_ref, z_ref, tilt_ref):
    start, begin = start_ref[0:1, 0:1], lax.axis_index("fcol") * x_ref.shape[-1]
    tilt_ref[0:1], tilt_ref[1:2] = unit(start * lanes(128), cols_total)
    tilt_ref[2:3], tilt_ref[3:4] = unit(start * (begin + 128 * lanes(128)), cols_total, 1.0 / math.sqrt(cols_total))
    made = {}

    def z_of(begin, size):
        if begin not in made:
            columns = slice(begin, begin + size)
            made[begin] = halves(jnp.concatenate([x_ref[0, :, columns], x_ref[1, :, columns]]))
            z_ref[0, :, columns], z_ref[1, :, columns] = made[begin]
        return made[begin]

    strip_sums(gs, z_of, x_ref.shape[-1], base_ref, steps_ref, tilt_ref, out_ref)


def first_strips(column_start, facets, waves, gs):
    cols, _, count, _ = waves[0].shape
    _, height, width = facets.shape
    return pl.pallas_call(
        functools.partial(first_strip_kernel, tuple(gs), cols * width),
        in_specs=[VMEM] * 4,
        out_specs=[VMEM] * 3,
        out_shape=[
            jax.ShapeDtypeStruct((len(gs), 2, count, height), F32),
            jax.ShapeDtypeStruct((2, 2 * height, width), BF),
            jax.ShapeDtypeStruct((4, 128), F32),
        ],
        compiler_params=LIMIT,
        cost_estimate=pl.CostEstimate(flops=10**9, bytes_accessed=2 << 20, transcendentals=0),
        name="first_strips",
    )(column_start, facets, *waves)


def columns_of(z_ref):
    return lambda begin, size: (z_ref[0, :, begin : begin + size], z_ref[1, :, begin : begin + size])


def far_strip_kernel(gs, z_ref, base_ref, steps_ref, tilt_ref, out_ref):
    strip_sums(gs, columns_of(z_ref), z_ref.shape[-1], base_ref, steps_ref, tilt_ref, out_ref)


def far_strips(z, waves, gs):
    return pl.pallas_call(
        functools.partial(far_strip_kernel, tuple(gs)),
        in_specs=[VMEM] * 4,
        out_specs=VMEM,
        out_shape=jax.ShapeDtypeStruct((len(gs), 2, waves[0].shape[2], z.shape[1] // 2), F32),
        compiler_params=LIMIT,
        cost_estimate=pl.CostEstimate(flops=10**9, bytes_accessed=2 << 20, transcendentals=0),
        name="far_strips",
    )(z, *waves)


def near_strip_kernel(groups, starts_ref, z_ref, base_ref, steps_ref, tilt_ref, *refs):
    out_refs, (turn_ref, away_ref, starts, sem) = refs[: len(groups)], refs[len(groups) :]
    copy = pltpu.make_async_copy(starts_ref, starts, sem)
    copy.start()
    for gs, out_ref in zip(groups, out_refs):
        strip_sums(gs, columns_of(z_ref), z_ref.shape[-1], base_ref, steps_ref, tilt_ref, out_ref)
    copy.wait()
    rows, _, height = turn_ref.shape
    rows_total = rows * height
    mine = starts[lax.axis_index("frow")]
    for r in range(rows):
        turn_ref[r, 0:1], turn_ref[r, 1:2] = unit(mine * (r * height + lanes(height)), rows_total, 1.0 / math.sqrt(rows_total))
        away_ref[r] = jnp.full((1, 128), mine - starts[r], jnp.int32)


def near_strips(starts, z, waves, groups):
    rows, count, height = starts.shape[0], waves[0].shape[2], z.shape[1] // 2
    return pl.pallas_call(
        functools.partial(near_strip_kernel, groups),
        in_specs=[pl.BlockSpec(memory_space=pl.ANY)] + [VMEM] * 4,
        out_specs=[VMEM] * (len(groups) + 2),
        out_shape=[jax.ShapeDtypeStruct((len(gs), 2, count, height), F32) for gs in groups]
        + [jax.ShapeDtypeStruct((rows, 2, height), F32), jax.ShapeDtypeStruct((rows, 1, 128), jnp.int32)],
        scratch_shapes=[pltpu.SMEM((rows,), jnp.int32), pltpu.SemaphoreType.DMA],
        compiler_params=LIMIT,
        cost_estimate=pl.CostEstimate(flops=4 * 10**9, bytes_accessed=2 << 20, transcendentals=0),
        name="near_strips",
    )(starts, z, *waves)


def pack_kernel(terms, *refs):
    weight_ref, row_ref, live_ref, out_ref = refs[terms:]
    count = refs[0].shape[2]
    strip = sum(ref[0] for ref in refs[:terms])
    out_ref[:count], out_ref[count : 2 * count] = strip[0], strip[1]
    width = out_ref.shape[1]
    weight = weight_ref[0]
    if count < width:
        weight = jnp.concatenate([weight, jnp.zeros((MAXB, width - count), F32)], 1)
    out_ref[2 * count : 2 * count + MAXB] = weight
    row = jnp.where(lanes(MAXB) < live_ref[0:1, 0:1], row_ref[...], -1).astype(F32)
    row = jnp.concatenate([row, jnp.zeros((1, width - MAXB), F32)], 1)
    out_ref[2 * count + MAXB :] = jnp.broadcast_to(row, (META, width))


def pack(terms, weight, row, live, count, height):
    return pl.pallas_call(
        functools.partial(pack_kernel, len(terms)),
        in_specs=[VMEM] * (len(terms) + 3),
        out_specs=VMEM,
        out_shape=jax.ShapeDtypeStruct((2 * count + MAXB + META, height), F32),
        compiler_params=LIMIT,
        name="pack",
    )(*terms, weight, row, live)


class Message:
    def __init__(self, r, message, refs, height, count, rows_total):
        b_ref, roots_ref, turn_ref, away_ref = refs
        own = lax.axis_index("frow")
        strip, rest = message[: 2 * count], message[2 * count :]
        pc, ps = turn_ref[r, 0:1], turn_ref[r, 1:2]
        re, im = strip[:count], strip[count:]
        re, im = re * pc + im * ps, im * pc - re * ps
        high, low = halves(jnp.concatenate([jnp.concatenate([re, im], 1), jnp.concatenate([im, -re], 1)]))
        self.left = jnp.concatenate([high, low, high], 1)

        self.rest, self.away, self.place = rest, away_ref[r][0:1, 0:1], None
        self.turn = lax.rem(r - own + rows_total // height, rows_total // height)
        self.refs, self.count, self.rows_total = (b_ref, roots_ref), count, rows_total

    def prepare(self):
        width = self.rest.shape[1]
        turned = jnp.transpose(jnp.concatenate([self.rest, jnp.zeros((width - self.rest.shape[0], width), F32)]))
        self.weight = jnp.concatenate(halves(turned[: self.count, :MAXB]), 1)
        row = turned[:MAXB, MAXB : MAXB + 1].astype(jnp.int32)
        self.place = jnp.where(row < 0, -1, (row - self.away) & (self.rows_total - 1))

    def chunk(self, begin, size):
        b_ref, roots_ref = self.refs
        part = lax.dot_general(self.left, b_ref[:, begin : begin + size], NN, preferred_element_type=F32)
        if self.place is None:
            self.prepare()
        pc, ps = roots_ref[self.turn, 0:1, begin : begin + size], roots_ref[self.turn, 1:2, begin : begin + size]
        re, im = part[: self.count], part[self.count :]
        freq = begin + lanes(size)
        hot = (begin + lanes(size, MAXB) == self.place).astype(F32).astype(BF)
        gain = lax.dot_general(self.weight, jnp.concatenate([hot, hot]), NN, preferred_element_type=F32)
        seen = (((freq + self.away) & (self.rows_total - 1)) < SG).astype(F32)
        return re * pc + im * ps, im * pc - re * ps, gain + seen


def chunks(total, size=256):
    return [(begin, min(size, total - begin)) for begin in range(0, total, size)]


def image_waves(base_ref, steps_ref, tilt_ref, out_ref):
    for g in range(out_ref.shape[0]):
        base = tilted((base_ref[g, 0], base_ref[g, 1]), tilt_ref, 0)
        turn = tilted((steps_ref[g, 0], steps_ref[g, 1]), tilt_ref, 2)
        for begin, size in chunks(out_ref.shape[-1]):
            columns = slice(begin, begin + size)
            out_ref[g, 0, :, columns], out_ref[g, 1, :, columns] = waves_in(base, turn, begin, size)


def last_chunks(total):
    return [(0, total // 2), (total // 2, total // 2)]


def gather_kernel(kind, steps, rows, height, count, *refs):
    tables, refs = refs[:4], refs[4:]
    odd = lax.rem(lax.axis_index("fcol"), 2) == 1
    at = ring_place(lax.axis_index("frow"), rows)

    def add(state_ref, arrived, out_ref, gain_ref=None):
        found = [
            Message(ring_block(at + step, rows), message[...], tables, height, count, rows * height)
            for step, message in arrived
        ]
        for begin, size in chunks(rows * height):
            terms = [message.chunk(begin, size) for message in found]
            if gain_ref is not None and begin < SG:
                gain_ref[:, begin : begin + size] = terms[0][2]
            for i in range(3):
                value = sum(term[i] for term in terms)
                if state_ref is not None:
                    value = value + state_ref[i, :, begin : begin + size]
                out_ref[i, :, begin : begin + size] = value

    if kind == "first":
        add(None, zip(steps, refs), refs[-1])
    elif kind == "plain":
        add(refs[0], zip(steps, refs[1:]), refs[-1])
    elif kind == "own":

        @pl.when(jnp.logical_not(odd))
        def _():
            add(None, zip(steps, refs), refs[-1])

    elif kind == "skip":

        @pl.when(jnp.logical_not(odd))
        def _():
            add(refs[0], zip(steps, refs[1:]), refs[-1])

    elif kind in ("late", "late own"):
        whole = kind == "late own"
        state_ref, before_ref, early, now, waves, (out_ref, made_ref, gain_ref) = (
            refs[0], refs[1], refs[2:4], refs[4:6], refs[6:9], refs[9:]
        )

        @pl.when(jnp.logical_not(odd))
        def _():
            add(state_ref, zip(steps[2:], now), out_ref)

        @pl.when(odd)
        def _():
            if whole:
                add(None, zip((0, *steps), [before_ref, *early, *now]), out_ref, gain_ref)
            else:
                add(before_ref, zip(steps, [*early, *now]), out_ref)
            image_waves(*waves, made_ref)

    else:
        state_ref, now, waves, made_ref, (out_ref, waves_ref) = refs[0], refs[1:3], refs[3:6], refs[6], refs[7:]
        add(state_ref, zip(steps, now), out_ref)

        @pl.when(odd)
        def _():
            waves_ref[...] = made_ref[...]

        @pl.when(jnp.logical_not(odd))
        def _():
            image_waves(*waves, waves_ref)


def gather_step(kind, tables, operands, steps, count, *more):
    height, rows_total = tables[2].shape[2], tables[0].shape[1]
    shapes = [jax.ShapeDtypeStruct((3, count, rows_total), F32), *more]
    out = pl.pallas_call(
        functools.partial(gather_kernel, kind, steps, rows_total // height, height, count),
        in_specs=[VMEM] * (len(tables) + len(operands)),
        out_specs=[VMEM] * len(shapes),
        out_shape=shapes,
        compiler_params=LIMIT,
        cost_estimate=pl.CostEstimate(flops=10**9, bytes_accessed=4 << 20, transcendentals=0),
        name="gather_step",
    )(*tables, *operands)
    return out if more else out[0]


def back_kernel(rows, height, count, *refs):
    tables, (turned_ref, state_ref, message_ref, back_ref, sub_ref) = refs[:4], refs[4:]
    rows_total = rows * height
    own = lax.axis_index("frow")
    r = ring_block(ring_place(own, rows) + rows // 2, rows)
    message = Message(r, message_ref[...], tables, height, count, rows_total)
    acc = None
    for begin, size in chunks(rows_total):
        terms = message.chunk(begin, size)
        re, im, gain = [term + state_ref[i, :, begin : begin + size] for i, term in enumerate(terms)]
        if begin < SG:
            sub_ref[0, :, begin : begin + size] = re
            sub_ref[1, :, begin : begin + size] = im
        high, low = halves(jnp.concatenate([re * gain, im * gain]))
        table = turned_ref[begin : begin + size]
        part = lax.dot_general(high, table, NN, preferred_element_type=F32)
        part = part[:, : 2 * height] + (
            part[:, 2 * height :] + lax.dot_general(low, table[:, : 2 * height], NN, preferred_element_type=F32)
        )
        acc = part if acc is None else acc + part
    re = acc[:count, :height] - acc[count:, height:]
    im = acc[count:, :height] + acc[:count, height:]
    pc, ps = tables[2][own, 0:1], tables[2][own, 1:2]
    back_ref[0] = jnp.transpose(re * pc - im * ps)
    back_ref[1] = jnp.transpose(im * pc + re * ps)


def back_step(tables, turned, state, message, height):
    count, rows_total = state.shape[1:]
    return pl.pallas_call(
        functools.partial(back_kernel, rows_total // height, height, count),
        in_specs=[VMEM] * 7,
        out_specs=[VMEM] * 2,
        out_shape=[
            jax.ShapeDtypeStruct((2, height, count), F32),
            jax.ShapeDtypeStruct((2, count, SG), F32),
        ],
        compiler_params=LIMIT,
        name="back_step",
    )(*tables, turned, state, message)


def correct_kernel(whole, sub_ref, gain_ref, late_ref, roots_ref, out_ref):
    count = sub_ref.shape[1]
    pieces = SG // 128
    own = lax.axis_index("frow")
    pc, ps = roots_ref[own, 0:1, :SG], roots_ref[own, 1:2, :SG]
    re, im, gain = sub_ref[0], sub_ref[1], gain_ref[2, :, :SG]
    if whole:
        gain = jnp.where(lax.rem(lax.axis_index("fcol"), 2) == 1, late_ref[...], gain)
    for part, value in enumerate([(re * pc + im * ps) * gain, (im * pc - re * ps) * gain]):
        for i in range(pieces):
            out_ref[pl.ds(2 * i + part, count, stride=2 * pieces), :] = value[:, 128 * i : 128 * (i + 1)]


def correct_step(whole, sub, first_state, own_gain, roots):
    count = sub.shape[1]
    out = pl.pallas_call(
        functools.partial(correct_kernel, whole),
        in_specs=[VMEM] * 4,
        out_specs=VMEM,
        out_shape=jax.ShapeDtypeStruct((count * 2 * SG // 128, 128), F32),
        compiler_params=LIMIT,
        cost_estimate=pl.CostEstimate(flops=4 * 10**9, bytes_accessed=4 << 20, transcendentals=0),
        name="correct_step",
    )(sub, first_state, own_gain, roots)
    out = out.reshape(count, SG // 128, 2, 128)
    return jnp.transpose(out, (0, 2, 1, 3)).reshape(1, count, 2, SG)


def image_kernel(gs, first, last, e_ref, *refs):
    backs, refs = refs[: len(gs)], refs[len(gs) :]
    acc_ref = None if first else refs[0]
    out_ref = refs[0 if first else 1]
    if last:
        scratch, sems = refs[-2:]
    width = e_ref.shape[-1]
    height = backs[0].shape[1]
    left = []
    for back in backs:
        re, im = back[0], back[1]
        left.append(halves(jnp.concatenate([jnp.concatenate([re, -im], 1), jnp.concatenate([im, re], 1)])))
    copies = []
    for begin, size in (last_chunks(width) if last else chunks(width)):
        columns = slice(begin, begin + size)
        acc = None if first else jnp.concatenate([acc_ref[0, :, columns], acc_ref[1, :, columns]])
        for (high, low), g in zip(left, gs):
            part = dot3((high, low), (e_ref[g, 0, :, columns], e_ref[g, 1, :, columns]), NN)
            acc = part if acc is None else acc + part
        re, im = acc[:height], acc[height:]
        if last:
            scratch[0, :, columns] = re
            scratch[1, :, columns] = im
            copies.append(
                pltpu.make_async_copy(scratch.at[:, :, columns], out_ref.at[:, :, columns], sems.at[len(copies)])
            )
            copies[-1].start()
        else:
            out_ref[0, :, columns] = re
            out_ref[1, :, columns] = im
    for copy in copies:
        copy.wait()


def image_step(table, gs, backs, acc, last):
    width = table.shape[-1]
    height = backs[0].shape[1]
    first = acc is None
    operands = list(backs) + ([] if first else [acc])
    return pl.pallas_call(
        functools.partial(image_kernel, tuple(gs), first, last),
        in_specs=[VMEM] * (1 + len(operands)),
        out_specs=pl.BlockSpec(memory_space=pl.ANY) if last else VMEM,
        out_shape=jax.ShapeDtypeStruct((2, height, width), F32),
        scratch_shapes=[pltpu.VMEM((2, height, width), F32), pltpu.SemaphoreType.DMA((len(last_chunks(width)),))] if last else [],
        compiler_params=LIMIT,
        cost_estimate=pl.CostEstimate(flops=4 * 10**9, bytes_accessed=4 << 20, transcendentals=0),
        name="image_step",
    )(table, *operands)


def swap(value, axis, bit):
    return lax.ppermute(value, axis, [(i, i ^ bit) for i in range(lax.axis_size(axis))])


def per_device(facets, column_start, subgrid_start, vis_count, vis_row, vis_weight):
    rows = lax.axis_size("frow")
    cols = lax.axis_size("fcol")
    height, width = facets.shape[1:]
    rows_total, cols_total = height * rows, width * cols
    count = SG // cols
    assert vis_count.shape[0] == 1 and count <= height

    b_table = wave_table(height, rows_total, rows_total)
    turned = jnp.asarray(b_table.reshape(4 * height, rows_total).T.copy())
    b_table = jnp.asarray(np.concatenate([b_table[:2], b_table]).reshape(6 * height, rows_total))
    angle = np.arange(rows)[:, None] * np.arange(rows_total)[None, :] % rows * (2.0 * np.pi / rows)
    roots = jnp.asarray(np.stack([np.cos(angle), np.sin(angle)], 1).astype(np.float32))

    top = cols // 2
    column_start = column_start.reshape(1, 1)
    waves = waves_of(count, width, cols_total)
    sent, z, tilt = first_strips(column_start, facets, waves, range(top + 1, cols, 2))
    waves = *waves, tilt
    far = far_strips(z, waves, range(top, cols, 2)) + swap(sent, "fcol", 1)
    far, z = lax.optimization_barrier((far, z))
    sent, near, *turns = near_strips(subgrid_start, z, waves, [tuple(range(1, top, 2)), tuple(range(0, top, 2))])
    terms = [near + swap(far, "fcol", top), swap(sent, "fcol", 1)]
    bit = 2
    while bit < top:
        pairs = sum(terms).reshape((-1, 2) + far.shape[1:])
        terms = [pairs[:, 0], swap(pairs[:, 1], "fcol", bit)]
        bit *= 2

    own = pack(terms, vis_weight, vis_row, vis_count.reshape(1, 1), count, height)
    tables = b_table, roots, *turns
    order = list(range(0, rows, 2)) + list(range(rows - 1, 0, -2))
    ahead = [(order[i], order[(i + 1) % rows]) for i in range(rows)]
    behind = [(b, a) for a, b in ahead]
    last = rows // 2 - 1
    assert last >= 3
    whole = last == 3
    first_state = state = gather_step("own" if whole else "first", tables, [own], (0,), count)
    made = jax.ShapeDtypeStruct((cols, 2, 2 * count, width), BF)
    up = down = own
    for step in range(1, last + 1):
        up = lax.ppermute(up, "frow", ahead)
        down = lax.ppermute(down, "frow", behind)
        up, state = lax.optimization_barrier((up, state))
        if step == last - 2:
            before, early = state, [up, down]
            state = gather_step("skip", tables, [state, up, down], (-step, step), count)
        elif step == last - 1:
            steps = (1 - step, step - 1, -step, step)
            operands = [state, own if whole else before, *early, up, down, *waves]
            own_gain = jax.ShapeDtypeStruct((count, SG), F32)
            kind = "late own" if whole else "late"
            state, image_table, own_gain = gather_step(kind, tables, operands, steps, count, made, own_gain)
        elif step == last:
            operands = [state, up, down, *waves, image_table]
            state, image_table = gather_step("last", tables, operands, (-step, step), count, made)
        else:
            state = gather_step("plain", tables, [state, up, down], (-step, step), count)
    up = lax.ppermute(up, "frow", ahead)
    back, sub = back_step(tables, turned, state, up, height)

    near, far = {0: back}, {top: swap(back, "fcol", top)}

    def spread(blocks, bit):
        return {g ^ bit: swap(b, "fcol", bit) for g, b in blocks.items()}

    def image(blocks, acc, last=False):
        return image_step(image_table, blocks.keys(), list(blocks.values()), acc, last)

    acc = image(near, None)
    near[0], acc = lax.optimization_barrier((back, acc))
    bit = top // 2
    while bit >= 1:
        near |= spread(near, bit)
        bit //= 2
    del near[0]
    acc = image(near, acc)
    corrected = correct_step(whole, sub, first_state, own_gain, roots)
    far[top], acc, corrected = lax.optimization_barrier((far[top], acc, corrected))
    bit = top // 2
    while bit > 1:
        far |= spread(far, bit)
        bit //= 2
    rest = spread(far, 1)
    acc = image(far, acc)
    return corrected, image(rest, acc, last=True)


def solution(mesh):
    return jax.shard_map(
        per_device,
        mesh=mesh,
        in_specs=(
            P(None, "frow", "fcol"),
            P(),
            P(),
            P("frow"),
            P("frow", None),
            P("frow", None, "fcol"),
        ),
        out_specs=(P("frow", "fcol", None, None), P(None, "frow", "fcol")),
        check_vma=False,
    )
```
